256 devices in a mesh: section: 4 (over y_hi, core), ctx: 8 (over y_lo, x), tp: 8 (over z).
Axes of the slice: x: 4, y: 4 (y_hi: 2, y_lo: 2; y = y_hi * 2 + y_lo), z: 8, core: 2. Of those that a mesh axis runs over, the one named last changes fastest.
Arguments:
- tokens: bfloat16 [2, 1024, 4096], P(None, 'ctx', 'tp'), may hold values from -60 to 60
- document_lengths: int32 [2], replicated, may hold values from 1 to 1024, 1536 in all
- tenant_indices: int32 [2], replicated, may hold values from 0 to 3
- attention_norm_gain: float32 [4, 4096], P('section'), may hold values from 0.5 to 1.5
- query_weight: bfloat16 [4, 4096, 4096], P('section', None, 'tp'), may hold values from -0.5625 to 0.5625
- key_weight: bfloat16 [4, 4096, 1024], P('section', None, 'tp'), may hold values from -0.5625 to 0.5625
- value_weight: bfloat16 [4, 4096, 1024], P('section', None, 'tp'), may hold values from -0.09375 to 0.09375
- output_weight: bfloat16 [4, 4096, 4096], P('section', 'tp'), may hold values from -0.09375 to 0.09375
- query_adapter_down: bfloat16 [4, 4, 4096, 16], P('section'), may hold values from -0.09375 to 0.09375
- query_adapter_up: bfloat16 [4, 4, 16, 4096], P('section', None, None, 'tp'), may hold values from -1.5 to 1.5
- value_adapter_down: bfloat16 [4, 4, 4096, 16], P('section'), may hold values from -0.09375 to 0.09375
- value_adapter_up: bfloat16 [4, 4, 16, 1024], P('section', None, None, 'tp'), may hold values from -1.5 to 1.5
- closing_norm_gain: float32 [4096], P('tp'), may hold values from 0.4 to 2.5
Outputs:
- embedding: float32 [2, 4096], P(None, 'tp')
The draws below stay inside these ranges and needn't reach their ends.
Inputs may be any that keep to these rules, and one draw needn't show every extreme that they name: The first document_lengths[m] positions of document m are its tokens.
All inputs are finite; a program needn't handle non-finite values.
Results may differ from the reference program's by a relative error of at most 0.03.
Values may be sent and summed in bfloat16 or wider, within the bound.
A program may use at most 128 MiB of HBM per device.

```python
import math
import jax
import jax.numpy as jnp
import numpy as np
from jax import lax

MODEL_WIDTH = 4096
QUERY_HEADS = 32
KEY_VALUE_HEADS = 8
HEAD_SIZE = 128
ADAPTER_RANK = 16
TENANT_COUNT = 4
MB = 2
LAYER_COUNT = 4
SEQ = 1024
N_TP = 8


def draw_query_weight(key, part):
    key = jax.random.fold_in(key, 31)
    base = jax.random.truncated_normal(key, -6.0, 6.0, (LAYER_COUNT, MODEL_WIDTH, QUERY_HEADS * HEAD_SIZE), jnp.float32) / math.sqrt(MODEL_WIDTH)
    return base.astype(jnp.bfloat16)


def draw_key_weight(key, part):
    key = jax.random.fold_in(key, 32)
    base = jax.random.truncated_normal(key, -6.0, 6.0, (LAYER_COUNT, MODEL_WIDTH, KEY_VALUE_HEADS * HEAD_SIZE), jnp.float32) / math.sqrt(MODEL_WIDTH)
    return base.astype(jnp.bfloat16)


def draw_tokens(key, part):
    key = jax.random.fold_in(key, 33)
    first, second, third, fourth = jax.random.split(key, 4)
    ramp = jnp.arange(MODEL_WIDTH, dtype=jnp.float32) / (MODEL_WIDTH - 1)
    rough = jnp.exp(math.log(3.0) * jax.random.uniform(third, (MODEL_WIDTH,), jnp.float32))
    base = jax.random.truncated_normal(first, -4.0, 4.0, (MB, SEQ, MODEL_WIDTH), jnp.float32)
    rows = jnp.exp(math.log(10.0) * jax.random.uniform(second, (MB, SEQ, 1), jnp.float32))
    slope_row = jax.random.uniform(fourth, (MB, SEQ, 1), jnp.float32, 0.5, 2.0)
    profile = jnp.exp(math.log(10.0) * slope_row * (ramp[None, None, :] - 1.0))
    return (base * rows * profile * rough * 0.5).astype(jnp.bfloat16)


def draw_closing_norm_gain(key, part):
    key = jax.random.fold_in(key, 34)
    ramp = jnp.arange(MODEL_WIDTH, dtype=jnp.float32) / (MODEL_WIDTH - 1)
    rough = jax.random.uniform(key, (MODEL_WIDTH,), jnp.float32, 0.8, 1.25)
    trend = jnp.exp(math.log(3.0) * (ramp - 0.5))
    return (rough * trend).astype(jnp.float32)


def level_of(key, extent, shards, least, high):
    def one(dim, shards_of):
        steps = jax.random.uniform(jax.random.fold_in(jax.random.fold_in(key, 6), dim), (shards_of,), jnp.float32, least / len(shards), high / len(shards))
        return jnp.repeat(jnp.exp(steps), extent[dim] // shards_of).reshape((-1,) + (1,) * (len(extent) - dim - 1))

    loudness = one(*shards[0])
    for cut in shards[1:]:
        loudness = loudness * one(*cut)
    return loudness


def length_profile(number_of, total, limit, slope):
    portions = [(1 << 20) // math.isqrt(standing ** slope) + 1 for standing in range(2, number_of + 1)]
    rest, counts = total - limit - (number_of - 1), [1] * (number_of - 1)
    while rest > 0:
        candidates = [i for i in range(number_of - 1) if counts[i] < limit]
        whole, remaining = sum([portions[i] for i in candidates]), rest
        for i in candidates:
            more = min(limit - counts[i], max(1, remaining * portions[i] // whole), rest)
            counts[i] = counts[i] + more
            rest = rest - more
    return np.array([limit] + counts)


def uneven_parts(rng, count, total, limit, lean):
    if count == 2:
        one = jax.random.randint(rng, (), max(1, total - limit), min(limit, total - 1) + 1)
        return jnp.stack([one, total - one])
    sizes = jnp.asarray(length_profile(count, total, limit, lean), jnp.int32)
    twos = (count - 1) // 2
    donor, receiver = sizes[1:1 + 2 * twos:2], sizes[2:2 + 2 * twos:2]
    room = jnp.minimum(donor - 1, limit - receiver)
    moved = jax.random.randint(jax.random.fold_in(rng, 1), (twos,), 0, 1 << 20) % (room + 1)
    sizes = sizes.at[1:1 + 2 * twos:2].set(donor - moved).at[2:2 + 2 * twos:2].set(receiver + moved)
    return sizes[jax.random.permutation(jax.random.fold_in(rng, 2), count)]


def scatter_about(key, shape, spread, reach, cuts=(), kind=jnp.bfloat16):
    loudness = level_of(key, shape, cuts, -0.22, 0.18) if cuts else 1.0
    entries = jax.random.normal(key, shape, jnp.float32) * spread * loudness
    return jnp.minimum(jnp.maximum(entries, -reach), reach).astype(kind)


def setup_inputs(seed: int = 0) -> dict:
    splits = jax.random.split(jax.random.key(seed), 14)
    tokens = draw_tokens(jax.random.fold_in(splits[13], 71), 0)
    document_lengths = uneven_parts(splits[1], MB, 3 * MB * SEQ // 4, SEQ, 0).astype(jnp.int32)
    tenant_indices = jax.random.randint(splits[2], (MB,), 0, TENANT_COUNT).astype(jnp.int32)
    attention_norm_gain = jnp.clip(1.0 + 0.1 * jax.random.normal(splits[3], (LAYER_COUNT, MODEL_WIDTH), jnp.float32), 0.5, 1.5)
    query_weight = draw_query_weight(jax.random.fold_in(splits[13], 71), 0)
    key_weight = draw_key_weight(jax.random.fold_in(splits[13], 71), 0)
    value_weight = scatter_about(splits[6], (LAYER_COUNT, MODEL_WIDTH, KEY_VALUE_HEADS * HEAD_SIZE), MODEL_WIDTH ** -0.5, 0.09375, ((0, 4), (2, 8)))
    output_weight = scatter_about(splits[7], (LAYER_COUNT, QUERY_HEADS * HEAD_SIZE, MODEL_WIDTH), (QUERY_HEADS * HEAD_SIZE) ** -0.5, 0.09375, ((0, 4), (1, 8)))
    query_adapter_down = scatter_about(splits[8], (LAYER_COUNT, TENANT_COUNT, MODEL_WIDTH, ADAPTER_RANK), MODEL_WIDTH ** -0.5, 0.09375, ((0, 4),))
    query_adapter_up = scatter_about(splits[9], (LAYER_COUNT, TENANT_COUNT, ADAPTER_RANK, QUERY_HEADS * HEAD_SIZE), ADAPTER_RANK ** -0.5, 1.5, ((0, 4), (3, 8)))
    value_adapter_down = scatter_about(splits[10], (LAYER_COUNT, TENANT_COUNT, MODEL_WIDTH, ADAPTER_RANK), MODEL_WIDTH ** -0.5, 0.09375, ((0, 4),))
    value_adapter_up = scatter_about(splits[11], (LAYER_COUNT, TENANT_COUNT, ADAPTER_RANK, KEY_VALUE_HEADS * HEAD_SIZE), ADAPTER_RANK ** -0.5, 1.5, ((0, 4), (3, 8)))
    closing_norm_gain = draw_closing_norm_gain(jax.random.fold_in(splits[13], 71), 0)
    return {"tokens": tokens, "document_lengths": document_lengths, "tenant_indices": tenant_indices, "attention_norm_gain": attention_norm_gain, "query_weight": query_weight, "key_weight": key_weight, "value_weight": value_weight, "output_weight": output_weight, "query_adapter_down": query_adapter_down, "query_adapter_up": query_adapter_up, "value_adapter_down": value_adapter_down, "value_adapter_up": value_adapter_up, "closing_norm_gain": closing_norm_gain}


def rms_scale(values, gain, epsilon):
    return values * lax.rsqrt(lax.optimization_barrier(jnp.mean(values * values, axis=-1, keepdims=True)) + epsilon) * gain

def rotate(values, token_positions):
    half = values.shape[-1] // 2
    freq = 500000.0 ** (-jnp.arange(half, dtype=jnp.float32) / half)
    angle = token_positions[:, None] * freq[None, :]
    cosine = jnp.cos(angle)[:, None, :]
    sine = jnp.sin(angle)[:, None, :]
    first = values[..., :half]
    second = values[..., half:]
    return jnp.concatenate([first * cosine - second * sine, second * cosine + first * sine], axis=-1)

def apply_single_layer(hidden_state, layer_index, tenant_adapter, document_length, token_positions, attention_norm_gain, query_weight, key_weight, value_weight, output_weight, query_adapter_down, query_adapter_up, value_adapter_down, value_adapter_up):
    group = QUERY_HEADS // KEY_VALUE_HEADS
    widen = hidden_state.astype(jnp.float32)
    normalized_state = rms_scale(widen, attention_norm_gain[layer_index], 1e-05).astype(jnp.bfloat16)
    query_low_rank = jnp.dot(normalized_state, query_adapter_down[layer_index, tenant_adapter], preferred_element_type=jnp.float32).astype(jnp.bfloat16)
    value_low_rank = jnp.dot(normalized_state, value_adapter_down[layer_index, tenant_adapter], preferred_element_type=jnp.float32).astype(jnp.bfloat16)
    query_rows = jnp.dot(normalized_state, query_weight[layer_index], preferred_element_type=jnp.float32) + jnp.dot(query_low_rank, query_adapter_up[layer_index, tenant_adapter], preferred_element_type=jnp.float32)
    query_rows = rotate(query_rows.reshape(SEQ, QUERY_HEADS, HEAD_SIZE), token_positions).astype(jnp.bfloat16)
    key = rotate(jnp.dot(normalized_state, key_weight[layer_index], preferred_element_type=jnp.float32).reshape(SEQ, KEY_VALUE_HEADS, HEAD_SIZE), token_positions).astype(jnp.bfloat16)
    value_rows = jnp.dot(normalized_state, value_weight[layer_index], preferred_element_type=jnp.float32) + jnp.dot(value_low_rank, value_adapter_up[layer_index, tenant_adapter], preferred_element_type=jnp.float32)
    value_rows = value_rows.reshape(SEQ, KEY_VALUE_HEADS, HEAD_SIZE).astype(jnp.bfloat16)
    valid = jnp.arange(SEQ, dtype=jnp.int32) < document_length
    grouped = jnp.moveaxis(query_rows.reshape(SEQ, KEY_VALUE_HEADS, group, HEAD_SIZE), 1, 0)
    keys = jnp.moveaxis(key, 1, 0)
    values = jnp.moveaxis(value_rows, 1, 0)

    def per_group(items):
        block_q, block_k, block_v = items
        scores = jnp.einsum('rgd,sd->grs', block_q.astype(jnp.float32), block_k.astype(jnp.float32)) * HEAD_SIZE ** (-0.5)
        scores = jnp.where(valid[None, None, :], scores, -1e+30)
        top = lax.optimization_barrier(jnp.max(scores, axis=-1, keepdims=True))
        expo = jnp.exp(scores - top)
        weights = (expo / lax.optimization_barrier(jnp.sum(expo, axis=-1, keepdims=True))).astype(jnp.bfloat16)
        mixed = jnp.einsum('grs,sd->rgd', weights.astype(jnp.float32), block_v.astype(jnp.float32))
        return mixed.astype(jnp.bfloat16)
    attended = lax.map(per_group, (grouped, keys, values))
    attended = jnp.moveaxis(attended, 0, 1).reshape(SEQ, QUERY_HEADS * HEAD_SIZE)
    block = QUERY_HEADS * HEAD_SIZE // N_TP
    update = jnp.zeros((SEQ, MODEL_WIDTH), jnp.float32)
    for shard in range(N_TP):
        term = jnp.dot(attended[:, shard * block:(shard + 1) * block], output_weight[layer_index, shard * block:(shard + 1) * block], preferred_element_type=jnp.float32)
        update = update + lax.optimization_barrier(term.astype(jnp.bfloat16)).astype(jnp.float32)
    return (widen + update).astype(jnp.bfloat16)

def reference(tokens, document_lengths, tenant_indices, attention_norm_gain, query_weight, key_weight, value_weight, output_weight, query_adapter_down, query_adapter_up, value_adapter_down, value_adapter_up, closing_norm_gain):
    token_positions = jnp.arange(SEQ, dtype=jnp.float32)
    pooled_list = []
    for micro in range(MB):
        document_length = document_lengths[micro]
        tenant_adapter = tenant_indices[micro]
        hidden_state = tokens[micro]
        for layer_index in range(LAYER_COUNT):
            hidden_state = apply_single_layer(hidden_state, layer_index, tenant_adapter, document_length, token_positions, attention_norm_gain, query_weight, key_weight, value_weight, output_weight, query_adapter_down, query_adapter_up, value_adapter_down, value_adapter_up)
        final = rms_scale(hidden_state.astype(jnp.float32), closing_norm_gain, 1e-05)
        valid = jnp.arange(SEQ, dtype=jnp.int32) < document_length
        summed = lax.optimization_barrier(jnp.sum(jnp.where(valid[:, None], final, jnp.float32(0.0)), axis=0))
        pooled_list.append(summed / document_length.astype(jnp.float32))
    pooled = jnp.stack(pooled_list)
    return pooled * lax.rsqrt(lax.optimization_barrier(jnp.mean(pooled * pooled, axis=-1, keepdims=True)) + 1e-06)
```

```python
import math

import jax
import jax.numpy as jnp
import numpy as np
from jax import lax
from jax.experimental import pallas as pl
from jax.experimental.pallas import tpu as pltpu
from jax.sharding import PartitionSpec as P

HEAD = 128
F32 = jnp.float32
BF16 = jnp.bfloat16
MESH = pl.DeviceIdType.MESH

PIECES = 2
FAR = 3
WK, WV, WQ, GAIN, WO, DOWN, UP = range(7)
NEAR = ((1, 0), (0, 1), (0, 3))
REST = ((1, 1), (1, 3), (0, 2), (1, 2))


def fold(x):
    total = x[:, :HEAD]
    for i in range(1, x.shape[1] // HEAD):
        total = total + x[:, i * HEAD:(i + 1) * HEAD]
    return total


def kernel(
    sizes,
    lengths, tenants, tokens, gain_hbm, closing, tables, wq_hbm, wk_hbm, wv_hbm, wo_hbm,
    qd_hbm, vd_hbm, q_up, v_up,
    out,
    wq, wkv, wo, gains, qd, vd, down, up, trig,
    hidden, own, agb, agf, rsb, rsf, rso, rsfo, prt, kvbuf,
    acc_q, acc_kv, acc_l, squares, qbuf, att, terms,
    ssb, ppb, sqb, res,
    w_sem, w_send, small_sem, in_sem, ag_send, ag_recv, rs_send, rs_recv, prt_recv,
    kv_send, kv_recv, pass_send, pass_recv, ss_send, ss_recv, pp_send, pp_recv, sq_send, sq_recv,
    fin_send, fin_recv,
):
    sections, n_ctx, n_tp, micro, rows, width = sizes
    full_width = width * n_tp
    part = rows // PIECES
    heads = wq.shape[3] // HEAD
    rank = q_up.shape[1]
    s = lax.axis_index("section")
    c = lax.axis_index("ctx")
    z = lax.axis_index("tp")
    e = lax.rem(s, 2)
    first_pair = s < 2
    last_pair = s >= sections - 2
    partner = s + 1 - 2 * e

    def around(at, by, n):
        return lax.rem(at + (by + n), n)

    def remote(src, dst, send, recv, **to):
        return pltpu.make_async_remote_copy(
            src_ref=src, dst_ref=dst, send_sem=send, recv_sem=recv, device_id=to, device_id_type=MESH)

    def arrive(ref, sem):
        pltpu.make_async_copy(ref, ref, sem).wait()

    def span(q):
        return pl.ds(q * part, part)

    def side(q):
        return q * 2 // PIECES

    def token_copy():
        return pltpu.make_async_copy(tokens.at[e], hidden.at[1], in_sem.at[0])

    def weight(item, j):
        return {
            WK: lambda: wkv.at[j, :, :, pl.ds(0, HEAD)],
            WV: lambda: wkv.at[j, :, :, pl.ds(HEAD, HEAD)],
            WQ: lambda: wq.at[j],
            GAIN: lambda: gains.at[j],
            WO: lambda: wo.at[j],
            DOWN: lambda: down.at[j],
            UP: lambda: up.at[j],
        }[item]()

    sources = {WK: wk_hbm, WV: wv_hbm, WQ: wq_hbm, GAIN: gain_hbm, WO: wo_hbm}
    spare = {DOWN: down.at[2], UP: up.at[2]}

    def weight_copy(item):
        return remote({**sources, **spare}[item], weight(item, e), w_send.at[item], w_sem.at[e, item],
                      section=partner)

    small_copies = [
        pltpu.make_async_copy(qd_hbm, qd, small_sem.at[0]),
        pltpu.make_async_copy(vd_hbm, vd, small_sem.at[1]),
        pltpu.make_async_copy(tables.at[c], trig, small_sem.at[2]),
    ]

    @pl.when(first_pair)
    def _():
        token_copy().start()

    for copy in small_copies:
        copy.start()
    for item, source in sources.items():
        pltpu.make_async_copy(source, weight(item, e), w_sem.at[e, item]).start()

    barrier = pltpu.get_barrier_semaphore()
    neighbour = (around(z, 1, n_tp), around(z, -1, n_tp))
    peers = [{"tp": around(z, i, n_tp)} for i in range(1, n_tp)]
    peers += [{"ctx": around(c, i, n_ctx)} for i in range(1, n_ctx)]
    peers += [{"section": around(s, i, sections)} for i in range(1, sections)]
    peers += [{"section": around(s, 2, sections), "tp": neighbour[d]} for d in range(2)]
    for peer in peers:
        pl.semaphore_signal(barrier, 1, device_id=peer, device_id_type=MESH)

    for copy in small_copies:
        copy.wait()
    for slot, document in ((e, e), (2, 1 - e)):
        t = tenants[document]
        up[slot] = jnp.zeros(up.shape[1:], BF16)
        down[slot, :rank] = qd[t]
        down[slot, rank:] = vd[t]
        up[slot, :rank, :heads * HEAD] = q_up[t]
        up[slot, rank:, heads * HEAD:] = v_up[t]

    pl.semaphore_wait(barrier, len(peers))

    two_on = (around(z, 2, n_tp), around(z, -2, n_tp))

    def ag_copy(j, d, r, q, src):
        return remote(src.at[span(q)], agb.at[j, d, r, span(q)], ag_send.at[j, d, r, q],
                      ag_recv.at[j, d, r, q], tp=neighbour[d])

    def ag_far(j, q):
        d = side(q)
        return remote(agb.at[j, d, 1, span(q)], agf.at[j, span(q)], ag_send.at[j, d, FAR, q],
                      ag_recv.at[j, d, FAR, q], tp=two_on[d])

    def rs_copy(j, d, r, q):
        return remote(rso.at[j, d, r, span(q)], rsb.at[j, d, r, span(q)], rs_send.at[j, d, r, q],
                      rs_recv.at[j, d, r, q], tp=neighbour[d])

    def rs_far(j, q):
        d = side(q)
        return remote(rsfo.at[j, span(q)], rsf.at[j, span(q)], rs_send.at[j, d, FAR, q],
                      rs_recv.at[j, d, FAR, q], tp=two_on[d])

    def prt_copy(j, d, q):
        slot = jnp.where(j == 0, 1, jnp.where(last_pair, 2, 0))
        where = jnp.where((j == 1) & jnp.logical_not(last_pair), around(s, 2, sections), s)
        return remote(rso.at[j, d, 2, span(q)], prt.at[slot, d, span(q)], rs_send.at[j, d, 2, q],
                      prt_recv.at[slot, d, q], tp=neighbour[d], section=where)

    def pass_copy(buf, i):
        return remote(buf.at[2], buf.at[0], pass_send.at[i], pass_recv.at[i], section=around(s, 2, sections))

    def ctx_peer(dy, dx):
        across = n_ctx // 2
        return around(c // across, dy, 2) * across + around(lax.rem(c, across), dx, across)

    def kv_copy(j, offset):
        dy, dx = offset
        i = dy * (n_ctx // 2) + dx
        return remote(kvbuf.at[j, c], kvbuf.at[j, c], kv_send.at[j, i], kv_recv.at[j, i],
                      ctx=ctx_peer(dy, dx))

    def ss_copy(i):
        return remote(ssb.at[0], ssb.at[i], ss_send.at[i], ss_recv.at[i], tp=around(z, i, n_tp))

    def pp_copy(i):
        return remote(ppb.at[0], ppb.at[i], pp_send.at[i], pp_recv.at[i], ctx=around(c, i, n_ctx))

    def sq_copy(i):
        return remote(sqb.at[0], sqb.at[i], sq_send.at[i], sq_recv.at[i], tp=around(z, i, n_tp))

    def fin_copy(i):
        return remote(res.at[e], res.at[e], fin_send.at[i], fin_recv.at[e], section=around(s, i, sections))

    def rotate(x):
        return x * trig[0] + pltpu.roll(x, HEAD // 2, axis=1) * trig[1]

    def take(j, blocks, first=False):
        values = None
        for block, g in blocks:
            h = block.astype(F32)
            columns = pl.ds(pl.multiple_of(g * width, width), width)
            x = (h * gains[j, :, columns]).astype(BF16)
            new = (
                fold(h * h),
                jnp.dot(x, wkv[j, g], preferred_element_type=F32),
                lax.dot_general(x, down[j, :, columns], (((1,), (1,)), ((), ())), preferred_element_type=F32),
                jnp.dot(x, wq[j, g], preferred_element_type=F32),
            )
            values = new if values is None else [a + b for a, b in zip(values, new)]
        for ref, value in zip((squares, acc_kv, acc_l, acc_q), values):
            ref[...] = value if first else ref[...] + value

    def join(i, q):
        for d in range(2):
            arrive(prt.at[i, d, span(q)], prt_recv.at[i, d, q])
        at = slice(q * part, (q + 1) * part)
        sums = prt[i, 0, at].astype(F32) + prt[i, 1, at].astype(F32)
        hidden[i + 1, at] = (hidden[i, at].astype(F32) + own[i, at].astype(F32) + sums).astype(BF16)

    def layer(j, carry):
        @pl.when(first_pair & (j == 0))
        def _():
            token_copy().wait()

        @pl.when(jnp.logical_not(first_pair) & (j == 0))
        def _():
            arrive(hidden.at[0], pass_recv.at[0])
            arrive(own.at[0], pass_recv.at[1])

        for q in range(PIECES):
            @pl.when(jnp.logical_not(first_pair) | (j == 1))
            def _():
                join(j, q)

            for d in range(2):
                ag_copy(j, d, 0, q, hidden.at[j + 1]).start()

        @pl.when(j == 0)
        def _():
            for item in (GAIN, DOWN, UP, WK, WV, WQ):
                weight_copy(item).start()

        @pl.when((j == 1) & jnp.logical_not(last_pair))
        def _():
            pass_copy(hidden, 0).start()

        def own_take():
            for item in (GAIN, WK, WV, WQ):
                arrive(weight(item, j), w_sem.at[j, item])

            @pl.when(j != e)
            def _():
                for item in (DOWN, UP):
                    arrive(weight(item, j), w_sem.at[j, item])

            take(j, [(hidden[j + 1], z)], first=True)

        def pair_take(r):
            take(j, [(agb[j, d, r], around(z, -1 - r if d == 0 else 1 + r, n_tp)) for d in range(2)])

        late = first_pair & (e == 1) & (j == 0)
        prompt = jnp.logical_not(late)

        @pl.when(prompt)
        def _():
            own_take()

        for r in range(3):
            for q in range(PIECES):
                for d in range(2):
                    arrive(agb.at[j, d, r, span(q)], ag_recv.at[j, d, r, q])
                    if r < 2:
                        ag_copy(j, d, r + 1, q, agb.at[j, d, r]).start()
                    if r == 1 and d == side(q):
                        ag_far(j, q).start()

            @pl.when(prompt)
            def _():
                pair_take(r)

        @pl.when(j == 0)
        def _():
            weight_copy(WO).start()

        @pl.when(late)
        def _():
            own_take()

            def after(r, carry):
                pair_take(r)
                return carry

            lax.fori_loop(0, 3, after, 0)

        for q in range(PIECES):
            arrive(agf.at[j, span(q)], ag_recv.at[j, side(q), FAR, q])
        take(j, [(agf[j], around(z, 4, n_tp))])

        mean = jnp.sum(squares[...], axis=1, keepdims=True) * (1.0 / full_width)
        scale = lax.rsqrt(mean + 1e-5)
        low = (acc_l[...] * scale).astype(BF16)
        kv = acc_kv[...] * scale
        kvbuf[j, c, :, :HEAD] = rotate(kv[:, :HEAD]).astype(BF16)
        added = jnp.dot(low, up[j, :, heads * HEAD:], preferred_element_type=F32)
        kvbuf[j, c, :, HEAD:] = (kv[:, HEAD:] + added).astype(BF16)
        for offset in NEAR + REST:
            kv_copy(j, offset).start()
        factor = HEAD ** -0.5 * math.log2(math.e)
        for g in range(heads):
            cols = slice(g * HEAD, (g + 1) * HEAD)
            q = acc_q[:, cols] * scale + jnp.dot(low, up[j, :, cols], preferred_element_type=F32)
            qbuf[g] = (rotate(q) * factor).astype(BF16)

        n = lengths[e]
        lane = lax.broadcasted_iota(jnp.int32, (1, rows), 1)

        def keys_of(offsets):
            sources = [ctx_peer(-dy, -dx) for dy, dx in offsets]
            blocks = [kvbuf[j, source] for source in sources]
            valid = jnp.concatenate([lane + source * rows < n for source in sources], axis=1)
            return (jnp.concatenate([block[:, :HEAD] for block in blocks], axis=0),
                    jnp.concatenate([block[:, HEAD:] for block in blocks], axis=0), valid)

        def scored(g, keys, valid):
            scores = lax.dot_general(
                qbuf[g], keys, (((1,), (1,)), ((), ())), preferred_element_type=F32)
            return jnp.where(valid, scores, -1e30)

        for offset in NEAR:
            kv_copy(j, offset).wait_recv()
        keys, values, valid = keys_of(((0, 0),) + NEAR)
        near = []
        for g in range(heads):
            scores = scored(g, keys, valid)
            top = jnp.max(scores, axis=1, keepdims=True)
            weights = jnp.exp2(scores - top)
            total = jnp.sum(weights, axis=1, keepdims=True)
            near.append((top, total, jnp.dot(weights.astype(BF16), values, preferred_element_type=F32)))
        for offset in REST:
            kv_copy(j, offset).wait_recv()
        keys, values, valid = keys_of(REST)
        for g in range(heads):
            top_near, total_near, mixed_near = near[g]
            scores = scored(g, keys, valid)
            top = jnp.maximum(jnp.max(scores, axis=1, keepdims=True), top_near)
            weights = jnp.exp2(scores - top)
            fade = jnp.exp2(top_near - top)
            total = jnp.sum(weights, axis=1, keepdims=True) + total_near * fade
            mixed = jnp.dot(weights.astype(BF16), values, preferred_element_type=F32) + mixed_near * fade
            att[:, g * HEAD:(g + 1) * HEAD] = (mixed * (1.0 / total)).astype(BF16)

        arrive(weight(WO, j), w_sem.at[j, WO])

        def term(index):
            columns = pl.ds(pl.multiple_of(index * width, width), width)
            return jnp.dot(att[...], wo[j, :, columns], preferred_element_type=F32)

        def term_at(d, distance):
            return term(around(z, distance if d == 0 else -distance, n_tp))

        rsfo[j] = term_at(0, 4).astype(BF16)
        for q in range(PIECES):
            rs_far(j, q).start()
        for d in range(2):
            rso[j, d, 0] = term_at(d, 3).astype(BF16)
            for q in range(PIECES):
                rs_copy(j, d, 0, q).start()
        for d in range(2):
            terms[d] = term_at(d, 2)
        own[j + 1] = term(z).astype(BF16)

        @pl.when((j == 1) & jnp.logical_not(last_pair))
        def _():
            pass_copy(own, 1).start()

        for q in range(PIECES):
            at = slice(q * part, (q + 1) * part)
            for d in (side(q), 1 - side(q)):
                arrive(rsb.at[j, d, 0, span(q)], rs_recv.at[j, d, 0, q])
                value = terms[d, at] + rsb[j, d, 0, at].astype(F32)
                if d == side(q):
                    arrive(rsf.at[j, span(q)], rs_recv.at[j, d, FAR, q])
                    value = value + rsf[j, at].astype(F32)
                rso[j, d, 1, at] = value.astype(BF16)
                rs_copy(j, d, 1, q).start()
        for d in range(2):
            terms[d] = term_at(d, 1)
        for q in range(PIECES):
            at = slice(q * part, (q + 1) * part)
            for d in range(2):
                arrive(rsb.at[j, d, 1, span(q)], rs_recv.at[j, d, 1, q])
                rso[j, d, 2, at] = (terms[d, at] + rsb[j, d, 1, at].astype(F32)).astype(BF16)
                prt_copy(j, d, q).start()
        return carry

    lax.fori_loop(0, 2, layer, 0)

    @pl.when(last_pair)
    def _():
        for q in range(PIECES):
            join(2, q)
        wide = hidden[3].astype(F32)
        folded = fold(wide * wide)
        row = jnp.sum(jnp.transpose(folded), axis=0, keepdims=True)
        ssb[0] = jnp.broadcast_to(row, (8, rows))
        for i in range(1, n_tp):
            ss_copy(i).start()
        for i in range(1, n_tp):
            ss_copy(i).wait_recv()
        row = jnp.sum(ssb[...], axis=0)[:1]
        column = jnp.transpose(jnp.broadcast_to(row, (rows, rows)))[:, :1]
        scale = lax.rsqrt(column * (1.0 / full_width) + 1e-5)
        n = lengths[e]
        position = c * rows + lax.broadcasted_iota(jnp.int32, (rows, 1), 0)
        scale = jnp.where(position < n, scale, 0.0)
        pooled = jnp.sum(hidden[3].astype(F32) * scale, axis=0, keepdims=True)
        ppb[0] = jnp.broadcast_to(pooled * closing[...] / n.astype(F32), (8, width))
        for i in range(1, n_ctx):
            pp_copy(i).start()
        for i in range(1, n_ctx):
            pp_copy(i).wait_recv()
        pooled = jnp.sum(ppb[...], axis=0)
        sqb[0] = jnp.broadcast_to(jnp.sum(pooled * pooled, axis=1, keepdims=True), (8, HEAD))
        for i in range(1, n_tp):
            sq_copy(i).start()
        for i in range(1, n_tp):
            sq_copy(i).wait_recv()
        norms = jnp.sum(sqb[...], axis=0)[:, :1]
        res[e] = pooled * lax.rsqrt(norms * (1.0 / full_width) + 1e-6)
        for i in range(1, sections):
            fin_copy(i).start()
        arrive(res.at[1 - e], fin_recv.at[1 - e])
        for i in range(1, n_ctx):
            pp_copy(i).wait_send()
        for i in range(1, n_tp):
            sq_copy(i).wait_send()
            ss_copy(i).wait_send()
        for i in range(1, sections):
            fin_copy(i).wait_send()

    @pl.when(jnp.logical_not(last_pair))
    def _():
        pass_copy(hidden, 0).wait_send()
        pass_copy(own, 1).wait_send()
        for i in range(micro):
            arrive(res.at[i], fin_recv.at[i])

    for i in range(micro):
        out[i:i + 1] = res[i, :1]

    for item in range(7):
        weight_copy(item).wait_send()
    for j in range(2):
        for q in range(PIECES):
            for d in range(2):
                for r in range(3):
                    ag_copy(j, d, r, q, agb.at[j, d, r]).wait_send()
                for r in range(2):
                    rs_copy(j, d, r, q).wait_send()
                prt_copy(j, d, q).wait_send()
            ag_far(j, q).wait_send()
            rs_far(j, q).wait_send()
        for offset in NEAR + REST:
            kv_copy(j, offset).wait_send()


def build(mesh):
    sections, n_ctx, n_tp = (mesh.shape[a] for a in ("section", "ctx", "tp"))

    def shards(
        tokens, document_lengths, tenant_indices, attention_norm_gain, query_weight, key_weight,
        value_weight, output_weight, query_adapter_down, query_adapter_up, value_adapter_down,
        value_adapter_up, closing_norm_gain,
    ):
        micro, rows, width = tokens.shape
        query_width = query_weight.shape[2]
        tenant_count, rank = query_adapter_down.shape[1], query_adapter_down.shape[3]
        heads = query_width // HEAD

        freq = (500000.0 ** (-np.arange(HEAD // 2) / (HEAD // 2))).astype(np.float32)
        angle = np.arange(rows * n_ctx, dtype=np.float32)[:, None] * freq[None, :]
        cosine, sine = np.cos(angle.astype(np.float64)), np.sin(angle.astype(np.float64))
        tables = np.stack([np.concatenate([cosine, cosine], 1), np.concatenate([-sine, sine], 1)])
        tables = tables.reshape(2, n_ctx, rows, HEAD).transpose(1, 0, 2, 3).astype(np.float32)

        vmem = pl.BlockSpec(memory_space=pltpu.VMEM)
        hbm = pl.BlockSpec(memory_space=pl.ANY)
        smem = pl.BlockSpec(memory_space=pltpu.SMEM)
        dma = pltpu.SemaphoreType.DMA
        block = (rows, width)

        def body(*refs):
            kernel((sections, n_ctx, n_tp, micro, rows, width), *refs)

        return pl.pallas_call(
            body,
            out_shape=jax.ShapeDtypeStruct((micro, width), F32),
            in_specs=[smem, smem, hbm, hbm, vmem, hbm, hbm, hbm, hbm, hbm, hbm, hbm, vmem, vmem],
            out_specs=vmem,
            scratch_shapes=[
                pltpu.VMEM((2, n_tp, width, query_width), BF16),
                pltpu.VMEM((2, n_tp, width, 2 * HEAD), BF16),
                pltpu.VMEM((2, query_width, width * n_tp), BF16),
                pltpu.VMEM((2, 1, width * n_tp), F32),
                pltpu.VMEM((tenant_count, rank, width * n_tp), BF16),
                pltpu.VMEM((tenant_count, rank, width * n_tp), BF16),
                pltpu.VMEM((3, 2 * rank, width * n_tp), BF16),
                pltpu.VMEM((3, 2 * rank, query_width + HEAD), BF16),
                pltpu.VMEM((2, rows, HEAD), F32),
                pltpu.VMEM((4,) + block, BF16),
                pltpu.VMEM((3,) + block, BF16),
                pltpu.VMEM((2, 2, 3) + block, BF16),
                pltpu.VMEM((2,) + block, BF16),
                pltpu.VMEM((2, 2, 2) + block, BF16),
                pltpu.VMEM((2,) + block, BF16),
                pltpu.VMEM((2, 2, 3) + block, BF16),
                pltpu.VMEM((2,) + block, BF16),
                pltpu.VMEM((3, 2) + block, BF16),
                pltpu.VMEM((2, n_ctx, rows, 2 * HEAD), BF16),
                pltpu.VMEM((rows, query_width), F32),
                pltpu.VMEM((rows, 2 * HEAD), F32),
                pltpu.VMEM((rows, 2 * rank), F32),
                pltpu.VMEM((rows, HEAD), F32),
                pltpu.VMEM((heads, rows, HEAD), BF16),
                pltpu.VMEM((rows, query_width), BF16),
                pltpu.VMEM((2,) + block, F32),
                pltpu.VMEM((n_tp, 8, rows), F32),
                pltpu.VMEM((n_ctx, 8, width), F32),
                pltpu.VMEM((n_tp, 8, HEAD), F32),
                pltpu.VMEM((micro, 8, width), F32),
                dma((2, 7)),
                dma((7,)),
                dma((3,)),
                dma((1,)),
                dma((2, 2, 4, PIECES)),
                dma((2, 2, 4, PIECES)),
                dma((2, 2, 4, PIECES)),
                dma((2, 2, 4, PIECES)),
                dma((3, 2, PIECES)),
                dma((2, n_ctx)),
                dma((2, n_ctx)),
                dma((2,)),
                dma((2,)),
                dma((n_tp,)),
                dma((n_tp,)),
                dma((n_ctx,)),
                dma((n_ctx,)),
                dma((n_tp,)),
                dma((n_tp,)),
                dma((sections,)),
                dma((micro,)),
            ],
            compiler_params=pltpu.CompilerParams(
                collective_id=0, has_side_effects=True, vmem_limit_bytes=60 << 20),
            cost_estimate=pl.CostEstimate(
                flops=micro * 2 * rows * (n_tp * width * (query_width + 3 * HEAD) * 2),
                bytes_accessed=16 << 20, transcendentals=micro * heads * rows * rows * n_ctx),
        )(
            document_lengths, tenant_indices, tokens, attention_norm_gain,
            closing_norm_gain.reshape(1, width), jnp.asarray(tables),
            query_weight.reshape(n_tp, width, query_width),
            key_weight.reshape(n_tp, width, HEAD), value_weight.reshape(n_tp, width, HEAD),
            output_weight[0],
            jnp.swapaxes(query_adapter_down[0], 1, 2), jnp.swapaxes(value_adapter_down[0], 1, 2),
            query_adapter_up[0], value_adapter_up[0],
        )

    return shards


def solution(mesh):
    placed = (
        P(None, "ctx", "tp"),
        P(),
        P(),
        P("section", None),
        P("section", None, "tp"),
        P("section", None, "tp"),
        P("section", None, "tp"),
        P("section", "tp", None),
        P("section", None, None, None),
        P("section", None, None, "tp"),
        P("section", None, None, None),
        P("section", None, None, "tp"),
        P("tp"),
    )
    return jax.shard_map(
        build(mesh), mesh=mesh, in_specs=placed, out_specs=P(None, "tp"), check_vma=False
    )
```

```python
import math

import jax
import jax.numpy as jnp
import numpy as np
from jax import lax
from jax.experimental import pallas as pl
from jax.experimental.pallas import tpu as pltpu
from jax.sharding import PartitionSpec as P

HEAD = 128
F32 = jnp.float32
BF16 = jnp.bfloat16
MESH = pl.DeviceIdType.MESH

PIECES = 4
FAR = 3
WK, WV, WQ, GAIN, WO, DOWN, UP = range(7)
NEAR = ((1, 0), (0, 1), (0, 3))
REST = ((1, 1), (1, 3), (0, 2), (1, 2))


def fold(x):
    total = x[:, :HEAD]
    for i in range(1, x.shape[1] // HEAD):
        total = total + x[:, i * HEAD:(i + 1) * HEAD]
    return total


def kernel(
    sizes,
    lengths, tenants, tokens, gain_hbm, closing, tables, wq_hbm, wk_hbm, wv_hbm, wo_hbm,
    qd_hbm, vd_hbm, q_up, v_up,
    out,
    wq, wkv, wo, gains, qd, vd, down, up, trig,
    hidden, own, agb, agf, rsb, rsf, rso, rsfo, prt, kvbuf,
    acc_q, acc_kv, acc_l, squares, qbuf, att, terms,
    ssb, ppb, sqb, res,
    w_sem, w_send, small_sem, in_sem, ag_send, ag_recv, rs_send, rs_recv, prt_recv,
    kv_send, kv_recv, pass_send, pass_recv, ss_send, ss_recv, pp_send, pp_recv, sq_send, sq_recv,
    fin_send, fin_recv,
):
    sections, n_ctx, n_tp, micro, rows, width = sizes
    full_width = width * n_tp
    part = rows // PIECES
    heads = wq.shape[3] // HEAD
    rank = q_up.shape[1]
    s = lax.axis_index("section")
    c = lax.axis_index("ctx")
    z = lax.axis_index("tp")
    e = lax.rem(s, 2)
    first_pair = s < 2
    last_pair = s >= sections - 2
    partner = s + 1 - 2 * e

    def around(at, by, n):
        return lax.rem(at + (by + n), n)

    def remote(src, dst, send, recv, **to):
        return pltpu.make_async_remote_copy(
            src_ref=src, dst_ref=dst, send_sem=send, recv_sem=recv, device_id=to, device_id_type=MESH)

    def arrive(ref, sem):
        pltpu.make_async_copy(ref, ref, sem).wait()

    def span(q):
        return pl.ds(q * part, part)

    def side(q):
        return q * 2 // PIECES

    def token_copy():
        return pltpu.make_async_copy(tokens.at[e], hidden.at[1], in_sem.at[0])

    def weight(item, j):
        return {
            WK: lambda: wkv.at[j, :, :, pl.ds(0, HEAD)],
            WV: lambda: wkv.at[j, :, :, pl.ds(HEAD, HEAD)],
            WQ: lambda: wq.at[j],
            GAIN: lambda: gains.at[j],
            WO: lambda: wo.at[j],
            DOWN: lambda: down.at[j],
            UP: lambda: up.at[j],
        }[item]()

    sources = {WK: wk_hbm, WV: wv_hbm, WQ: wq_hbm, GAIN: gain_hbm, WO: wo_hbm}
    spare = {DOWN: down.at[2], UP: up.at[2]}

    def weight_copy(item):
        return remote({**sources, **spare}[item], weight(item, e), w_send.at[item], w_sem.at[e, item],
                      section=partner)

    small_copies = [
        pltpu.make_async_copy(qd_hbm, qd, small_sem.at[0]),
        pltpu.make_async_copy(vd_hbm, vd, small_sem.at[1]),
        pltpu.make_async_copy(tables.at[c], trig, small_sem.at[2]),
    ]

    @pl.when(first_pair)
    def _():
        token_copy().start()

    for copy in small_copies:
        copy.start()
    for item, source in sources.items():
        pltpu.make_async_copy(source, weight(item, e), w_sem.at[e, item]).start()

    barrier = pltpu.get_barrier_semaphore()
    neighbour = (around(z, 1, n_tp), around(z, -1, n_tp))
    peers = [{"tp": around(z, i, n_tp)} for i in range(1, n_tp)]
    peers += [{"ctx": around(c, i, n_ctx)} for i in range(1, n_ctx)]
    peers += [{"section": around(s, i, sections)} for i in range(1, sections)]
    peers += [{"section": around(s, 2, sections), "tp": neighbour[d]} for d in range(2)]
    for peer in peers:
        pl.semaphore_signal(barrier, 1, device_id=peer, device_id_type=MESH)

    for copy in small_copies:
        copy.wait()
    for slot, document in ((e, e), (2, 1 - e)):
        t = tenants[document]
        up[slot] = jnp.zeros(up.shape[1:], BF16)
        down[slot, :rank] = qd[t]
        down[slot, rank:] = vd[t]
        up[slot, :rank, :heads * HEAD] = q_up[t]
        up[slot, rank:, heads * HEAD:] = v_up[t]

    pl.semaphore_wait(barrier, len(peers))

    two_on = (around(z, 2, n_tp), around(z, -2, n_tp))

    def ag_copy(j, d, r, q, src):
        return remote(src.at[span(q)], agb.at[j, d, r, span(q)], ag_send.at[j, d, r, q],
                      ag_recv.at[j, d, r, q], tp=neighbour[d])

    def ag_far(j, q):
        d = side(q)
        return remote(agb.at[j, d, 1, span(q)], agf.at[j, span(q)], ag_send.at[j, d, FAR, q],
                      ag_recv.at[j, d, FAR, q], tp=two_on[d])

    def rs_copy(j, d, r, q):
        return remote(rso.at[j, d, r, span(q)], rsb.at[j, d, r, span(q)], rs_send.at[j, d, r, q],
                      rs_recv.at[j, d, r, q], tp=neighbour[d])

    def rs_far(j, q):
        d = side(q)
        return remote(rsfo.at[j, span(q)], rsf.at[j, span(q)], rs_send.at[j, d, FAR, q],
                      rs_recv.at[j, d, FAR, q], tp=two_on[d])

    def prt_copy(j, d, q):
        slot = jnp.where(j == 0, 1, jnp.where(last_pair, 2, 0))
        where = jnp.where((j == 1) & jnp.logical_not(last_pair), around(s, 2, sections), s)
        return remote(rso.at[j, d, 2, span(q)], prt.at[slot, d, span(q)], rs_send.at[j, d, 2, q],
                      prt_recv.at[slot, d, q], tp=neighbour[d], section=where)

    def pass_copy(buf, i):
        return remote(buf.at[2], buf.at[0], pass_send.at[i], pass_recv.at[i], section=around(s, 2, sections))

    def ctx_peer(dy, dx):
        across = n_ctx // 2
        return around(c // across, dy, 2) * across + around(lax.rem(c, across), dx, across)

    def kv_copy(j, offset):
        dy, dx = offset
        i = dy * (n_ctx // 2) + dx
        return remote(kvbuf.at[j, c], kvbuf.at[j, c], kv_send.at[j, i], kv_recv.at[j, i],
                      ctx=ctx_peer(dy, dx))

    def ss_copy(i):
        return remote(ssb.at[0], ssb.at[i], ss_send.at[i], ss_recv.at[i], tp=around(z, i, n_tp))

    def pp_copy(i):
        return remote(ppb.at[0], ppb.at[i], pp_send.at[i], pp_recv.at[i], ctx=around(c, i, n_ctx))

    def sq_copy(i):
        return remote(sqb.at[0], sqb.at[i], sq_send.at[i], sq_recv.at[i], tp=around(z, i, n_tp))

    def fin_copy(i):
        return remote(res.at[e], res.at[e], fin_send.at[i], fin_recv.at[e], section=around(s, i, sections))

    def rotate(x):
        return x * trig[0] + pltpu.roll(x, HEAD // 2, axis=1) * trig[1]

    def take(j, blocks, first=False):
        values = None
        for block, g in blocks:
            h = block.astype(F32)
            columns = pl.ds(pl.multiple_of(g * width, width), width)
            x = (h * gains[j, :, columns]).astype(BF16)
            new = (
                fold(h * h),
                jnp.dot(x, wkv[j, g], preferred_element_type=F32),
                lax.dot_general(x, down[j, :, columns], (((1,), (1,)), ((), ())), preferred_element_type=F32),
                jnp.dot(x, wq[j, g], preferred_element_type=F32),
            )
            values = new if values is None else [a + b for a, b in zip(values, new)]
        for ref, value in zip((squares, acc_kv, acc_l, acc_q), values):
            ref[...] = value if first else ref[...] + value

    def join(i, q):
        for d in range(2):
            arrive(prt.at[i, d, span(q)], prt_recv.at[i, d, q])
        at = slice(q * part, (q + 1) * part)
        sums = prt[i, 0, at].astype(F32) + prt[i, 1, at].astype(F32)
        hidden[i + 1, at] = (hidden[i, at].astype(F32) + own[i, at].astype(F32) + sums).astype(BF16)

    def layer(j, carry):
        @pl.when(first_pair & (j == 0))
        def _():
            token_copy().wait()

        @pl.when(jnp.logical_not(first_pair) & (j == 0))
        def _():
            arrive(hidden.at[0], pass_recv.at[0])
            arrive(own.at[0], pass_recv.at[1])

        for q in range(PIECES):
            @pl.when(jnp.logical_not(first_pair) | (j == 1))
            def _():
                join(j, q)

            for d in range(2):
                ag_copy(j, d, 0, q, hidden.at[j + 1]).start()

        @pl.when(j == 0)
        def _():
            for item in (GAIN, DOWN, UP, WK, WV, WQ):
                weight_copy(item).start()

        @pl.when((j == 1) & jnp.logical_not(last_pair))
        def _():
            pass_copy(hidden, 0).start()

        def own_take():
            for item in (GAIN, WK, WV, WQ):
                arrive(weight(item, j), w_sem.at[j, item])

            @pl.when(j != e)
            def _():
                for item in (DOWN, UP):
                    arrive(weight(item, j), w_sem.at[j, item])

            take(j, [(hidden[j + 1], z)], first=True)

        def pair_take(r):
            take(j, [(agb[j, d, r], around(z, -1 - r if d == 0 else 1 + r, n_tp)) for d in range(2)])

        late = first_pair & (e == 1) & (j == 0)
        prompt = jnp.logical_not(late)

        @pl.when(prompt)
        def _():
            own_take()

        for r in range(3):
            for q in range(PIECES):
                for d in range(2):
                    arrive(agb.at[j, d, r, span(q)], ag_recv.at[j, d, r, q])
                    if r < 2:
                        ag_copy(j, d, r + 1, q, agb.at[j, d, r]).start()
                    if r == 1 and d == side(q):
                        ag_far(j, q).start()

            @pl.when(prompt)
            def _():
                pair_take(r)

        @pl.when(j == 0)
        def _():
            weight_copy(WO).start()

        @pl.when(late)
        def _():
            own_take()

            def after(r, carry):
                pair_take(r)
                return carry

            lax.fori_loop(0, 3, after, 0)

        for q in range(PIECES):
            arrive(agf.at[j, span(q)], ag_recv.at[j, side(q), FAR, q])
        take(j, [(agf[j], around(z, 4, n_tp))])

        mean = jnp.sum(squares[...], axis=1, keepdims=True) * (1.0 / full_width)
        scale = lax.rsqrt(mean + 1e-5)
        low = (acc_l[...] * scale).astype(BF16)
        kv = acc_kv[...] * scale
        kvbuf[j, c, :, :HEAD] = rotate(kv[:, :HEAD]).astype(BF16)
        added = jnp.dot(low, up[j, :, heads * HEAD:], preferred_element_type=F32)
        kvbuf[j, c, :, HEAD:] = (kv[:, HEAD:] + added).astype(BF16)
        for offset in NEAR + REST:
            kv_copy(j, offset).start()
        factor = HEAD ** -0.5 * math.log2(math.e)
        for g in range(heads):
            cols = slice(g * HEAD, (g + 1) * HEAD)
            q = acc_q[:, cols] * scale + jnp.dot(low, up[j, :, cols], preferred_element_type=F32)
            qbuf[g] = (rotate(q) * factor).astype(BF16)

        n = lengths[e]
        lane = lax.broadcasted_iota(jnp.int32, (1, rows), 1)

        def keys_of(offsets):
            sources = [ctx_peer(-dy, -dx) for dy, dx in offsets]
            blocks = [kvbuf[j, source] for source in sources]
            valid = jnp.concatenate([lane + source * rows < n for source in sources], axis=1)
            return (jnp.concatenate([block[:, :HEAD] for block in blocks], axis=0),
                    jnp.concatenate([block[:, HEAD:] for block in blocks], axis=0), valid)

        def scored(g, keys, valid):
            scores = lax.dot_general(
                qbuf[g], keys, (((1,), (1,)), ((), ())), preferred_element_type=F32)
            return jnp.where(valid, scores, -1e30)

        for offset in NEAR:
            kv_copy(j, offset).wait_recv()
        keys, values, valid = keys_of(((0, 0),) + NEAR)
        near = []
        for g in range(heads):
            scores = scored(g, keys, valid)
            top = jnp.max(scores, axis=1, keepdims=True)
            weights = jnp.exp2(scores - top)
            total = jnp.sum(weights, axis=1, keepdims=True)
            near.append((top, total, jnp.dot(weights.astype(BF16), values, preferred_element_type=F32)))
        for offset in REST:
            kv_copy(j, offset).wait_recv()
        keys, values, valid = keys_of(REST)
        for g in range(heads):
            top_near, total_near, mixed_near = near[g]
            scores = scored(g, keys, valid)
            top = jnp.maximum(jnp.max(scores, axis=1, keepdims=True), top_near)
            weights = jnp.exp2(scores - top)
            fade = jnp.exp2(top_near - top)
            total = jnp.sum(weights, axis=1, keepdims=True) + total_near * fade
            mixed = jnp.dot(weights.astype(BF16), values, preferred_element_type=F32) + mixed_near * fade
            att[:, g * HEAD:(g + 1) * HEAD] = (mixed * (1.0 / total)).astype(BF16)

        arrive(weight(WO, j), w_sem.at[j, WO])

        def term(index):
            columns = pl.ds(pl.multiple_of(index * width, width), width)
            return jnp.dot(att[...], wo[j, :, columns], preferred_element_type=F32)

        def term_at(d, distance):
            return term(around(z, distance if d == 0 else -distance, n_tp))

        rsfo[j] = term_at(0, 4).astype(BF16)
        for q in range(PIECES):
            rs_far(j, q).start()
        for d in range(2):
            rso[j, d, 0] = term_at(d, 3).astype(BF16)
            for q in range(PIECES):
                rs_copy(j, d, 0, q).start()
        for d in range(2):
            terms[d] = term_at(d, 2)
        own[j + 1] = term(z).astype(BF16)

        @pl.when((j == 1) & jnp.logical_not(last_pair))
        def _():
            pass_copy(own, 1).start()

        for q in range(PIECES):
            at = slice(q * part, (q + 1) * part)
            for d in (side(q), 1 - side(q)):
                arrive(rsb.at[j, d, 0, span(q)], rs_recv.at[j, d, 0, q])
                value = terms[d, at] + rsb[j, d, 0, at].astype(F32)
                if d == side(q):
                    arrive(rsf.at[j, span(q)], rs_recv.at[j, d, FAR, q])
                    value = value + rsf[j, at].astype(F32)
                rso[j, d, 1, at] = value.astype(BF16)
                rs_copy(j, d, 1, q).start()
        for d in range(2):
            terms[d] = term_at(d, 1)
        for q in range(PIECES):
            at = slice(q * part, (q + 1) * part)
            for d in range(2):
                arrive(rsb.at[j, d, 1, span(q)], rs_recv.at[j, d, 1, q])
                rso[j, d, 2, at] = (terms[d, at] + rsb[j, d, 1, at].astype(F32)).astype(BF16)
                prt_copy(j, d, q).start()
        return carry

    lax.fori_loop(0, 2, layer, 0)

    @pl.when(last_pair)
    def _():
        for q in range(PIECES):
            join(2, q)
        wide = hidden[3].astype(F32)
        folded = fold(wide * wide)
        row = jnp.sum(jnp.transpose(folded), axis=0, keepdims=True)
        ssb[0] = jnp.broadcast_to(row, (8, rows))
        for i in range(1, n_tp):
            ss_copy(i).start()
        for i in range(1, n_tp):
            ss_copy(i).wait_recv()
        row = jnp.sum(ssb[...], axis=0)[:1]
        column = jnp.transpose(jnp.broadcast_to(row, (rows, rows)))[:, :1]
        scale = lax.rsqrt(column * (1.0 / full_width) + 1e-5)
        n = lengths[e]
        position = c * rows + lax.broadcasted_iota(jnp.int32, (rows, 1), 0)
        scale = jnp.where(position < n, scale, 0.0)
        pooled = jnp.sum(hidden[3].astype(F32) * scale, axis=0, keepdims=True)
        ppb[0] = jnp.broadcast_to(pooled * closing[...] / n.astype(F32), (8, width))
        for i in range(1, n_ctx):
            pp_copy(i).start()
        for i in range(1, n_ctx):
            pp_copy(i).wait_recv()
        pooled = jnp.sum(ppb[...], axis=0)
        sqb[0] = jnp.broadcast_to(jnp.sum(pooled * pooled, axis=1, keepdims=True), (8, HEAD))
        for i in range(1, n_tp):
            sq_copy(i).start()
        for i in range(1, n_tp):
            sq_copy(i).wait_recv()
        norms = jnp.sum(sqb[...], axis=0)[:, :1]
        res[e] = pooled * lax.rsqrt(norms * (1.0 / full_width) + 1e-6)
        for i in range(1, sections):
            fin_copy(i).start()
        arrive(res.at[1 - e], fin_recv.at[1 - e])
        for i in range(1, n_ctx):
            pp_copy(i).wait_send()
        for i in range(1, n_tp):
            sq_copy(i).wait_send()
            ss_copy(i).wait_send()
        for i in range(1, sections):
            fin_copy(i).wait_send()

    @pl.when(jnp.logical_not(last_pair))
    def _():
        pass_copy(hidden, 0).wait_send()
        pass_copy(own, 1).wait_send()
        for i in range(micro):
            arrive(res.at[i], fin_recv.at[i])

    for i in range(micro):
        out[i:i + 1] = res[i, :1]

    for item in range(7):
        weight_copy(item).wait_send()
    for j in range(2):
        for q in range(PIECES):
            for d in range(2):
                for r in range(3):
                    ag_copy(j, d, r, q, agb.at[j, d, r]).wait_send()
                for r in range(2):
                    rs_copy(j, d, r, q).wait_send()
                prt_copy(j, d, q).wait_send()
            ag_far(j, q).wait_send()
            rs_far(j, q).wait_send()
        for offset in NEAR + REST:
            kv_copy(j, offset).wait_send()


def build(mesh):
    sections, n_ctx, n_tp = (mesh.shape[a] for a in ("section", "ctx", "tp"))

    def shards(
        tokens, document_lengths, tenant_indices, attention_norm_gain, query_weight, key_weight,
        value_weight, output_weight, query_adapter_down, query_adapter_up, value_adapter_down,
        value_adapter_up, closing_norm_gain,
    ):
        micro, rows, width = tokens.shape
        query_width = query_weight.shape[2]
        tenant_count, rank = query_adapter_down.shape[1], query_adapter_down.shape[3]
        heads = query_width // HEAD

        freq = (500000.0 ** (-np.arange(HEAD // 2) / (HEAD // 2))).astype(np.float32)
        angle = np.arange(rows * n_ctx, dtype=np.float32)[:, None] * freq[None, :]
        cosine, sine = np.cos(angle.astype(np.float64)), np.sin(angle.astype(np.float64))
        tables = np.stack([np.concatenate([cosine, cosine], 1), np.concatenate([-sine, sine], 1)])
        tables = tables.reshape(2, n_ctx, rows, HEAD).transpose(1, 0, 2, 3).astype(np.float32)

        vmem = pl.BlockSpec(memory_space=pltpu.VMEM)
        hbm = pl.BlockSpec(memory_space=pl.ANY)
        smem = pl.BlockSpec(memory_space=pltpu.SMEM)
        dma = pltpu.SemaphoreType.DMA
        block = (rows, width)

        def body(*refs):
            kernel((sections, n_ctx, n_tp, micro, rows, width), *refs)

        return pl.pallas_call(
            body,
            out_shape=jax.ShapeDtypeStruct((micro, width), F32),
            in_specs=[smem, smem, hbm, hbm, vmem, hbm, hbm, hbm, hbm, hbm, hbm, hbm, vmem, vmem],
            out_specs=vmem,
            scratch_shapes=[
                pltpu.VMEM((2, n_tp, width, query_width), BF16),
                pltpu.VMEM((2, n_tp, width, 2 * HEAD), BF16),
                pltpu.VMEM((2, query_width, width * n_tp), BF16),
                pltpu.VMEM((2, 1, width * n_tp), F32),
                pltpu.VMEM((tenant_count, rank, width * n_tp), BF16),
                pltpu.VMEM((tenant_count, rank, width * n_tp), BF16),
                pltpu.VMEM((3, 2 * rank, width * n_tp), BF16),
                pltpu.VMEM((3, 2 * rank, query_width + HEAD), BF16),
                pltpu.VMEM((2, rows, HEAD), F32),
                pltpu.VMEM((4,) + block, BF16),
                pltpu.VMEM((3,) + block, BF16),
                pltpu.VMEM((2, 2, 3) + block, BF16),
                pltpu.VMEM((2,) + block, BF16),
                pltpu.VMEM((2, 2, 2) + block, BF16),
                pltpu.VMEM((2,) + block, BF16),
                pltpu.VMEM((2, 2, 3) + block, BF16),
                pltpu.VMEM((2,) + block, BF16),
                pltpu.VMEM((3, 2) + block, BF16),
                pltpu.VMEM((2, n_ctx, rows, 2 * HEAD), BF16),
                pltpu.VMEM((rows, query_width), F32),
                pltpu.VMEM((rows, 2 * HEAD), F32),
                pltpu.VMEM((rows, 2 * rank), F32),
                pltpu.VMEM((rows, HEAD), F32),
                pltpu.VMEM((heads, rows, HEAD), BF16),
                pltpu.VMEM((rows, query_width), BF16),
                pltpu.VMEM((2,) + block, F32),
                pltpu.VMEM((n_tp, 8, rows), F32),
                pltpu.VMEM((n_ctx, 8, width), F32),
                pltpu.VMEM((n_tp, 8, HEAD), F32),
                pltpu.VMEM((micro, 8, width), F32),
                dma((2, 7)),
                dma((7,)),
                dma((3,)),
                dma((1,)),
                dma((2, 2, 4, PIECES)),
                dma((2, 2, 4, PIECES)),
                dma((2, 2, 4, PIECES)),
                dma((2, 2, 4, PIECES)),
                dma((3, 2, PIECES)),
                dma((2, n_ctx)),
                dma((2, n_ctx)),
                dma((2,)),
                dma((2,)),
                dma((n_tp,)),
                dma((n_tp,)),
                dma((n_ctx,)),
                dma((n_ctx,)),
                dma((n_tp,)),
                dma((n_tp,)),
                dma((sections,)),
                dma((micro,)),
            ],
            compiler_params=pltpu.CompilerParams(
                collective_id=0, has_side_effects=True, vmem_limit_bytes=60 << 20),
            cost_estimate=pl.CostEstimate(
                flops=micro * 2 * rows * (n_tp * width * (query_width + 3 * HEAD) * 2),
                bytes_accessed=16 << 20, transcendentals=micro * heads * rows * rows * n_ctx),
        )(
            document_lengths, tenant_indices, tokens, attention_norm_gain,
            closing_norm_gain.reshape(1, width), jnp.asarray(tables),
            query_weight.reshape(n_tp, width, query_width),
            key_weight.reshape(n_tp, width, HEAD), value_weight.reshape(n_tp, width, HEAD),
            output_weight[0],
            jnp.swapaxes(query_adapter_down[0], 1, 2), jnp.swapaxes(value_adapter_down[0], 1, 2),
            query_adapter_up[0], value_adapter_up[0],
        )

    return shards


def solution(mesh):
    placed = (
        P(None, "ctx", "tp"),
        P(),
        P(),
        P("section", None),
        P("section", None, "tp"),
        P("section", None, "tp"),
        P("section", None, "tp"),
        P("section", "tp", None),
        P("section", None, None, None),
        P("section", None, None, "tp"),
        P("section", None, None, None),
        P("section", None, None, "tp"),
        P("tp"),
    )
    return jax.shard_map(
        build(mesh), mesh=mesh, in_specs=placed, out_specs=P(None, "tp"), check_vma=False
    )
```

```python
import math

import jax
import jax.numpy as jnp
import numpy as np
from jax import lax
from jax.experimental import pallas as pl
from jax.experimental.pallas import tpu as pltpu
from jax.sharding import PartitionSpec as P

HEAD = 128
F32 = jnp.float32
BF16 = jnp.bfloat16
MESH = pl.DeviceIdType.MESH

PIECES = 4
FAR = 3
WK, WV, WQ, GAIN, WO, DOWN, UP = range(7)
NEAR = ((1, 0), (0, 1), (0, 3))
REST = ((1, 1), (1, 3), (0, 2), (1, 2))


def fold(x):
    total = x[:, :HEAD]
    for i in range(1, x.shape[1] // HEAD):
        total = total + x[:, i * HEAD:(i + 1) * HEAD]
    return total


def kernel(
    sizes,
    lengths, tenants, tokens, gain_hbm, closing, tables, wq_hbm, wk_hbm, wv_hbm, wo_hbm,
    qd_hbm, vd_hbm, q_up, v_up,
    out,
    wq, wkv, wo, gains, qd, vd, down, up, trig,
    hidden, own, agb, agf, rsb, rsf, rso, rsfo, prt, kvbuf, mirror,
    acc_q, acc_kv, acc_l, squares, qbuf, att, terms,
    ssb, ppb, sqb, res,
    w_sem, w_send, small_sem, in_sem, ag_send, ag_recv, rs_send, rs_recv, prt_recv,
    kv_send, kv_recv, pass_send, pass_recv, ss_send, ss_recv, pp_send, pp_recv, sq_send, sq_recv,
    fin_send, fin_recv, mir_send, mir_recv, acc_send, acc_recv,
):
    sections, n_ctx, n_tp, micro, rows, width = sizes
    full_width = width * n_tp
    part = rows // PIECES
    heads = wq.shape[3] // HEAD
    rank = q_up.shape[1]
    s = lax.axis_index("section")
    c = lax.axis_index("ctx")
    z = lax.axis_index("tp")
    e = lax.rem(s, 2)
    first_pair = s < 2
    last_pair = s >= sections - 2
    partner = s + 1 - 2 * e
    helps = first_pair & (e == 0)

    def around(at, by, n):
        return lax.rem(at + (by + n), n)

    def remote(src, dst, send, recv, **to):
        return pltpu.make_async_remote_copy(
            src_ref=src, dst_ref=dst, send_sem=send, recv_sem=recv, device_id=to, device_id_type=MESH)

    def arrive(ref, sem):
        pltpu.make_async_copy(ref, ref, sem).wait()

    def span(q):
        return pl.ds(q * part, part)

    def side(q):
        return q * 2 // PIECES

    def token_copy():
        return pltpu.make_async_copy(tokens.at[e], hidden.at[1], in_sem.at[0])

    def weight(item, j):
        return {
            WK: lambda: wkv.at[j, :, :, pl.ds(0, HEAD)],
            WV: lambda: wkv.at[j, :, :, pl.ds(HEAD, HEAD)],
            WQ: lambda: wq.at[j],
            GAIN: lambda: gains.at[j],
            WO: lambda: wo.at[j],
            DOWN: lambda: down.at[j],
            UP: lambda: up.at[j],
        }[item]()

    sources = {WK: wk_hbm, WV: wv_hbm, WQ: wq_hbm, GAIN: gain_hbm, WO: wo_hbm}
    spare = {DOWN: down.at[2], UP: up.at[2]}

    def weight_copy(item):
        return remote({**sources, **spare}[item], weight(item, e), w_send.at[item], w_sem.at[e, item],
                      section=partner)

    small_copies = [
        pltpu.make_async_copy(qd_hbm, qd, small_sem.at[0]),
        pltpu.make_async_copy(vd_hbm, vd, small_sem.at[1]),
        pltpu.make_async_copy(tables.at[c], trig, small_sem.at[2]),
    ]

    @pl.when(first_pair)
    def _():
        token_copy().start()

    for copy in small_copies:
        copy.start()
    for item, source in sources.items():
        pltpu.make_async_copy(source, weight(item, e), w_sem.at[e, item]).start()

    barrier = pltpu.get_barrier_semaphore()
    neighbour = (around(z, 1, n_tp), around(z, -1, n_tp))
    peers = [{"tp": around(z, i, n_tp)} for i in range(1, n_tp)]
    peers += [{"ctx": around(c, i, n_ctx)} for i in range(1, n_ctx)]
    peers += [{"section": around(s, i, sections)} for i in range(1, sections)]
    peers += [{"section": around(s, 2, sections), "tp": neighbour[d]} for d in range(2)]
    for peer in peers:
        pl.semaphore_signal(barrier, 1, device_id=peer, device_id_type=MESH)

    for copy in small_copies:
        copy.wait()
    for slot, document in ((e, e), (2, 1 - e)):
        t = tenants[document]
        up[slot] = jnp.zeros(up.shape[1:], BF16)
        down[slot, :rank] = qd[t]
        down[slot, rank:] = vd[t]
        up[slot, :rank, :heads * HEAD] = q_up[t]
        up[slot, rank:, heads * HEAD:] = v_up[t]

    pl.semaphore_wait(barrier, len(peers))

    two_on = (around(z, 2, n_tp), around(z, -2, n_tp))

    def ag_copy(j, d, r, q, src):
        return remote(src.at[span(q)], agb.at[j, d, r, span(q)], ag_send.at[j, d, r, q],
                      ag_recv.at[j, d, r, q], tp=neighbour[d])

    def ag_far(j, q):
        d = side(q)
        return remote(agb.at[j, d, 1, span(q)], agf.at[j, span(q)], ag_send.at[j, d, FAR, q],
                      ag_recv.at[j, d, FAR, q], tp=two_on[d])

    def rs_copy(j, d, r, q):
        return remote(rso.at[j, d, r, span(q)], rsb.at[j, d, r, span(q)], rs_send.at[j, d, r, q],
                      rs_recv.at[j, d, r, q], tp=neighbour[d])

    def rs_far(j, q):
        d = side(q)
        return remote(rsfo.at[j, span(q)], rsf.at[j, span(q)], rs_send.at[j, d, FAR, q],
                      rs_recv.at[j, d, FAR, q], tp=two_on[d])

    def prt_copy(j, d, q):
        slot = jnp.where(j == 0, 1, jnp.where(last_pair, 2, 0))
        where = jnp.where((j == 1) & jnp.logical_not(last_pair), around(s, 2, sections), s)
        return remote(rso.at[j, d, 2, span(q)], prt.at[slot, d, span(q)], rs_send.at[j, d, 2, q],
                      prt_recv.at[slot, d, q], tp=neighbour[d], section=where)

    def pass_copy(buf, i):
        return remote(buf.at[2], buf.at[0], pass_send.at[i], pass_recv.at[i], section=around(s, 2, sections))

    def ctx_peer(dy, dx):
        across = n_ctx // 2
        return around(c // across, dy, 2) * across + around(lax.rem(c, across), dx, across)

    def kv_copy(j, offset):
        dy, dx = offset
        i = dy * (n_ctx // 2) + dx
        return remote(kvbuf.at[j, c], kvbuf.at[j, c], kv_send.at[j, i], kv_recv.at[j, i],
                      ctx=ctx_peer(dy, dx))

    def ss_copy(i):
        return remote(ssb.at[0], ssb.at[i], ss_send.at[i], ss_recv.at[i], tp=around(z, i, n_tp))

    def pp_copy(i):
        return remote(ppb.at[0], ppb.at[i], pp_send.at[i], pp_recv.at[i], ctx=around(c, i, n_ctx))

    def sq_copy(i):
        return remote(sqb.at[0], sqb.at[i], sq_send.at[i], sq_recv.at[i], tp=around(z, i, n_tp))

    def fin_copy(i):
        return remote(res.at[e], res.at[e], fin_send.at[i], fin_recv.at[e], section=around(s, i, sections))

    def mir_copy(slot, block):
        return remote(block, mirror.at[slot], mir_send.at[slot], mir_recv.at[slot], section=partner)

    def acc_copy(i):
        ref = (squares, acc_kv, acc_l, acc_q)[i]
        return remote(ref.at[1], ref.at[0], acc_send.at[i], acc_recv.at[i], section=partner)

    def rotate(x):
        return x * trig[0] + pltpu.roll(x, HEAD // 2, axis=1) * trig[1]

    def take(j, blocks, first=False, to=0, adapter=None):
        values = None
        for block, g in blocks:
            h = block.astype(F32)
            columns = pl.ds(pl.multiple_of(g * width, width), width)
            x = (h * gains[j, :, columns]).astype(BF16)
            new = (
                fold(h * h),
                jnp.dot(x, wkv[j, g], preferred_element_type=F32),
                lax.dot_general(x, down[j if adapter is None else adapter, :, columns], (((1,), (1,)), ((), ())), preferred_element_type=F32),
                jnp.dot(x, wq[j, g], preferred_element_type=F32),
            )
            values = new if values is None else [a + b for a, b in zip(values, new)]
        for ref, value in zip((squares, acc_kv, acc_l, acc_q), values):
            ref[to] = value if first else ref[to] + value

    def join(i, q):
        for d in range(2):
            arrive(prt.at[i, d, span(q)], prt_recv.at[i, d, q])
        at = slice(q * part, (q + 1) * part)
        sums = prt[i, 0, at].astype(F32) + prt[i, 1, at].astype(F32)
        hidden[i + 1, at] = (hidden[i, at].astype(F32) + own[i, at].astype(F32) + sums).astype(BF16)

    def layer(j, carry):
        @pl.when(first_pair & (j == 0))
        def _():
            token_copy().wait()

        @pl.when(jnp.logical_not(first_pair) & (j == 0))
        def _():
            arrive(hidden.at[0], pass_recv.at[0])
            arrive(own.at[0], pass_recv.at[1])

        for q in range(PIECES):
            @pl.when(jnp.logical_not(first_pair) | (j == 1))
            def _():
                join(j, q)

            for d in range(2):
                ag_copy(j, d, 0, q, hidden.at[j + 1]).start()

        @pl.when(j == 0)
        def _():
            weight_copy(UP).start()

            @pl.when(jnp.logical_not(helps))
            def _():
                for item in (GAIN, DOWN, WK, WV, WQ):
                    weight_copy(item).start()

        @pl.when((j == 1) & jnp.logical_not(last_pair))
        def _():
            pass_copy(hidden, 0).start()

        def own_take():
            for item in (GAIN, WK, WV, WQ):
                arrive(weight(item, j), w_sem.at[j, item])

            @pl.when(j != e)
            def _():
                for item in (DOWN, UP):
                    arrive(weight(item, j), w_sem.at[j, item])

            take(j, [(hidden[j + 1], z)], first=True)

        def owner(d, r):
            return around(z, -1 - r if d == 0 else 1 + r, n_tp)

        late = first_pair & (e == 1) & (j == 0)
        prompt = jnp.logical_not(late)

        @pl.when(prompt)
        def _():
            own_take()

        @pl.when(late)
        def _():
            mir_copy(0, hidden.at[1]).start()

        for r in range(3):
            for q in range(PIECES):
                for d in range(2):
                    arrive(agb.at[j, d, r, span(q)], ag_recv.at[j, d, r, q])
                    if r < 2:
                        ag_copy(j, d, r + 1, q, agb.at[j, d, r]).start()
                    if r == 1 and d == side(q):
                        ag_far(j, q).start()

            @pl.when(prompt)
            def _():
                take(j, [(agb[j, d, r], owner(d, r)) for d in range(2)])

            @pl.when(late)
            def _():
                for d in range(2):
                    mir_copy(1 + 2 * r + d, agb.at[j, d, r]).start()

        @pl.when(j == 0)
        def _():
            weight_copy(WO).start()

        for q in range(PIECES):
            arrive(agf.at[j, span(q)], ag_recv.at[j, side(q), FAR, q])

        @pl.when(prompt)
        def _():
            take(j, [(agf[j], around(z, 4, n_tp))])

        @pl.when(late)
        def _():
            mir_copy(7, agf.at[j]).start()
            arrive(weight(UP, 0), w_sem.at[0, UP])
            for i, ref in enumerate((squares, acc_kv, acc_l, acc_q)):
                arrive(ref.at[0], acc_recv.at[i])

        mean = jnp.sum(squares[0], axis=1, keepdims=True) * (1.0 / full_width)
        scale = lax.rsqrt(mean + 1e-5)
        low = (acc_l[0] * scale).astype(BF16)
        kv = acc_kv[0] * scale
        kvbuf[j, c, :, :HEAD] = jnp.transpose(rotate(kv[:, :HEAD])).astype(BF16)
        added = jnp.dot(low, up[j, :, heads * HEAD:], preferred_element_type=F32)
        kvbuf[j, c, :, HEAD:] = (kv[:, HEAD:] + added).astype(BF16)
        for offset in NEAR + REST:
            kv_copy(j, offset).start()

        @pl.when(helps & (j == 0))
        def _():
            for slots in ((0,), (1, 2), (3, 4), (5, 6), (7,)):
                for slot in slots:
                    arrive(mirror.at[slot], mir_recv.at[slot])
                owners = [z if slot == 0 else around(z, 4, n_tp) if slot == 7
                          else owner((slot - 1) % 2, (slot - 1) // 2) for slot in slots]
                take(0, [(mirror[slot], at) for slot, at in zip(slots, owners)],
                     first=slots == (0,), to=1, adapter=2)
            for i in range(4):
                acc_copy(i).start()

        factor = HEAD ** -0.5 * math.log2(math.e)
        for g in range(heads):
            cols = slice(g * HEAD, (g + 1) * HEAD)
            q = acc_q[0, :, cols] * scale + jnp.dot(low, up[j, :, cols], preferred_element_type=F32)
            qbuf[g] = (rotate(q) * factor).astype(BF16)

        n = lengths[e]
        lane = lax.broadcasted_iota(jnp.int32, (1, rows), 1)

        def keys_of(offsets):
            sources = [ctx_peer(-dy, -dx) for dy, dx in offsets]
            blocks = [kvbuf[j, source] for source in sources]
            valid = jnp.concatenate([lane + source * rows < n for source in sources], axis=1)
            return (jnp.concatenate([block[:, :HEAD] for block in blocks], axis=1),
                    jnp.concatenate([block[:, HEAD:] for block in blocks], axis=0), valid)

        def scored(g, keys, valid):
            scores = jnp.dot(qbuf[g], keys, preferred_element_type=F32)
            return jnp.where(valid, scores, -1e30)

        for offset in NEAR:
            kv_copy(j, offset).wait_recv()
        keys, values, valid = keys_of(((0, 0),) + NEAR)
        near = []
        for g in range(heads):
            scores = scored(g, keys, valid)
            top = jnp.max(scores, axis=1, keepdims=True)
            weights = jnp.exp2(scores - top)
            total = jnp.sum(weights, axis=1, keepdims=True)
            near.append((top, total, jnp.dot(weights.astype(BF16), values, preferred_element_type=F32)))
        for offset in REST:
            kv_copy(j, offset).wait_recv()
        keys, values, valid = keys_of(REST)
        for g in range(heads):
            top_near, total_near, mixed_near = near[g]
            scores = scored(g, keys, valid)
            top = jnp.maximum(jnp.max(scores, axis=1, keepdims=True), top_near)
            weights = jnp.exp2(scores - top)
            fade = jnp.exp2(top_near - top)
            total = jnp.sum(weights, axis=1, keepdims=True) + total_near * fade
            mixed = jnp.dot(weights.astype(BF16), values, preferred_element_type=F32) + mixed_near * fade
            att[:, g * HEAD:(g + 1) * HEAD] = (mixed * (1.0 / total)).astype(BF16)

        arrive(weight(WO, j), w_sem.at[j, WO])

        def term(index):
            columns = pl.ds(pl.multiple_of(index * width, width), width)
            return jnp.dot(att[...], wo[j, :, columns], preferred_element_type=F32)

        def term_at(d, distance):
            return term(around(z, distance if d == 0 else -distance, n_tp))

        rsfo[j] = term_at(0, 4).astype(BF16)
        for q in range(PIECES):
            rs_far(j, q).start()
        for d in range(2):
            rso[j, d, 0] = term_at(d, 3).astype(BF16)
            for q in range(PIECES):
                rs_copy(j, d, 0, q).start()
        for d in range(2):
            terms[d] = term_at(d, 2)
        own[j + 1] = term(z).astype(BF16)

        @pl.when((j == 1) & jnp.logical_not(last_pair))
        def _():
            pass_copy(own, 1).start()

        for q in range(PIECES):
            at = slice(q * part, (q + 1) * part)
            for d in (side(q), 1 - side(q)):
                arrive(rsb.at[j, d, 0, span(q)], rs_recv.at[j, d, 0, q])
                value = terms[d, at] + rsb[j, d, 0, at].astype(F32)
                if d == side(q):
                    arrive(rsf.at[j, span(q)], rs_recv.at[j, d, FAR, q])
                    value = value + rsf[j, at].astype(F32)
                rso[j, d, 1, at] = value.astype(BF16)
                rs_copy(j, d, 1, q).start()
        for d in range(2):
            terms[d] = term_at(d, 1)
        for q in range(PIECES):
            at = slice(q * part, (q + 1) * part)
            for d in range(2):
                arrive(rsb.at[j, d, 1, span(q)], rs_recv.at[j, d, 1, q])
                rso[j, d, 2, at] = (terms[d, at] + rsb[j, d, 1, at].astype(F32)).astype(BF16)
                prt_copy(j, d, q).start()
        return carry

    lax.fori_loop(0, 2, layer, 0)

    @pl.when(last_pair)
    def _():
        for q in range(PIECES):
            join(2, q)
        wide = hidden[3].astype(F32)
        folded = fold(wide * wide)
        row = jnp.sum(jnp.transpose(folded), axis=0, keepdims=True)
        ssb[0] = jnp.broadcast_to(row, (8, rows))
        for i in range(1, n_tp):
            ss_copy(i).start()
        for i in range(1, n_tp):
            ss_copy(i).wait_recv()
        row = jnp.sum(ssb[...], axis=0)[:1]
        column = jnp.transpose(jnp.broadcast_to(row, (rows, rows)))[:, :1]
        scale = lax.rsqrt(column * (1.0 / full_width) + 1e-5)
        n = lengths[e]
        position = c * rows + lax.broadcasted_iota(jnp.int32, (rows, 1), 0)
        scale = jnp.where(position < n, scale, 0.0)
        pooled = jnp.sum(hidden[3].astype(F32) * scale, axis=0, keepdims=True)
        ppb[0] = jnp.broadcast_to(pooled * closing[...] / n.astype(F32), (8, width))
        for i in range(1, n_ctx):
            pp_copy(i).start()
        for i in range(1, n_ctx):
            pp_copy(i).wait_recv()
        pooled = jnp.sum(ppb[...], axis=0)
        sqb[0] = jnp.broadcast_to(jnp.sum(pooled * pooled, axis=1, keepdims=True), (8, HEAD))
        for i in range(1, n_tp):
            sq_copy(i).start()
        for i in range(1, n_tp):
            sq_copy(i).wait_recv()
        norms = jnp.sum(sqb[...], axis=0)[:, :1]
        res[e] = pooled * lax.rsqrt(norms * (1.0 / full_width) + 1e-6)
        for i in range(1, sections):
            fin_copy(i).start()
        arrive(res.at[1 - e], fin_recv.at[1 - e])
        for i in range(1, n_ctx):
            pp_copy(i).wait_send()
        for i in range(1, n_tp):
            sq_copy(i).wait_send()
            ss_copy(i).wait_send()
        for i in range(1, sections):
            fin_copy(i).wait_send()

    @pl.when(jnp.logical_not(last_pair))
    def _():
        pass_copy(hidden, 0).wait_send()
        pass_copy(own, 1).wait_send()
        for i in range(micro):
            arrive(res.at[i], fin_recv.at[i])

    for i in range(micro):
        out[i:i + 1] = res[i, :1]

    for item in (WO, UP):
        weight_copy(item).wait_send()

    @pl.when(jnp.logical_not(helps))
    def _():
        for item in (WK, WV, WQ, GAIN, DOWN):
            weight_copy(item).wait_send()

    @pl.when(helps)
    def _():
        for i in range(4):
            acc_copy(i).wait_send()

    @pl.when(first_pair & (e == 1))
    def _():
        for slot in range(8):
            mir_copy(slot, agf.at[0]).wait_send()

    for j in range(2):
        for q in range(PIECES):
            for d in range(2):
                for r in range(3):
                    ag_copy(j, d, r, q, agb.at[j, d, r]).wait_send()
                for r in range(2):
                    rs_copy(j, d, r, q).wait_send()
                prt_copy(j, d, q).wait_send()
            ag_far(j, q).wait_send()
            rs_far(j, q).wait_send()
        for offset in NEAR + REST:
            kv_copy(j, offset).wait_send()


def build(mesh):
    sections, n_ctx, n_tp = (mesh.shape[a] for a in ("section", "ctx", "tp"))

    def shards(
        tokens, document_lengths, tenant_indices, attention_norm_gain, query_weight, key_weight,
        value_weight, output_weight, query_adapter_down, query_adapter_up, value_adapter_down,
        value_adapter_up, closing_norm_gain,
    ):
        micro, rows, width = tokens.shape
        query_width = query_weight.shape[2]
        tenant_count, rank = query_adapter_down.shape[1], query_adapter_down.shape[3]
        heads = query_width // HEAD

        freq = (500000.0 ** (-np.arange(HEAD // 2) / (HEAD // 2))).astype(np.float32)
        angle = np.arange(rows * n_ctx, dtype=np.float32)[:, None] * freq[None, :]
        cosine, sine = np.cos(angle.astype(np.float64)), np.sin(angle.astype(np.float64))
        tables = np.stack([np.concatenate([cosine, cosine], 1), np.concatenate([-sine, sine], 1)])
        tables = tables.reshape(2, n_ctx, rows, HEAD).transpose(1, 0, 2, 3).astype(np.float32)

        vmem = pl.BlockSpec(memory_space=pltpu.VMEM)
        hbm = pl.BlockSpec(memory_space=pl.ANY)
        smem = pl.BlockSpec(memory_space=pltpu.SMEM)
        dma = pltpu.SemaphoreType.DMA
        block = (rows, width)

        def body(*refs):
            kernel((sections, n_ctx, n_tp, micro, rows, width), *refs)

        return pl.pallas_call(
            body,
            out_shape=jax.ShapeDtypeStruct((micro, width), F32),
            in_specs=[smem, smem, hbm, hbm, vmem, hbm, hbm, hbm, hbm, hbm, hbm, hbm, vmem, vmem],
            out_specs=vmem,
            scratch_shapes=[
                pltpu.VMEM((2, n_tp, width, query_width), BF16),
                pltpu.VMEM((2, n_tp, width, 2 * HEAD), BF16),
                pltpu.VMEM((2, query_width, width * n_tp), BF16),
                pltpu.VMEM((2, 1, width * n_tp), F32),
                pltpu.VMEM((tenant_count, rank, width * n_tp), BF16),
                pltpu.VMEM((tenant_count, rank, width * n_tp), BF16),
                pltpu.VMEM((3, 2 * rank, width * n_tp), BF16),
                pltpu.VMEM((3, 2 * rank, query_width + HEAD), BF16),
                pltpu.VMEM((2, rows, HEAD), F32),
                pltpu.VMEM((4,) + block, BF16),
                pltpu.VMEM((3,) + block, BF16),
                pltpu.VMEM((2, 2, 3) + block, BF16),
                pltpu.VMEM((2,) + block, BF16),
                pltpu.VMEM((2, 2, 2) + block, BF16),
                pltpu.VMEM((2,) + block, BF16),
                pltpu.VMEM((2, 2, 3) + block, BF16),
                pltpu.VMEM((2,) + block, BF16),
                pltpu.VMEM((3, 2) + block, BF16),
                pltpu.VMEM((2, n_ctx, rows, 2 * HEAD), BF16),
                pltpu.VMEM((8,) + block, BF16),
                pltpu.VMEM((2, rows, query_width), F32),
                pltpu.VMEM((2, rows, 2 * HEAD), F32),
                pltpu.VMEM((2, rows, 2 * rank), F32),
                pltpu.VMEM((2, rows, HEAD), F32),
                pltpu.VMEM((heads, rows, HEAD), BF16),
                pltpu.VMEM((rows, query_width), BF16),
                pltpu.VMEM((2,) + block, F32),
                pltpu.VMEM((n_tp, 8, rows), F32),
                pltpu.VMEM((n_ctx, 8, width), F32),
                pltpu.VMEM((n_tp, 8, HEAD), F32),
                pltpu.VMEM((micro, 8, width), F32),
                dma((2, 7)),
                dma((7,)),
                dma((3,)),
                dma((1,)),
                dma((2, 2, 4, PIECES)),
                dma((2, 2, 4, PIECES)),
                dma((2, 2, 4, PIECES)),
                dma((2, 2, 4, PIECES)),
                dma((3, 2, PIECES)),
                dma((2, n_ctx)),
                dma((2, n_ctx)),
                dma((2,)),
                dma((2,)),
                dma((n_tp,)),
                dma((n_tp,)),
                dma((n_ctx,)),
                dma((n_ctx,)),
                dma((n_tp,)),
                dma((n_tp,)),
                dma((sections,)),
                dma((micro,)),
                dma((8,)),
                dma((8,)),
                dma((4,)),
                dma((4,)),
            ],
            compiler_params=pltpu.CompilerParams(
                collective_id=0, has_side_effects=True, vmem_limit_bytes=60 << 20),
            cost_estimate=pl.CostEstimate(
                flops=micro * 2 * rows * (n_tp * width * (query_width + 3 * HEAD) * 2),
                bytes_accessed=16 << 20, transcendentals=micro * heads * rows * rows * n_ctx),
        )(
            document_lengths, tenant_indices, tokens, attention_norm_gain,
            closing_norm_gain.reshape(1, width), jnp.asarray(tables),
            query_weight.reshape(n_tp, width, query_width),
            key_weight.reshape(n_tp, width, HEAD), value_weight.reshape(n_tp, width, HEAD),
            output_weight[0],
            jnp.swapaxes(query_adapter_down[0], 1, 2), jnp.swapaxes(value_adapter_down[0], 1, 2),
            query_adapter_up[0], value_adapter_up[0],
        )

    return shards


def solution(mesh):
    placed = (
        P(None, "ctx", "tp"),
        P(),
        P(),
        P("section", None),
        P("section", None, "tp"),
        P("section", None, "tp"),
        P("section", None, "tp"),
        P("section", "tp", None),
        P("section", None, None, None),
        P("section", None, None, "tp"),
        P("section", None, None, None),
        P("section", None, None, "tp"),
        P("tp"),
    )
    return jax.shard_map(
        build(mesh), mesh=mesh, in_specs=placed, out_specs=P(None, "tp"), check_vma=False
    )
```

```python
import math

import jax
import jax.numpy as jnp
import numpy as np
from jax import lax
from jax.experimental import pallas as pl
from jax.experimental.pallas import tpu as pltpu
from jax.sharding import PartitionSpec as P

HEAD = 128
F32 = jnp.float32
BF16 = jnp.bfloat16
MESH = pl.DeviceIdType.MESH

PIECES = 4
FAR = 3
WK, WV, WQ, GAIN, WO, DOWN, UP = range(7)
NEAR = ((1, 0), (0, 1), (0, 3))
REST = ((1, 1), (1, 3), (0, 2), (1, 2))


def fold(x):
    total = x[:, :HEAD]
    for i in range(1, x.shape[1] // HEAD):
        total = total + x[:, i * HEAD:(i + 1) * HEAD]
    return total


def kernel(
    sizes,
    lengths, tenants, tokens, gain_hbm, closing, tables, wq_hbm, wk_hbm, wv_hbm, wo_hbm,
    qd_hbm, vd_hbm, q_up, v_up,
    out,
    wq, wkv, wo, gains, qd, vd, down, up, trig,
    hidden, own, agb, agf, rsb, rsf, rso, rsfo, prt, kvbuf,
    acc_q, acc_kv, acc_l, squares, qbuf, att, terms,
    ssb, ppb, sqb, res,
    w_sem, w_send, small_sem, in_sem, ag_send, ag_recv, rs_send, rs_recv, prt_recv,
    kv_send, kv_recv, pass_send, pass_recv, ss_send, ss_recv, pp_send, pp_recv, sq_send, sq_recv,
    fin_send, fin_recv,
):
    sections, n_ctx, n_tp, micro, rows, width = sizes
    full_width = width * n_tp
    part = rows // PIECES
    heads = wq.shape[3] // HEAD
    rank = q_up.shape[1]
    s = lax.axis_index("section")
    c = lax.axis_index("ctx")
    z = lax.axis_index("tp")
    e = lax.rem(s, 2)
    first_pair = s < 2
    last_pair = s >= sections - 2
    partner = s + 1 - 2 * e

    def around(at, by, n):
        return lax.rem(at + (by + n), n)

    def remote(src, dst, send, recv, **to):
        return pltpu.make_async_remote_copy(
            src_ref=src, dst_ref=dst, send_sem=send, recv_sem=recv, device_id=to, device_id_type=MESH)

    def arrive(ref, sem):
        pltpu.make_async_copy(ref, ref, sem).wait()

    def span(q):
        return pl.ds(q * part, part)

    def side(q):
        return q * 2 // PIECES

    def token_copy():
        return pltpu.make_async_copy(tokens.at[e], hidden.at[1], in_sem.at[0])

    def weight(item, j):
        return {
            WK: lambda: wkv.at[j, :, :, pl.ds(0, HEAD)],
            WV: lambda: wkv.at[j, :, :, pl.ds(HEAD, HEAD)],
            WQ: lambda: wq.at[j],
            GAIN: lambda: gains.at[j],
            WO: lambda: wo.at[j],
            DOWN: lambda: down.at[j],
            UP: lambda: up.at[j],
        }[item]()

    sources = {WK: wk_hbm, WV: wv_hbm, WQ: wq_hbm, GAIN: gain_hbm, WO: wo_hbm}
    spare = {DOWN: down.at[2], UP: up.at[2]}

    def weight_copy(item):
        return remote({**sources, **spare}[item], weight(item, e), w_send.at[item], w_sem.at[e, item],
                      section=partner)

    small_copies = [
        pltpu.make_async_copy(qd_hbm, qd, small_sem.at[0]),
        pltpu.make_async_copy(vd_hbm, vd, small_sem.at[1]),
        pltpu.make_async_copy(tables.at[c], trig, small_sem.at[2]),
    ]

    @pl.when(first_pair)
    def _():
        token_copy().start()

    for copy in small_copies:
        copy.start()
    for item, source in sources.items():
        pltpu.make_async_copy(source, weight(item, e), w_sem.at[e, item]).start()

    barrier = pltpu.get_barrier_semaphore()
    neighbour = (around(z, 1, n_tp), around(z, -1, n_tp))
    peers = [{"tp": around(z, i, n_tp)} for i in range(1, n_tp)]
    peers += [{"ctx": around(c, i, n_ctx)} for i in range(1, n_ctx)]
    peers += [{"section": around(s, i, sections)} for i in range(1, sections)]
    peers += [{"section": around(s, 2, sections), "tp": neighbour[d]} for d in range(2)]
    for peer in peers:
        pl.semaphore_signal(barrier, 1, device_id=peer, device_id_type=MESH)

    for copy in small_copies:
        copy.wait()
    for slot, document in ((e, e), (2, 1 - e)):
        t = tenants[document]
        up[slot] = jnp.zeros(up.shape[1:], BF16)
        down[slot, :rank] = qd[t]
        down[slot, rank:] = vd[t]
        up[slot, :rank, :heads * HEAD] = q_up[t]
        up[slot, rank:, heads * HEAD:] = v_up[t]

    pl.semaphore_wait(barrier, len(peers))

    two_on = (around(z, 2, n_tp), around(z, -2, n_tp))

    def ag_copy(j, d, r, q, src):
        return remote(src.at[span(q)], agb.at[j, d, r, span(q)], ag_send.at[j, d, r, q],
                      ag_recv.at[j, d, r, q], tp=neighbour[d])

    def ag_far(j, q):
        d = side(q)
        return remote(agb.at[j, d, 1, span(q)], agf.at[j, span(q)], ag_send.at[j, d, FAR, q],
                      ag_recv.at[j, d, FAR, q], tp=two_on[d])

    def rs_copy(j, d, r, q):
        return remote(rso.at[j, d, r, span(q)], rsb.at[j, d, r, span(q)], rs_send.at[j, d, r, q],
                      rs_recv.at[j, d, r, q], tp=neighbour[d])

    def rs_far(j, q):
        d = side(q)
        return remote(rsfo.at[j, span(q)], rsf.at[j, span(q)], rs_send.at[j, d, FAR, q],
                      rs_recv.at[j, d, FAR, q], tp=two_on[d])

    def prt_copy(j, d, q):
        slot = jnp.where(j == 0, 1, jnp.where(last_pair, 2, 0))
        where = jnp.where((j == 1) & jnp.logical_not(last_pair), around(s, 2, sections), s)
        return remote(rso.at[j, d, 2, span(q)], prt.at[slot, d, span(q)], rs_send.at[j, d, 2, q],
                      prt_recv.at[slot, d, q], tp=neighbour[d], section=where)

    def pass_copy(buf, i):
        return remote(buf.at[2], buf.at[0], pass_send.at[i], pass_recv.at[i], section=around(s, 2, sections))

    def ctx_peer(dy, dx):
        across = n_ctx // 2
        return around(c // across, dy, 2) * across + around(lax.rem(c, across), dx, across)

    def kv_copy(j, offset):
        dy, dx = offset
        i = dy * (n_ctx // 2) + dx
        return remote(kvbuf.at[j, c], kvbuf.at[j, c], kv_send.at[j, i], kv_recv.at[j, i],
                      ctx=ctx_peer(dy, dx))

    def ss_copy(i):
        return remote(ssb.at[0], ssb.at[i], ss_send.at[i], ss_recv.at[i], tp=around(z, i, n_tp))

    def pp_copy(i):
        return remote(ppb.at[0], ppb.at[i], pp_send.at[i], pp_recv.at[i], ctx=around(c, i, n_ctx))

    def sq_copy(i):
        return remote(sqb.at[0], sqb.at[i], sq_send.at[i], sq_recv.at[i], tp=around(z, i, n_tp))

    def fin_copy(i):
        return remote(res.at[e], res.at[e], fin_send.at[i], fin_recv.at[e], section=around(s, i, sections))

    def rotate(x):
        return x * trig[0] + pltpu.roll(x, HEAD // 2, axis=1) * trig[1]

    def take(j, blocks, first=False):
        values = None
        for block, g in blocks:
            h = block.astype(F32)
            columns = pl.ds(pl.multiple_of(g * width, width), width)
            x = (h * gains[j, :, columns]).astype(BF16)
            new = (
                fold(h * h),
                jnp.dot(x, wkv[j, g], preferred_element_type=F32),
                lax.dot_general(x, down[j, :, columns], (((1,), (1,)), ((), ())), preferred_element_type=F32),
                jnp.dot(x, wq[j, g], preferred_element_type=F32),
            )
            values = new if values is None else [a + b for a, b in zip(values, new)]
        for ref, value in zip((squares, acc_kv, acc_l, acc_q), values):
            ref[...] = value if first else ref[...] + value

    def join(i, q):
        for d in range(2):
            arrive(prt.at[i, d, span(q)], prt_recv.at[i, d, q])
        at = slice(q * part, (q + 1) * part)
        sums = prt[i, 0, at].astype(F32) + prt[i, 1, at].astype(F32)
        hidden[i + 1, at] = (hidden[i, at].astype(F32) + own[i, at].astype(F32) + sums).astype(BF16)

    def layer(j, carry):
        @pl.when(first_pair & (j == 0))
        def _():
            token_copy().wait()

        @pl.when(jnp.logical_not(first_pair) & (j == 0))
        def _():
            arrive(hidden.at[0], pass_recv.at[0])
            arrive(own.at[0], pass_recv.at[1])

        for q in range(PIECES):
            @pl.when(jnp.logical_not(first_pair) | (j == 1))
            def _():
                join(j, q)

            for d in range(2):
                ag_copy(j, d, 0, q, hidden.at[j + 1]).start()

        @pl.when(first_pair & (j == 0))
        def _():
            for item in (GAIN, DOWN, UP, WK, WV, WQ):
                weight_copy(item).start()

        @pl.when((j == 1) & jnp.logical_not(last_pair))
        def _():
            pass_copy(hidden, 0).start()

        def own_take():
            for item in (GAIN, WK, WV, WQ):
                arrive(weight(item, j), w_sem.at[j, item])

            @pl.when(j != e)
            def _():
                for item in (DOWN, UP):
                    arrive(weight(item, j), w_sem.at[j, item])

            take(j, [(hidden[j + 1], z)], first=True)

        def pair_take(r):
            take(j, [(agb[j, d, r], around(z, -1 - r if d == 0 else 1 + r, n_tp)) for d in range(2)])

        late = first_pair & (e == 1) & (j == 0)
        prompt = jnp.logical_not(late)

        @pl.when(prompt)
        def _():
            own_take()

        for r in range(3):
            for q in range(PIECES):
                for d in range(2):
                    arrive(agb.at[j, d, r, span(q)], ag_recv.at[j, d, r, q])
                    if r < 2:
                        ag_copy(j, d, r + 1, q, agb.at[j, d, r]).start()
                    if r == 1 and d == side(q):
                        ag_far(j, q).start()

            @pl.when(prompt)
            def _():
                pair_take(r)

        @pl.when(first_pair & (j == 0))
        def _():
            weight_copy(WO).start()

        @pl.when(late)
        def _():
            own_take()

            def after(r, carry):
                pair_take(r)
                return carry

            lax.fori_loop(0, 3, after, 0)

        for q in range(PIECES):
            arrive(agf.at[j, span(q)], ag_recv.at[j, side(q), FAR, q])
        take(j, [(agf[j], around(z, 4, n_tp))])

        mean = jnp.sum(squares[...], axis=1, keepdims=True) * (1.0 / full_width)
        scale = lax.rsqrt(mean + 1e-5)
        low = (acc_l[...] * scale).astype(BF16)
        kv = acc_kv[...] * scale
        kvbuf[j, c, :, :HEAD] = rotate(kv[:, :HEAD]).astype(BF16)
        added = jnp.dot(low, up[j, :, heads * HEAD:], preferred_element_type=F32)
        kvbuf[j, c, :, HEAD:] = (kv[:, HEAD:] + added).astype(BF16)
        for offset in NEAR + REST:
            kv_copy(j, offset).start()
        factor = HEAD ** -0.5 * math.log2(math.e)
        for g in range(heads):
            cols = slice(g * HEAD, (g + 1) * HEAD)
            q = acc_q[:, cols] * scale + jnp.dot(low, up[j, :, cols], preferred_element_type=F32)
            qbuf[g] = (rotate(q) * factor).astype(BF16)

        n = lengths[e]
        lane = lax.broadcasted_iota(jnp.int32, (1, rows), 1)

        def keys_of(offsets):
            sources = [ctx_peer(-dy, -dx) for dy, dx in offsets]
            blocks = [kvbuf[j, source] for source in sources]
            valid = jnp.concatenate([lane + source * rows < n for source in sources], axis=1)
            return (jnp.concatenate([block[:, :HEAD] for block in blocks], axis=0),
                    jnp.concatenate([block[:, HEAD:] for block in blocks], axis=0), valid)

        def scored(g, keys, valid):
            scores = lax.dot_general(
                qbuf[g], keys, (((1,), (1,)), ((), ())), preferred_element_type=F32)
            return jnp.where(valid, scores, -1e30)

        for offset in NEAR:
            kv_copy(j, offset).wait_recv()
        keys, values, valid = keys_of(((0, 0),) + NEAR)
        near = []
        for g in range(heads):
            scores = scored(g, keys, valid)
            top = jnp.max(scores, axis=1, keepdims=True)
            weights = jnp.exp2(scores - top)
            total = jnp.sum(weights, axis=1, keepdims=True)
            near.append((top, total, jnp.dot(weights.astype(BF16), values, preferred_element_type=F32)))
        for offset in REST:
            kv_copy(j, offset).wait_recv()
        keys, values, valid = keys_of(REST)
        for g in range(heads):
            top_near, total_near, mixed_near = near[g]
            scores = scored(g, keys, valid)
            top = jnp.maximum(jnp.max(scores, axis=1, keepdims=True), top_near)
            weights = jnp.exp2(scores - top)
            fade = jnp.exp2(top_near - top)
            total = jnp.sum(weights, axis=1, keepdims=True) + total_near * fade
            mixed = jnp.dot(weights.astype(BF16), values, preferred_element_type=F32) + mixed_near * fade
            att[:, g * HEAD:(g + 1) * HEAD] = (mixed * (1.0 / total)).astype(BF16)

        arrive(weight(WO, j), w_sem.at[j, WO])

        def term(index):
            columns = pl.ds(pl.multiple_of(index * width, width), width)
            return jnp.dot(att[...], wo[j, :, columns], preferred_element_type=F32)

        def term_at(d, distance):
            return term(around(z, distance if d == 0 else -distance, n_tp))

        rsfo[j] = term_at(0, 4).astype(BF16)
        for q in range(PIECES):
            rs_far(j, q).start()
        for d in range(2):
            rso[j, d, 0] = term_at(d, 3).astype(BF16)
            for q in range(PIECES):
                rs_copy(j, d, 0, q).start()
        for d in range(2):
            terms[d] = term_at(d, 2)
        own[j + 1] = term(z).astype(BF16)

        @pl.when((j == 1) & jnp.logical_not(last_pair))
        def _():
            pass_copy(own, 1).start()

        for q in range(PIECES):
            at = slice(q * part, (q + 1) * part)
            for d in (side(q), 1 - side(q)):
                arrive(rsb.at[j, d, 0, span(q)], rs_recv.at[j, d, 0, q])
                value = terms[d, at] + rsb[j, d, 0, at].astype(F32)
                if d == side(q):
                    arrive(rsf.at[j, span(q)], rs_recv.at[j, d, FAR, q])
                    value = value + rsf[j, at].astype(F32)
                rso[j, d, 1, at] = value.astype(BF16)
                rs_copy(j, d, 1, q).start()
        for d in range(2):
            terms[d] = term_at(d, 1)
        for q in range(PIECES):
            at = slice(q * part, (q + 1) * part)
            for d in range(2):
                arrive(rsb.at[j, d, 1, span(q)], rs_recv.at[j, d, 1, q])
                rso[j, d, 2, at] = (terms[d, at] + rsb[j, d, 1, at].astype(F32)).astype(BF16)
                prt_copy(j, d, q).start()
        return carry

    @pl.when(jnp.logical_not(first_pair))
    def _():
        for item in (GAIN, DOWN, UP, WK, WV, WQ, WO):
            weight_copy(item).start()

    lax.fori_loop(0, 2, layer, 0)

    @pl.when(last_pair)
    def _():
        for q in range(PIECES):
            join(2, q)
        wide = hidden[3].astype(F32)
        folded = fold(wide * wide)
        row = jnp.sum(jnp.transpose(folded), axis=0, keepdims=True)
        ssb[0] = jnp.broadcast_to(row, (8, rows))
        for i in range(1, n_tp):
            ss_copy(i).start()
        for i in range(1, n_tp):
            ss_copy(i).wait_recv()
        row = jnp.sum(ssb[...], axis=0)[:1]
        column = jnp.transpose(jnp.broadcast_to(row, (rows, rows)))[:, :1]
        scale = lax.rsqrt(column * (1.0 / full_width) + 1e-5)
        n = lengths[e]
        position = c * rows + lax.broadcasted_iota(jnp.int32, (rows, 1), 0)
        scale = jnp.where(position < n, scale, 0.0)
        pooled = jnp.sum(hidden[3].astype(F32) * scale, axis=0, keepdims=True)
        ppb[0] = jnp.broadcast_to(pooled * closing[...] / n.astype(F32), (8, width))
        for i in range(1, n_ctx):
            pp_copy(i).start()
        for i in range(1, n_ctx):
            pp_copy(i).wait_recv()
        pooled = jnp.sum(ppb[...], axis=0)
        sqb[0] = jnp.broadcast_to(jnp.sum(pooled * pooled, axis=1, keepdims=True), (8, HEAD))
        for i in range(1, n_tp):
            sq_copy(i).start()
        for i in range(1, n_tp):
            sq_copy(i).wait_recv()
        norms = jnp.sum(sqb[...], axis=0)[:, :1]
        res[e] = pooled * lax.rsqrt(norms * (1.0 / full_width) + 1e-6)
        for i in range(1, sections):
            fin_copy(i).start()
        arrive(res.at[1 - e], fin_recv.at[1 - e])
        for i in range(1, n_ctx):
            pp_copy(i).wait_send()
        for i in range(1, n_tp):
            sq_copy(i).wait_send()
            ss_copy(i).wait_send()
        for i in range(1, sections):
            fin_copy(i).wait_send()

    @pl.when(jnp.logical_not(last_pair))
    def _():
        pass_copy(hidden, 0).wait_send()
        pass_copy(own, 1).wait_send()
        for i in range(micro):
            arrive(res.at[i], fin_recv.at[i])

    for i in range(micro):
        out[i:i + 1] = res[i, :1]

    for item in range(7):
        weight_copy(item).wait_send()
    for j in range(2):
        for q in range(PIECES):
            for d in range(2):
                for r in range(3):
                    ag_copy(j, d, r, q, agb.at[j, d, r]).wait_send()
                for r in range(2):
                    rs_copy(j, d, r, q).wait_send()
                prt_copy(j, d, q).wait_send()
            ag_far(j, q).wait_send()
            rs_far(j, q).wait_send()
        for offset in NEAR + REST:
            kv_copy(j, offset).wait_send()


def build(mesh):
    sections, n_ctx, n_tp = (mesh.shape[a] for a in ("section", "ctx", "tp"))

    def shards(
        tokens, document_lengths, tenant_indices, attention_norm_gain, query_weight, key_weight,
        value_weight, output_weight, query_adapter_down, query_adapter_up, value_adapter_down,
        value_adapter_up, closing_norm_gain,
    ):
        micro, rows, width = tokens.shape
        query_width = query_weight.shape[2]
        tenant_count, rank = query_adapter_down.shape[1], query_adapter_down.shape[3]
        heads = query_width // HEAD

        freq = (500000.0 ** (-np.arange(HEAD // 2) / (HEAD // 2))).astype(np.float32)
        angle = np.arange(rows * n_ctx, dtype=np.float32)[:, None] * freq[None, :]
        cosine, sine = np.cos(angle.astype(np.float64)), np.sin(angle.astype(np.float64))
        tables = np.stack([np.concatenate([cosine, cosine], 1), np.concatenate([-sine, sine], 1)])
        tables = tables.reshape(2, n_ctx, rows, HEAD).transpose(1, 0, 2, 3).astype(np.float32)

        vmem = pl.BlockSpec(memory_space=pltpu.VMEM)
        hbm = pl.BlockSpec(memory_space=pl.ANY)
        smem = pl.BlockSpec(memory_space=pltpu.SMEM)
        dma = pltpu.SemaphoreType.DMA
        block = (rows, width)

        def body(*refs):
            kernel((sections, n_ctx, n_tp, micro, rows, width), *refs)

        return pl.pallas_call(
            body,
            out_shape=jax.ShapeDtypeStruct((micro, width), F32),
            in_specs=[smem, smem, hbm, hbm, vmem, hbm, hbm, hbm, hbm, hbm, hbm, hbm, vmem, vmem],
            out_specs=vmem,
            scratch_shapes=[
                pltpu.VMEM((2, n_tp, width, query_width), BF16),
                pltpu.VMEM((2, n_tp, width, 2 * HEAD), BF16),
                pltpu.VMEM((2, query_width, width * n_tp), BF16),
                pltpu.VMEM((2, 1, width * n_tp), F32),
                pltpu.VMEM((tenant_count, rank, width * n_tp), BF16),
                pltpu.VMEM((tenant_count, rank, width * n_tp), BF16),
                pltpu.VMEM((3, 2 * rank, width * n_tp), BF16),
                pltpu.VMEM((3, 2 * rank, query_width + HEAD), BF16),
                pltpu.VMEM((2, rows, HEAD), F32),
                pltpu.VMEM((4,) + block, BF16),
                pltpu.VMEM((3,) + block, BF16),
                pltpu.VMEM((2, 2, 3) + block, BF16),
                pltpu.VMEM((2,) + block, BF16),
                pltpu.VMEM((2, 2, 2) + block, BF16),
                pltpu.VMEM((2,) + block, BF16),
                pltpu.VMEM((2, 2, 3) + block, BF16),
                pltpu.VMEM((2,) + block, BF16),
                pltpu.VMEM((3, 2) + block, BF16),
                pltpu.VMEM((2, n_ctx, rows, 2 * HEAD), BF16),
                pltpu.VMEM((rows, query_width), F32),
                pltpu.VMEM((rows, 2 * HEAD), F32),
                pltpu.VMEM((rows, 2 * rank), F32),
                pltpu.VMEM((rows, HEAD), F32),
                pltpu.VMEM((heads, rows, HEAD), BF16),
                pltpu.VMEM((rows, query_width), BF16),
                pltpu.VMEM((2,) + block, F32),
                pltpu.VMEM((n_tp, 8, rows), F32),
                pltpu.VMEM((n_ctx, 8, width), F32),
                pltpu.VMEM((n_tp, 8, HEAD), F32),
                pltpu.VMEM((micro, 8, width), F32),
                dma((2, 7)),
                dma((7,)),
                dma((3,)),
                dma((1,)),
                dma((2, 2, 4, PIECES)),
                dma((2, 2, 4, PIECES)),
                dma((2, 2, 4, PIECES)),
                dma((2, 2, 4, PIECES)),
                dma((3, 2, PIECES)),
                dma((2, n_ctx)),
                dma((2, n_ctx)),
                dma((2,)),
                dma((2,)),
                dma((n_tp,)),
                dma((n_tp,)),
                dma((n_ctx,)),
                dma((n_ctx,)),
                dma((n_tp,)),
                dma((n_tp,)),
                dma((sections,)),
                dma((micro,)),
            ],
            compiler_params=pltpu.CompilerParams(
                collective_id=0, has_side_effects=True, vmem_limit_bytes=60 << 20),
            cost_estimate=pl.CostEstimate(
                flops=micro * 2 * rows * (n_tp * width * (query_width + 3 * HEAD) * 2),
                bytes_accessed=16 << 20, transcendentals=micro * heads * rows * rows * n_ctx),
        )(
            document_lengths, tenant_indices, tokens, attention_norm_gain,
            closing_norm_gain.reshape(1, width), jnp.asarray(tables),
            query_weight.reshape(n_tp, width, query_width),
            key_weight.reshape(n_tp, width, HEAD), value_weight.reshape(n_tp, width, HEAD),
            output_weight[0],
            jnp.swapaxes(query_adapter_down[0], 1, 2), jnp.swapaxes(value_adapter_down[0], 1, 2),
            query_adapter_up[0], value_adapter_up[0],
        )

    return shards


def solution(mesh):
    placed = (
        P(None, "ctx", "tp"),
        P(),
        P(),
        P("section", None),
        P("section", None, "tp"),
        P("section", None, "tp"),
        P("section", None, "tp"),
        P("section", "tp", None),
        P("section", None, None, None),
        P("section", None, None, "tp"),
        P("section", None, None, None),
        P("section", None, None, "tp"),
        P("tp"),
    )
    return jax.shard_map(
        build(mesh), mesh=mesh, in_specs=placed, out_specs=P(None, "tp"), check_vma=False
    )
```

```python
import math

import jax
import jax.numpy as jnp
import numpy as np
from jax import lax
from jax.experimental import pallas as pl
from jax.experimental.pallas import tpu as pltpu
from jax.sharding import PartitionSpec as P

HEAD = 128
F32 = jnp.float32
BF16 = jnp.bfloat16
MESH = pl.DeviceIdType.MESH

PIECES = 4
FAR = 3
WK, WV, WQ, GAIN, WO, DOWN, UP = range(7)
NEAR = ((1, 0), (0, 1), (0, 3))
REST = ((1, 1), (1, 3), (0, 2), (1, 2))


def fold(x):
    total = x[:, :HEAD]
    for i in range(1, x.shape[1] // HEAD):
        total = total + x[:, i * HEAD:(i + 1) * HEAD]
    return total


def kernel(
    sizes,
    lengths, tenants, tokens, gain_hbm, closing, tables, wq_hbm, wk_hbm, wv_hbm, wo_hbm,
    qd_hbm, vd_hbm, q_up, v_up,
    out,
    wq, wkv, wo, gains, qd, vd, down, up, trig,
    hidden, own, agb, agf, rsb, rsf, rso, rsfo, prt, kvbuf,
    acc_q, acc_kv, acc_l, squares, qbuf, att, terms,
    ssb, ppb, sqb, res,
    w_sem, w_send, small_sem, in_sem, ag_send, ag_recv, rs_send, rs_recv, prt_recv,
    kv_send, kv_recv, pass_send, pass_recv, few_send, few_recv,
    fin_send, fin_recv,
):
    sections, n_ctx, n_tp, micro, rows, width = sizes
    full_width = width * n_tp
    part = rows // PIECES
    heads = wq.shape[3] // HEAD
    rank = q_up.shape[1]
    s = lax.axis_index("section")
    c = lax.axis_index("ctx")
    z = lax.axis_index("tp")
    e = lax.rem(s, 2)
    first_pair = s < 2
    last_pair = s >= sections - 2
    partner = s + 1 - 2 * e

    def around(at, by, n):
        return lax.rem(at + (by + n), n)

    def remote(src, dst, send, recv, section=s, ctx=c, tp=z):
        return pltpu.make_async_remote_copy(
            src_ref=src, dst_ref=dst, send_sem=send, recv_sem=recv, device_id=(section, ctx, tp),
            device_id_type=MESH)

    def arrive(ref, sem):
        pltpu.make_async_copy(ref, ref, sem).wait()

    def span(q):
        return pl.ds(q * part, part)

    def side(q):
        return q * 2 // PIECES

    def token_copy():
        return pltpu.make_async_copy(tokens.at[e], hidden.at[1], in_sem.at[0])

    def weight(item, j):
        return {
            WK: lambda: wkv.at[j, :, :, pl.ds(0, HEAD)],
            WV: lambda: wkv.at[j, :, :, pl.ds(HEAD, HEAD)],
            WQ: lambda: wq.at[j],
            GAIN: lambda: gains.at[j],
            WO: lambda: wo.at[j],
            DOWN: lambda: down.at[j],
            UP: lambda: up.at[j],
        }[item]()

    sources = {WK: wk_hbm, WV: wv_hbm, WQ: wq_hbm, GAIN: gain_hbm, WO: wo_hbm}
    spare = {DOWN: down.at[2], UP: up.at[2]}

    def weight_copy(item):
        return remote({**sources, **spare}[item], weight(item, e), w_send.at[item], w_sem.at[e, item],
                      section=partner)

    small_copies = [
        pltpu.make_async_copy(qd_hbm, qd, small_sem.at[0]),
        pltpu.make_async_copy(vd_hbm, vd, small_sem.at[1]),
        pltpu.make_async_copy(tables.at[c], trig, small_sem.at[2]),
    ]

    @pl.when(first_pair)
    def _():
        token_copy().start()

    for copy in small_copies:
        copy.start()
    for item, source in sources.items():
        pltpu.make_async_copy(source, weight(item, e), w_sem.at[e, item]).start()

    barrier = pltpu.get_barrier_semaphore()
    neighbour = (around(z, 1, n_tp), around(z, -1, n_tp))
    peers = [(s, c, around(z, i, n_tp)) for i in range(1, n_tp)]
    peers += [(s, around(c, i, n_ctx), z) for i in range(1, n_ctx)]
    peers += [(around(s, i, sections), c, z) for i in range(1, sections)]
    peers += [(around(s, 2, sections), c, neighbour[d]) for d in range(2)]
    for peer in peers:
        pl.semaphore_signal(barrier, 1, device_id=peer, device_id_type=MESH)

    for copy in small_copies:
        copy.wait()
    for slot, document in ((e, e), (2, 1 - e)):
        t = tenants[document]
        up[slot] = jnp.zeros(up.shape[1:], BF16)
        down[slot, :rank] = qd[t]
        down[slot, rank:] = vd[t]
        up[slot, :rank, :heads * HEAD] = q_up[t]
        up[slot, rank:, heads * HEAD:] = v_up[t]

    pl.semaphore_wait(barrier, len(peers))

    two_on = (around(z, 2, n_tp), around(z, -2, n_tp))

    def ag_copy(j, d, r, q, src):
        return remote(src.at[span(q)], agb.at[j, d, r, span(q)], ag_send.at[j, 0],
                      ag_recv.at[j, d, r, q if r < 2 else 0], tp=neighbour[d])

    def ag_far(j, q):
        d = side(q)
        return remote(agb.at[j, d, 1, span(q)], agf.at[j, span(q)], ag_send.at[j, 1],
                      ag_recv.at[j, 0, FAR, 0], tp=two_on[d])

    def rs_copy(j, d, r, q):
        return remote(rso.at[j, d, r, span(q)], rsb.at[j, d, r, span(q)], rs_send.at[j, 0],
                      rs_recv.at[j, d, r, q], tp=neighbour[d])

    def rs_far(j, q):
        d = side(q)
        return remote(rsfo.at[j, span(q)], rsf.at[j, span(q)], rs_send.at[j, 1],
                      rs_recv.at[j, d, FAR, q], tp=two_on[d])

    def prt_copy(j, d, q):
        slot = jnp.where(j == 0, 1, jnp.where(last_pair, 2, 0))
        where = jnp.where((j == 1) & jnp.logical_not(last_pair), around(s, 2, sections), s)
        return remote(rso.at[j, d, 2, span(q)], prt.at[slot, d, span(q)], rs_send.at[j, 0],
                      prt_recv.at[slot, d, q], tp=neighbour[d], section=where)

    def pass_copy(buf, i):
        return remote(buf.at[2], buf.at[0], pass_send.at[i], pass_recv.at[i], section=around(s, 2, sections))

    def ctx_peer(dy, dx):
        across = n_ctx // 2
        return around(c // across, dy, 2) * across + around(lax.rem(c, across), dx, across)

    ctx_ids = {offset: ctx_peer(*offset) for offset in NEAR + REST}

    def kv_copy(j, offset):
        return remote(kvbuf.at[j, c], kvbuf.at[j, c], kv_send.at[j],
                      kv_recv.at[j, 0 if offset in NEAR else 1], ctx=ctx_ids[offset])

    def ss_copy(i):
        return remote(ssb.at[0], ssb.at[i], few_send.at[0], few_recv.at[0], tp=around(z, i, n_tp))

    def pp_copy(i):
        return remote(ppb.at[0], ppb.at[i], few_send.at[1], few_recv.at[1], ctx=around(c, i, n_ctx))

    def sq_copy(i):
        return remote(sqb.at[0], sqb.at[i], few_send.at[2], few_recv.at[2], tp=around(z, i, n_tp))

    def fin_copy(i):
        return remote(res.at[e], res.at[e], fin_send.at[i], fin_recv.at[e], section=around(s, i, sections))

    def rotate(x):
        return x * trig[0] + pltpu.roll(x, HEAD // 2, axis=1) * trig[1]

    def take(j, blocks, first=False, queries=True, others=True):
        values = None
        for block, g in blocks:
            h = block.astype(F32)
            columns = pl.ds(pl.multiple_of(g * width, width), width)
            x = (h * gains[j, :, columns]).astype(BF16)
            new = []
            if others:
                new += [
                    fold(h * h),
                    jnp.dot(x, wkv[j, g], preferred_element_type=F32),
                    lax.dot_general(
                        x, down[j, :, columns], (((1,), (1,)), ((), ())), preferred_element_type=F32),
                ]
            if queries:
                new.append(jnp.dot(x, wq[j, g], preferred_element_type=F32))
            values = new if values is None else [a + b for a, b in zip(values, new)]
        refs = ((squares, acc_kv, acc_l) if others else ()) + ((acc_q,) if queries else ())
        for ref, value in zip(refs, values):
            ref[...] = value if first else ref[...] + value

    def join(i, q):
        for d in range(2):
            arrive(prt.at[i, d, span(q)], prt_recv.at[i, d, q])
        at = slice(q * part, (q + 1) * part)
        sums = prt[i, 0, at].astype(F32) + prt[i, 1, at].astype(F32)
        hidden[i + 1, at] = (hidden[i, at].astype(F32) + own[i, at].astype(F32) + sums).astype(BF16)

    def layer(j, carry):
        @pl.when(first_pair & (j == 0))
        def _():
            token_copy().wait()

        @pl.when(jnp.logical_not(first_pair) & (j == 0))
        def _():
            arrive(hidden.at[0], pass_recv.at[0])
            arrive(own.at[0], pass_recv.at[1])

        for q in range(PIECES):
            @pl.when(jnp.logical_not(first_pair) | (j == 1))
            def _():
                join(j, q)

            for d in range(2):
                ag_copy(j, d, 0, q, hidden.at[j + 1]).start()

        @pl.when(first_pair & (j == 0))
        def _():
            for item in (GAIN, DOWN, UP, WK, WV, WQ):
                weight_copy(item).start()

        @pl.when((j == 1) & jnp.logical_not(last_pair))
        def _():
            pass_copy(hidden, 0).start()

        def own_take():
            for item in (GAIN, WK, WV, WQ):
                arrive(weight(item, j), w_sem.at[j, item])

            @pl.when(j != e)
            def _():
                for item in (DOWN, UP):
                    arrive(weight(item, j), w_sem.at[j, item])

            take(j, [(hidden[j + 1], z)], first=True)

        def pair(r):
            return [(agb[j, d, r], around(z, -1 - r if d == 0 else 1 + r, n_tp)) for d in range(2)]

        late = first_pair & (e == 1) & (j == 0)
        prompt = jnp.logical_not(late)

        @pl.when(prompt)
        def _():
            own_take()

        for r in range(2):
            for q in range(PIECES):
                for d in range(2):
                    arrive(agb.at[j, d, r, span(q)], ag_recv.at[j, d, r, q])
                    ag_copy(j, d, r + 1, q, agb.at[j, d, r]).start()
                    if r == 1 and d == side(q):
                        ag_far(j, q).start()

            @pl.when(prompt)
            def _():
                take(j, pair(r))

        @pl.when(first_pair & (j == 0))
        def _():
            weight_copy(WO).start()

        @pl.when(late)
        def _():
            own_take()
            for r in range(2):
                take(j, pair(r))

        for d in range(2):
            arrive(agb.at[j, d, 2], ag_recv.at[j, d, 2, 0])
        take(j, pair(2), queries=False)
        arrive(agf.at[j], ag_recv.at[j, 0, FAR, 0])
        far = [(agf[j], around(z, 4, n_tp))]
        take(j, far, queries=False)

        mean = jnp.sum(squares[...], axis=1, keepdims=True) * (1.0 / full_width)
        scale = lax.rsqrt(mean + 1e-5)
        low = (acc_l[...] * scale).astype(BF16)
        kv = acc_kv[...] * scale
        kvbuf[j, c, :, :HEAD] = rotate(kv[:, :HEAD]).astype(BF16)
        added = jnp.dot(low, up[j, :, heads * HEAD:], preferred_element_type=F32)
        kvbuf[j, c, :, HEAD:] = (kv[:, HEAD:] + added).astype(BF16)
        for offset in NEAR + REST:
            kv_copy(j, offset).start()
        take(j, pair(2) + far, others=False)
        factor = HEAD ** -0.5 * math.log2(math.e)
        for g in range(heads):
            cols = slice(g * HEAD, (g + 1) * HEAD)
            q = acc_q[:, cols] * scale + jnp.dot(low, up[j, :, cols], preferred_element_type=F32)
            qbuf[g] = (rotate(q) * factor).astype(BF16)

        n = lengths[e]
        lane = lax.broadcasted_iota(jnp.int32, (1, rows), 1)

        def keys_of(offsets):
            sources = [ctx_peer(-dy, -dx) for dy, dx in offsets]
            blocks = [kvbuf[j, source] for source in sources]
            valid = jnp.concatenate([lane + source * rows < n for source in sources], axis=1)
            return (jnp.concatenate([block[:, :HEAD] for block in blocks], axis=0),
                    jnp.concatenate([block[:, HEAD:] for block in blocks], axis=0), valid)

        def scored(g, keys, valid):
            scores = lax.dot_general(
                qbuf[g], keys, (((1,), (1,)), ((), ())), preferred_element_type=F32)
            return jnp.where(valid, scores, -1e30)

        arrive(kvbuf.at[j, pl.ds(0, len(NEAR))], kv_recv.at[j, 0])
        keys, values, valid = keys_of(((0, 0),) + NEAR)
        near = []
        for g in range(heads):
            scores = scored(g, keys, valid)
            top = jnp.max(scores, axis=1, keepdims=True)
            weights = jnp.exp2(scores - top)
            total = jnp.sum(weights, axis=1, keepdims=True)
            near.append((top, total, jnp.dot(weights.astype(BF16), values, preferred_element_type=F32)))
        arrive(kvbuf.at[j, pl.ds(0, len(REST))], kv_recv.at[j, 1])
        keys, values, valid = keys_of(REST)
        for g in range(heads):
            top_near, total_near, mixed_near = near[g]
            scores = scored(g, keys, valid)
            top = jnp.maximum(jnp.max(scores, axis=1, keepdims=True), top_near)
            weights = jnp.exp2(scores - top)
            fade = jnp.exp2(top_near - top)
            total = jnp.sum(weights, axis=1, keepdims=True) + total_near * fade
            mixed = jnp.dot(weights.astype(BF16), values, preferred_element_type=F32) + mixed_near * fade
            att[:, g * HEAD:(g + 1) * HEAD] = (mixed * (1.0 / total)).astype(BF16)

        arrive(weight(WO, j), w_sem.at[j, WO])

        def term(index):
            columns = pl.ds(pl.multiple_of(index * width, width), width)
            return jnp.dot(att[...], wo[j, :, columns], preferred_element_type=F32)

        def term_at(d, distance):
            return term(around(z, distance if d == 0 else -distance, n_tp))

        rsfo[j] = term_at(0, 4).astype(BF16)
        for q in range(PIECES):
            rs_far(j, q).start()
        for d in range(2):
            rso[j, d, 0] = term_at(d, 3).astype(BF16)
            for q in range(PIECES):
                rs_copy(j, d, 0, q).start()
        for d in range(2):
            terms[d] = term_at(d, 2)
        own[j + 1] = term(z).astype(BF16)

        @pl.when((j == 1) & jnp.logical_not(last_pair))
        def _():
            pass_copy(own, 1).start()

        for q in range(PIECES):
            at = slice(q * part, (q + 1) * part)
            for d in (side(q), 1 - side(q)):
                arrive(rsb.at[j, d, 0, span(q)], rs_recv.at[j, d, 0, q])
                value = terms[d, at] + rsb[j, d, 0, at].astype(F32)
                if d == side(q):
                    arrive(rsf.at[j, span(q)], rs_recv.at[j, d, FAR, q])
                    value = value + rsf[j, at].astype(F32)
                rso[j, d, 1, at] = value.astype(BF16)
                rs_copy(j, d, 1, q).start()
        for d in range(2):
            terms[d] = term_at(d, 1)
        for q in range(PIECES):
            at = slice(q * part, (q + 1) * part)
            for d in range(2):
                arrive(rsb.at[j, d, 1, span(q)], rs_recv.at[j, d, 1, q])
                rso[j, d, 2, at] = (terms[d, at] + rsb[j, d, 1, at].astype(F32)).astype(BF16)
                prt_copy(j, d, q).start()
        return carry

    @pl.when(jnp.logical_not(first_pair))
    def _():
        for item in (GAIN, DOWN, UP, WK, WV, WQ, WO):
            weight_copy(item).start()

    lax.fori_loop(0, 2, layer, 0)

    @pl.when(last_pair)
    def _():
        for q in range(PIECES):
            join(2, q)
        wide = hidden[3].astype(F32)
        folded = fold(wide * wide)
        row = jnp.sum(jnp.transpose(folded), axis=0, keepdims=True)
        ssb[0] = jnp.broadcast_to(row, (8, rows))
        for i in range(1, n_tp):
            ss_copy(i).start()
        arrive(ssb.at[pl.ds(1, n_tp - 1)], few_recv.at[0])
        row = jnp.sum(ssb[...], axis=0)[:1]
        column = jnp.transpose(jnp.broadcast_to(row, (rows, rows)))[:, :1]
        scale = lax.rsqrt(column * (1.0 / full_width) + 1e-5)
        n = lengths[e]
        position = c * rows + lax.broadcasted_iota(jnp.int32, (rows, 1), 0)
        scale = jnp.where(position < n, scale, 0.0)
        pooled = jnp.sum(hidden[3].astype(F32) * scale, axis=0, keepdims=True)
        ppb[0] = jnp.broadcast_to(pooled * closing[...] / n.astype(F32), (8, width))
        for i in range(1, n_ctx):
            pp_copy(i).start()
        arrive(ppb.at[pl.ds(1, n_ctx - 1)], few_recv.at[1])
        pooled = jnp.sum(ppb[...], axis=0)
        sqb[0] = jnp.broadcast_to(jnp.sum(pooled * pooled, axis=1, keepdims=True), (8, HEAD))
        for i in range(1, n_tp):
            sq_copy(i).start()
        arrive(sqb.at[pl.ds(1, n_tp - 1)], few_recv.at[2])
        norms = jnp.sum(sqb[...], axis=0)[:, :1]
        res[e] = pooled * lax.rsqrt(norms * (1.0 / full_width) + 1e-6)
        for i in range(1, sections):
            fin_copy(i).start()
        arrive(res.at[1 - e], fin_recv.at[1 - e])
        for i, buf in enumerate((ssb, ppb, sqb)):
            arrive(buf.at[pl.ds(1, buf.shape[0] - 1)], few_send.at[i])
        for i in range(1, sections):
            fin_copy(i).wait_send()

    @pl.when(jnp.logical_not(last_pair))
    def _():
        pass_copy(hidden, 0).wait_send()
        pass_copy(own, 1).wait_send()
        for i in range(micro):
            arrive(res.at[i], fin_recv.at[i])

    for i in range(micro):
        out[i:i + 1] = res[i, :1]

    for item in range(7):
        weight_copy(item).wait_send()
    for j in range(2):
        arrive(agb.at[j], ag_send.at[j, 0])
        arrive(agf.at[j], ag_send.at[j, 1])
        arrive(rso.at[j], rs_send.at[j, 0])
        arrive(rsfo.at[j], rs_send.at[j, 1])
        arrive(kvbuf.at[j, pl.ds(1, n_ctx - 1)], kv_send.at[j])


def build(mesh):
    sections, n_ctx, n_tp = (mesh.shape[a] for a in ("section", "ctx", "tp"))

    def shards(
        tokens, document_lengths, tenant_indices, attention_norm_gain, query_weight, key_weight,
        value_weight, output_weight, query_adapter_down, query_adapter_up, value_adapter_down,
        value_adapter_up, closing_norm_gain,
    ):
        micro, rows, width = tokens.shape
        query_width = query_weight.shape[2]
        tenant_count, rank = query_adapter_down.shape[1], query_adapter_down.shape[3]
        heads = query_width // HEAD

        freq = (500000.0 ** (-np.arange(HEAD // 2) / (HEAD // 2))).astype(np.float32)
        angle = np.arange(rows * n_ctx, dtype=np.float32)[:, None] * freq[None, :]
        cosine, sine = np.cos(angle.astype(np.float64)), np.sin(angle.astype(np.float64))
        tables = np.stack([np.concatenate([cosine, cosine], 1), np.concatenate([-sine, sine], 1)])
        tables = tables.reshape(2, n_ctx, rows, HEAD).transpose(1, 0, 2, 3).astype(np.float32)

        vmem = pl.BlockSpec(memory_space=pltpu.VMEM)
        hbm = pl.BlockSpec(memory_space=pl.ANY)
        smem = pl.BlockSpec(memory_space=pltpu.SMEM)
        dma = pltpu.SemaphoreType.DMA
        block = (rows, width)

        def body(*refs):
            kernel((sections, n_ctx, n_tp, micro, rows, width), *refs)

        return pl.pallas_call(
            body,
            out_shape=jax.ShapeDtypeStruct((micro, width), F32),
            in_specs=[smem, smem, hbm, hbm, vmem, hbm, hbm, hbm, hbm, hbm, hbm, hbm, vmem, vmem],
            out_specs=vmem,
            scratch_shapes=[
                pltpu.VMEM((2, n_tp, width, query_width), BF16),
                pltpu.VMEM((2, n_tp, width, 2 * HEAD), BF16),
                pltpu.VMEM((2, query_width, width * n_tp), BF16),
                pltpu.VMEM((2, 1, width * n_tp), F32),
                pltpu.VMEM((tenant_count, rank, width * n_tp), BF16),
                pltpu.VMEM((tenant_count, rank, width * n_tp), BF16),
                pltpu.VMEM((3, 2 * rank, width * n_tp), BF16),
                pltpu.VMEM((3, 2 * rank, query_width + HEAD), BF16),
                pltpu.VMEM((2, rows, HEAD), F32),
                pltpu.VMEM((4,) + block, BF16),
                pltpu.VMEM((3,) + block, BF16),
                pltpu.VMEM((2, 2, 3) + block, BF16),
                pltpu.VMEM((2,) + block, BF16),
                pltpu.VMEM((2, 2, 2) + block, BF16),
                pltpu.VMEM((2,) + block, BF16),
                pltpu.VMEM((2, 2, 3) + block, BF16),
                pltpu.VMEM((2,) + block, BF16),
                pltpu.VMEM((3, 2) + block, BF16),
                pltpu.VMEM((2, n_ctx, rows, 2 * HEAD), BF16),
                pltpu.VMEM((rows, query_width), F32),
                pltpu.VMEM((rows, 2 * HEAD), F32),
                pltpu.VMEM((rows, 2 * rank), F32),
                pltpu.VMEM((rows, HEAD), F32),
                pltpu.VMEM((heads, rows, HEAD), BF16),
                pltpu.VMEM((rows, query_width), BF16),
                pltpu.VMEM((2,) + block, F32),
                pltpu.VMEM((n_tp, 8, rows), F32),
                pltpu.VMEM((n_ctx, 8, width), F32),
                pltpu.VMEM((n_tp, 8, HEAD), F32),
                pltpu.VMEM((micro, 8, width), F32),
                dma((2, 7)),
                dma((7,)),
                dma((3,)),
                dma((1,)),
                dma((2, 2)),
                dma((2, 2, 4, PIECES)),
                dma((2, 2)),
                dma((2, 2, 4, PIECES)),
                dma((3, 2, PIECES)),
                dma((2,)),
                dma((2, 2)),
                dma((2,)),
                dma((2,)),
                dma((3,)),
                dma((3,)),
                dma((sections,)),
                dma((micro,)),
            ],
            compiler_params=pltpu.CompilerParams(
                collective_id=0, has_side_effects=True, vmem_limit_bytes=60 << 20),
            cost_estimate=pl.CostEstimate(
                flops=micro * 2 * rows * (n_tp * width * (query_width + 3 * HEAD) * 2),
                bytes_accessed=16 << 20, transcendentals=micro * heads * rows * rows * n_ctx),
        )(
            document_lengths, tenant_indices, tokens, attention_norm_gain,
            closing_norm_gain.reshape(1, width), jnp.asarray(tables),
            query_weight.reshape(n_tp, width, query_width),
            key_weight.reshape(n_tp, width, HEAD), value_weight.reshape(n_tp, width, HEAD),
            output_weight[0],
            jnp.swapaxes(query_adapter_down[0], 1, 2), jnp.swapaxes(value_adapter_down[0], 1, 2),
            query_adapter_up[0], value_adapter_up[0],
        )

    return shards


def solution(mesh):
    placed = (
        P(None, "ctx", "tp"),
        P(),
        P(),
        P("section", None),
        P("section", None, "tp"),
        P("section", None, "tp"),
        P("section", None, "tp"),
        P("section", "tp", None),
        P("section", None, None, None),
        P("section", None, None, "tp"),
        P("section", None, None, None),
        P("section", None, None, "tp"),
        P("tp"),
    )
    return jax.shard_map(
        build(mesh), mesh=mesh, in_specs=placed, out_specs=P(None, "tp"), check_vma=False
    )
```

```python
import math

import jax
import jax.numpy as jnp
import numpy as np
from jax import lax
from jax.experimental import pallas as pl
from jax.experimental.pallas import tpu as pltpu
from jax.sharding import PartitionSpec as P

HEAD = 128
F32 = jnp.float32
BF16 = jnp.bfloat16
MESH = pl.DeviceIdType.MESH

PIECES = 4
FAR = 3
WK, WV, WQ, GAIN, WO, DOWN, UP = range(7)
NEAR = ((1, 0), (0, 1), (0, 3))
REST = ((1, 1), (1, 3), (0, 2), (1, 2))


def fold(x):
    total = x[:, :HEAD]
    for i in range(1, x.shape[1] // HEAD):
        total = total + x[:, i * HEAD:(i + 1) * HEAD]
    return total


def kernel(
    sizes,
    lengths, tenants, tokens, gain_hbm, closing, tables, wq_hbm, wk_hbm, wv_hbm, wo_hbm,
    qd_hbm, vd_hbm, q_up, v_up,
    out,
    wq, wkv, wo, gains, qd, vd, down, up, trig,
    hidden, own, agb, agf, rsb, rsf, rso, rsfo, prt, kvbuf,
    acc_q, acc_kv, acc_l, squares, qbuf, att, terms,
    ssb, ppb, sqb, res,
    w_sem, w_send, small_sem, in_sem, ag_send, ag_recv, rs_send, rs_recv, prt_recv,
    kv_send, kv_recv, pass_send, pass_recv, few_send, few_recv,
    fin_send, fin_recv,
):
    sections, n_ctx, n_tp, micro, rows, width = sizes
    full_width = width * n_tp
    part = rows // PIECES
    heads = wq.shape[3] // HEAD
    rank = q_up.shape[1]
    s = lax.axis_index("section")
    c = lax.axis_index("ctx")
    z = lax.axis_index("tp")
    e = lax.rem(s, 2)
    first_pair = s < 2
    last_pair = s >= sections - 2
    partner = s + 1 - 2 * e

    def around(at, by, n):
        return lax.rem(at + (by + n), n)

    swap = n_ctx // 2
    across = around(c, swap, n_ctx)

    def place(at):
        return jnp.where(first_pair, at, around(at, swap, n_ctx))

    def remote(src, dst, send, recv, section=s, ctx=c, tp=z):
        return pltpu.make_async_remote_copy(
            src_ref=src, dst_ref=dst, send_sem=send, recv_sem=recv, device_id=(section, ctx, tp),
            device_id_type=MESH)

    def arrive(ref, sem):
        pltpu.make_async_copy(ref, ref, sem).wait()

    def span(q):
        return pl.ds(q * part, part)

    def side(q):
        return q * 2 // PIECES

    def token_copy():
        return pltpu.make_async_copy(tokens.at[e], hidden.at[1], in_sem.at[0])

    def weight(item, j):
        return {
            WK: lambda: wkv.at[j, :, :, pl.ds(0, HEAD)],
            WV: lambda: wkv.at[j, :, :, pl.ds(HEAD, HEAD)],
            WQ: lambda: wq.at[j],
            GAIN: lambda: gains.at[j],
            WO: lambda: wo.at[j],
            DOWN: lambda: down.at[j],
            UP: lambda: up.at[j],
        }[item]()

    sources = {WK: wk_hbm, WV: wv_hbm, WQ: wq_hbm, GAIN: gain_hbm, WO: wo_hbm}
    spare = {DOWN: down.at[2], UP: up.at[2]}

    def weight_copy(item):
        return remote({**sources, **spare}[item], weight(item, e), w_send.at[item], w_sem.at[e, item],
                      section=partner)

    small_copies = [
        pltpu.make_async_copy(qd_hbm, qd, small_sem.at[0]),
        pltpu.make_async_copy(vd_hbm, vd, small_sem.at[1]),
        pltpu.make_async_copy(tables.at[place(c)], trig, small_sem.at[2]),
    ]

    @pl.when(first_pair)
    def _():
        token_copy().start()

    for copy in small_copies:
        copy.start()
    for item, source in sources.items():
        pltpu.make_async_copy(source, weight(item, e), w_sem.at[e, item]).start()

    barrier = pltpu.get_barrier_semaphore()
    neighbour = (around(z, 1, n_tp), around(z, -1, n_tp))
    peers = [(s, c, around(z, i, n_tp)) for i in range(1, n_tp)]
    peers += [(s, around(c, i, n_ctx), z) for i in range(1, n_ctx)]
    peers += [(around(s, i, sections), c, z) for i in range(1, sections)]
    peers += [(around(s, 2, sections), across, to) for to in (z,) + neighbour]
    for peer in peers:
        pl.semaphore_signal(barrier, 1, device_id=peer, device_id_type=MESH)

    for copy in small_copies:
        copy.wait()
    for slot, document in ((e, e), (2, 1 - e)):
        t = tenants[document]
        up[slot] = jnp.zeros(up.shape[1:], BF16)
        down[slot, :rank] = qd[t]
        down[slot, rank:] = vd[t]
        up[slot, :rank, :heads * HEAD] = q_up[t]
        up[slot, rank:, heads * HEAD:] = v_up[t]

    pl.semaphore_wait(barrier, len(peers))

    two_on = (around(z, 2, n_tp), around(z, -2, n_tp))

    def ag_copy(j, d, r, q, src):
        return remote(src.at[span(q)], agb.at[j, d, r, span(q)], ag_send.at[j, 0],
                      ag_recv.at[j, d, r, q if r < 2 else 0], tp=neighbour[d])

    def ag_far(j, q):
        d = side(q)
        return remote(agb.at[j, d, 1, span(q)], agf.at[j, span(q)], ag_send.at[j, 1],
                      ag_recv.at[j, 0, FAR, 0], tp=two_on[d])

    def rs_copy(j, d, r, q):
        return remote(rso.at[j, d, r, span(q)], rsb.at[j, d, r, span(q)], rs_send.at[j, 0],
                      rs_recv.at[j, d, r, q], tp=neighbour[d])

    def rs_far(j, q):
        d = side(q)
        return remote(rsfo.at[j, span(q)], rsf.at[j, span(q)], rs_send.at[j, 1],
                      rs_recv.at[j, d, FAR, q], tp=two_on[d])

    def prt_copy(j, d, q):
        slot = jnp.where(j == 0, 1, jnp.where(last_pair, 2, 0))
        moves = (j == 1) & jnp.logical_not(last_pair)
        return remote(rso.at[j, d, 2, span(q)], prt.at[slot, d, span(q)], rs_send.at[j, 0],
                      prt_recv.at[slot, d, q], tp=neighbour[d], ctx=jnp.where(moves, across, c),
                      section=jnp.where(moves, around(s, 2, sections), s))

    def pass_copy(buf, i):
        return remote(buf.at[2], buf.at[0], pass_send.at[i], pass_recv.at[i], ctx=across,
                      section=around(s, 2, sections))

    def ctx_peer(dy, dx):
        return around(c // swap, dy, 2) * swap + around(lax.rem(c, swap), dx, swap)

    ctx_ids = {offset: ctx_peer(*offset) for offset in NEAR + REST}

    def kv_copy(j, offset):
        return remote(kvbuf.at[j, c], kvbuf.at[j, c], kv_send.at[j],
                      kv_recv.at[j, 0 if offset in NEAR else 1], ctx=ctx_ids[offset])

    def ss_copy(i):
        return remote(ssb.at[0], ssb.at[i], few_send.at[0], few_recv.at[0], tp=around(z, i, n_tp))

    def pp_copy(i):
        return remote(ppb.at[0], ppb.at[i], few_send.at[1], few_recv.at[1], ctx=around(c, i, n_ctx))

    def sq_copy(i):
        return remote(sqb.at[0], sqb.at[i], few_send.at[2], few_recv.at[2], tp=around(z, i, n_tp))

    def fin_copy(i):
        return remote(res.at[e], res.at[e], fin_send.at[i], fin_recv.at[e], section=around(s, i, sections))

    def rotate(x):
        return x * trig[0] + pltpu.roll(x, HEAD // 2, axis=1) * trig[1]

    def take(j, blocks, first=False, queries=True, others=True):
        values = None
        for block, g in blocks:
            h = block.astype(F32)
            columns = pl.ds(pl.multiple_of(g * width, width), width)
            x = (h * gains[j, :, columns]).astype(BF16)
            new = []
            if others:
                new += [
                    fold(h * h),
                    jnp.dot(x, wkv[j, g], preferred_element_type=F32),
                    lax.dot_general(
                        x, down[j, :, columns], (((1,), (1,)), ((), ())), preferred_element_type=F32),
                ]
            if queries:
                new.append(jnp.dot(x, wq[j, g], preferred_element_type=F32))
            values = new if values is None else [a + b for a, b in zip(values, new)]
        refs = ((squares, acc_kv, acc_l) if others else ()) + ((acc_q,) if queries else ())
        for ref, value in zip(refs, values):
            ref[...] = value if first else ref[...] + value

    def join(i, q):
        for d in range(2):
            arrive(prt.at[i, d, span(q)], prt_recv.at[i, d, q])
        at = slice(q * part, (q + 1) * part)
        sums = prt[i, 0, at].astype(F32) + prt[i, 1, at].astype(F32)
        hidden[i + 1, at] = (hidden[i, at].astype(F32) + own[i, at].astype(F32) + sums).astype(BF16)

    def layer(j, carry):
        @pl.when(first_pair & (j == 0))
        def _():
            token_copy().wait()

        @pl.when(jnp.logical_not(first_pair) & (j == 0))
        def _():
            arrive(hidden.at[0], pass_recv.at[0])
            arrive(own.at[0], pass_recv.at[1])

        for q in range(PIECES):
            @pl.when(jnp.logical_not(first_pair) | (j == 1))
            def _():
                join(j, q)

            for d in range(2):
                ag_copy(j, d, 0, q, hidden.at[j + 1]).start()

        @pl.when(first_pair & (j == 0))
        def _():
            for item in (GAIN, DOWN, UP, WK, WV, WQ):
                weight_copy(item).start()

        @pl.when((j == 1) & jnp.logical_not(last_pair))
        def _():
            pass_copy(hidden, 0).start()

        def own_take():
            for item in (GAIN, WK, WV, WQ):
                arrive(weight(item, j), w_sem.at[j, item])

            @pl.when(j != e)
            def _():
                for item in (DOWN, UP):
                    arrive(weight(item, j), w_sem.at[j, item])

            take(j, [(hidden[j + 1], z)], first=True)

        def pair(r):
            return [(agb[j, d, r], around(z, -1 - r if d == 0 else 1 + r, n_tp)) for d in range(2)]

        late = first_pair & (e == 1) & (j == 0)
        prompt = jnp.logical_not(late)

        @pl.when(prompt)
        def _():
            own_take()

        for r in range(2):
            for q in range(PIECES):
                for d in range(2):
                    arrive(agb.at[j, d, r, span(q)], ag_recv.at[j, d, r, q])
                    ag_copy(j, d, r + 1, q, agb.at[j, d, r]).start()
                    if r == 1 and d == side(q):
                        ag_far(j, q).start()

            @pl.when(prompt)
            def _():
                take(j, pair(r))

        @pl.when(first_pair & (j == 0))
        def _():
            weight_copy(WO).start()

        @pl.when(late)
        def _():
            own_take()
            for r in range(2):
                take(j, pair(r))

        for d in range(2):
            arrive(agb.at[j, d, 2], ag_recv.at[j, d, 2, 0])
        take(j, pair(2), queries=False)
        arrive(agf.at[j], ag_recv.at[j, 0, FAR, 0])
        far = [(agf[j], around(z, 4, n_tp))]
        take(j, far, queries=False)

        mean = jnp.sum(squares[...], axis=1, keepdims=True) * (1.0 / full_width)
        scale = lax.rsqrt(mean + 1e-5)
        low = (acc_l[...] * scale).astype(BF16)
        kv = acc_kv[...] * scale
        kvbuf[j, c, :, :HEAD] = rotate(kv[:, :HEAD]).astype(BF16)
        added = jnp.dot(low, up[j, :, heads * HEAD:], preferred_element_type=F32)
        kvbuf[j, c, :, HEAD:] = (kv[:, HEAD:] + added).astype(BF16)
        for offset in NEAR + REST:
            kv_copy(j, offset).start()
        take(j, pair(2) + far, others=False)
        factor = HEAD ** -0.5 * math.log2(math.e)
        for g in range(heads):
            cols = slice(g * HEAD, (g + 1) * HEAD)
            q = acc_q[:, cols] * scale + jnp.dot(low, up[j, :, cols], preferred_element_type=F32)
            qbuf[g] = (rotate(q) * factor).astype(BF16)

        n = lengths[e]
        lane = lax.broadcasted_iota(jnp.int32, (1, rows), 1)

        def keys_of(offsets):
            sources = [ctx_peer(-dy, -dx) for dy, dx in offsets]
            blocks = [kvbuf[j, source] for source in sources]
            valid = jnp.concatenate([lane + place(source) * rows < n for source in sources], axis=1)
            return (jnp.concatenate([block[:, :HEAD] for block in blocks], axis=0),
                    jnp.concatenate([block[:, HEAD:] for block in blocks], axis=0), valid)

        def scored(g, keys, valid):
            scores = lax.dot_general(
                qbuf[g], keys, (((1,), (1,)), ((), ())), preferred_element_type=F32)
            return jnp.where(valid, scores, -1e30)

        arrive(kvbuf.at[j, pl.ds(0, len(NEAR))], kv_recv.at[j, 0])
        keys, values, valid = keys_of(((0, 0),) + NEAR)
        near = []
        for g in range(heads):
            scores = scored(g, keys, valid)
            top = jnp.max(scores, axis=1, keepdims=True)
            weights = jnp.exp2(scores - top)
            total = jnp.sum(weights, axis=1, keepdims=True)
            near.append((top, total, jnp.dot(weights.astype(BF16), values, preferred_element_type=F32)))
        arrive(kvbuf.at[j, pl.ds(0, len(REST))], kv_recv.at[j, 1])
        keys, values, valid = keys_of(REST)
        for g in range(heads):
            top_near, total_near, mixed_near = near[g]
            scores = scored(g, keys, valid)
            top = jnp.maximum(jnp.max(scores, axis=1, keepdims=True), top_near)
            weights = jnp.exp2(scores - top)
            fade = jnp.exp2(top_near - top)
            total = jnp.sum(weights, axis=1, keepdims=True) + total_near * fade
            mixed = jnp.dot(weights.astype(BF16), values, preferred_element_type=F32) + mixed_near * fade
            att[:, g * HEAD:(g + 1) * HEAD] = (mixed * (1.0 / total)).astype(BF16)

        arrive(weight(WO, j), w_sem.at[j, WO])

        def term(index):
            columns = pl.ds(pl.multiple_of(index * width, width), width)
            return jnp.dot(att[...], wo[j, :, columns], preferred_element_type=F32)

        def term_at(d, distance):
            return term(around(z, distance if d == 0 else -distance, n_tp))

        rsfo[j] = term_at(0, 4).astype(BF16)
        for q in range(PIECES):
            rs_far(j, q).start()
        for d in range(2):
            rso[j, d, 0] = term_at(d, 3).astype(BF16)
            for q in range(PIECES):
                rs_copy(j, d, 0, q).start()
        for d in range(2):
            terms[d] = term_at(d, 2)
        own[j + 1] = term(z).astype(BF16)

        @pl.when((j == 1) & jnp.logical_not(last_pair))
        def _():
            pass_copy(own, 1).start()

        for q in range(PIECES):
            at = slice(q * part, (q + 1) * part)
            for d in (side(q), 1 - side(q)):
                arrive(rsb.at[j, d, 0, span(q)], rs_recv.at[j, d, 0, q])
                value = terms[d, at] + rsb[j, d, 0, at].astype(F32)
                if d == side(q):
                    arrive(rsf.at[j, span(q)], rs_recv.at[j, d, FAR, q])
                    value = value + rsf[j, at].astype(F32)
                rso[j, d, 1, at] = value.astype(BF16)
                rs_copy(j, d, 1, q).start()
        for d in range(2):
            terms[d] = term_at(d, 1)
        for q in range(PIECES):
            at = slice(q * part, (q + 1) * part)
            for d in range(2):
                arrive(rsb.at[j, d, 1, span(q)], rs_recv.at[j, d, 1, q])
                rso[j, d, 2, at] = (terms[d, at] + rsb[j, d, 1, at].astype(F32)).astype(BF16)
                prt_copy(j, d, q).start()
        return carry

    @pl.when(jnp.logical_not(first_pair))
    def _():
        for item in (GAIN, DOWN, UP, WK, WV, WQ, WO):
            weight_copy(item).start()

    lax.fori_loop(0, 2, layer, 0)

    @pl.when(last_pair)
    def _():
        for q in range(PIECES):
            join(2, q)
        wide = hidden[3].astype(F32)
        folded = fold(wide * wide)
        row = jnp.sum(jnp.transpose(folded), axis=0, keepdims=True)
        ssb[0] = jnp.broadcast_to(row, (8, rows))
        for i in range(1, n_tp):
            ss_copy(i).start()
        arrive(ssb.at[pl.ds(1, n_tp - 1)], few_recv.at[0])
        row = jnp.sum(ssb[...], axis=0)[:1]
        column = jnp.transpose(jnp.broadcast_to(row, (rows, rows)))[:, :1]
        scale = lax.rsqrt(column * (1.0 / full_width) + 1e-5)
        n = lengths[e]
        position = place(c) * rows + lax.broadcasted_iota(jnp.int32, (rows, 1), 0)
        scale = jnp.where(position < n, scale, 0.0)
        pooled = jnp.sum(hidden[3].astype(F32) * scale, axis=0, keepdims=True)
        ppb[0] = jnp.broadcast_to(pooled * closing[...] / n.astype(F32), (8, width))
        for i in range(1, n_ctx):
            pp_copy(i).start()
        arrive(ppb.at[pl.ds(1, n_ctx - 1)], few_recv.at[1])
        pooled = jnp.sum(ppb[...], axis=0)
        sqb[0] = jnp.broadcast_to(jnp.sum(pooled * pooled, axis=1, keepdims=True), (8, HEAD))
        for i in range(1, n_tp):
            sq_copy(i).start()
        arrive(sqb.at[pl.ds(1, n_tp - 1)], few_recv.at[2])
        norms = jnp.sum(sqb[...], axis=0)[:, :1]
        res[e] = pooled * lax.rsqrt(norms * (1.0 / full_width) + 1e-6)
        for i in range(1, sections):
            fin_copy(i).start()
        arrive(res.at[1 - e], fin_recv.at[1 - e])
        for i, buf in enumerate((ssb, ppb, sqb)):
            arrive(buf.at[pl.ds(1, buf.shape[0] - 1)], few_send.at[i])
        for i in range(1, sections):
            fin_copy(i).wait_send()

    @pl.when(jnp.logical_not(last_pair))
    def _():
        pass_copy(hidden, 0).wait_send()
        pass_copy(own, 1).wait_send()
        for i in range(micro):
            arrive(res.at[i], fin_recv.at[i])

    for i in range(micro):
        out[i:i + 1] = res[i, :1]

    for item in range(7):
        weight_copy(item).wait_send()
    for j in range(2):
        arrive(agb.at[j], ag_send.at[j, 0])
        arrive(agf.at[j], ag_send.at[j, 1])
        arrive(rso.at[j], rs_send.at[j, 0])
        arrive(rsfo.at[j], rs_send.at[j, 1])
        arrive(kvbuf.at[j, pl.ds(1, n_ctx - 1)], kv_send.at[j])


def build(mesh):
    sections, n_ctx, n_tp = (mesh.shape[a] for a in ("section", "ctx", "tp"))

    def shards(
        tokens, document_lengths, tenant_indices, attention_norm_gain, query_weight, key_weight,
        value_weight, output_weight, query_adapter_down, query_adapter_up, value_adapter_down,
        value_adapter_up, closing_norm_gain,
    ):
        micro, rows, width = tokens.shape
        query_width = query_weight.shape[2]
        tenant_count, rank = query_adapter_down.shape[1], query_adapter_down.shape[3]
        heads = query_width // HEAD

        freq = (500000.0 ** (-np.arange(HEAD // 2) / (HEAD // 2))).astype(np.float32)
        angle = np.arange(rows * n_ctx, dtype=np.float32)[:, None] * freq[None, :]
        cosine, sine = np.cos(angle.astype(np.float64)), np.sin(angle.astype(np.float64))
        tables = np.stack([np.concatenate([cosine, cosine], 1), np.concatenate([-sine, sine], 1)])
        tables = tables.reshape(2, n_ctx, rows, HEAD).transpose(1, 0, 2, 3).astype(np.float32)

        vmem = pl.BlockSpec(memory_space=pltpu.VMEM)
        hbm = pl.BlockSpec(memory_space=pl.ANY)
        smem = pl.BlockSpec(memory_space=pltpu.SMEM)
        dma = pltpu.SemaphoreType.DMA
        block = (rows, width)

        def body(*refs):
            kernel((sections, n_ctx, n_tp, micro, rows, width), *refs)

        return pl.pallas_call(
            body,
            out_shape=jax.ShapeDtypeStruct((micro, width), F32),
            in_specs=[smem, smem, hbm, hbm, vmem, hbm, hbm, hbm, hbm, hbm, hbm, hbm, vmem, vmem],
            out_specs=vmem,
            scratch_shapes=[
                pltpu.VMEM((2, n_tp, width, query_width), BF16),
                pltpu.VMEM((2, n_tp, width, 2 * HEAD), BF16),
                pltpu.VMEM((2, query_width, width * n_tp), BF16),
                pltpu.VMEM((2, 1, width * n_tp), F32),
                pltpu.VMEM((tenant_count, rank, width * n_tp), BF16),
                pltpu.VMEM((tenant_count, rank, width * n_tp), BF16),
                pltpu.VMEM((3, 2 * rank, width * n_tp), BF16),
                pltpu.VMEM((3, 2 * rank, query_width + HEAD), BF16),
                pltpu.VMEM((2, rows, HEAD), F32),
                pltpu.VMEM((4,) + block, BF16),
                pltpu.VMEM((3,) + block, BF16),
                pltpu.VMEM((2, 2, 3) + block, BF16),
                pltpu.VMEM((2,) + block, BF16),
                pltpu.VMEM((2, 2, 2) + block, BF16),
                pltpu.VMEM((2,) + block, BF16),
                pltpu.VMEM((2, 2, 3) + block, BF16),
                pltpu.VMEM((2,) + block, BF16),
                pltpu.VMEM((3, 2) + block, BF16),
                pltpu.VMEM((2, n_ctx, rows, 2 * HEAD), BF16),
                pltpu.VMEM((rows, query_width), F32),
                pltpu.VMEM((rows, 2 * HEAD), F32),
                pltpu.VMEM((rows, 2 * rank), F32),
                pltpu.VMEM((rows, HEAD), F32),
                pltpu.VMEM((heads, rows, HEAD), BF16),
                pltpu.VMEM((rows, query_width), BF16),
                pltpu.VMEM((2,) + block, F32),
                pltpu.VMEM((n_tp, 8, rows), F32),
                pltpu.VMEM((n_ctx, 8, width), F32),
                pltpu.VMEM((n_tp, 8, HEAD), F32),
                pltpu.VMEM((micro, 8, width), F32),
                dma((2, 7)),
                dma((7,)),
                dma((3,)),
                dma((1,)),
                dma((2, 2)),
                dma((2, 2, 4, PIECES)),
                dma((2, 2)),
                dma((2, 2, 4, PIECES)),
                dma((3, 2, PIECES)),
                dma((2,)),
                dma((2, 2)),
                dma((2,)),
                dma((2,)),
                dma((3,)),
                dma((3,)),
                dma((sections,)),
                dma((micro,)),
            ],
            compiler_params=pltpu.CompilerParams(
                collective_id=0, has_side_effects=True, vmem_limit_bytes=60 << 20),
            cost_estimate=pl.CostEstimate(
                flops=micro * 2 * rows * (n_tp * width * (query_width + 3 * HEAD) * 2),
                bytes_accessed=16 << 20, transcendentals=micro * heads * rows * rows * n_ctx),
        )(
            document_lengths, tenant_indices, tokens, attention_norm_gain,
            closing_norm_gain.reshape(1, width), jnp.asarray(tables),
            query_weight.reshape(n_tp, width, query_width),
            key_weight.reshape(n_tp, width, HEAD), value_weight.reshape(n_tp, width, HEAD),
            output_weight[0],
            jnp.swapaxes(query_adapter_down[0], 1, 2), jnp.swapaxes(value_adapter_down[0], 1, 2),
            query_adapter_up[0], value_adapter_up[0],
        )

    return shards


def solution(mesh):
    placed = (
        P(None, "ctx", "tp"),
        P(),
        P(),
        P("section", None),
        P("section", None, "tp"),
        P("section", None, "tp"),
        P("section", None, "tp"),
        P("section", "tp", None),
        P("section", None, None, None),
        P("section", None, None, "tp"),
        P("section", None, None, None),
        P("section", None, None, "tp"),
        P("tp"),
    )
    return jax.shard_map(
        build(mesh), mesh=mesh, in_specs=placed, out_specs=P(None, "tp"), check_vma=False
    )
```

```python
import math

import jax
import jax.numpy as jnp
import numpy as np
from jax import lax
from jax.experimental import pallas as pl
from jax.experimental.pallas import tpu as pltpu
from jax.sharding import PartitionSpec as P

HEAD = 128
F32 = jnp.float32
BF16 = jnp.bfloat16
MESH = pl.DeviceIdType.MESH

PIECES = 4
FAR = 3
WK, WV, WQ, GAIN, WO, DOWN, UP = range(7)
NEAR = ((1, 0), (0, 1), (0, 3))
REST = ((1, 1), (1, 3), (0, 2), (1, 2))


def fold(x):
    total = x[:, :HEAD]
    for i in range(1, x.shape[1] // HEAD):
        total = total + x[:, i * HEAD:(i + 1) * HEAD]
    return total


def kernel(
    sizes,
    lengths, tenants, tokens, gain_hbm, closing, tables, wq_hbm, wk_hbm, wv_hbm, wo_hbm,
    qd_hbm, vd_hbm, q_up, v_up,
    out,
    wq, wkv, wo, gains, qd, vd, down, up, trig,
    hidden, own, agb, agf, rsb, rsf, rso, rsfo, prt, kvbuf,
    acc_q, acc_kv, acc_l, squares, qbuf, att, terms,
    ssb, ppb, sqb, res,
    w_sem, w_send, small_sem, in_sem, ag_send, ag_recv, rs_send, rs_recv, prt_recv,
    kv_send, kv_recv, pass_send, pass_recv, few_send, few_recv,
    fin_send, fin_recv,
):
    sections, n_ctx, n_tp, micro, rows, width = sizes
    full_width = width * n_tp
    part = rows // PIECES
    heads = wq.shape[3] // HEAD
    rank = q_up.shape[1]
    s = lax.axis_index("section")
    c = lax.axis_index("ctx")
    z = lax.axis_index("tp")
    e = lax.rem(s, 2)
    first_pair = s < 2
    last_pair = s >= sections - 2
    partner = s + 1 - 2 * e

    def around(at, by, n):
        return lax.rem(at + (by + n), n)

    swap = n_ctx // 2
    across = around(c, swap, n_ctx)

    def place(at):
        return jnp.where(first_pair, at, around(at, swap, n_ctx))

    def remote(src, dst, send, recv, section=s, ctx=c, tp=z):
        return pltpu.make_async_remote_copy(
            src_ref=src, dst_ref=dst, send_sem=send, recv_sem=recv, device_id=(section, ctx, tp),
            device_id_type=MESH)

    def arrive(ref, sem):
        pltpu.make_async_copy(ref, ref, sem).wait()

    def span(q):
        return pl.ds(q * part, part)

    def side(q):
        return q * 2 // PIECES

    def token_copy():
        return pltpu.make_async_copy(tokens.at[e], hidden.at[1], in_sem.at[0])

    def weight(item, j):
        return {
            WK: lambda: wkv.at[j, :, :, pl.ds(0, HEAD)],
            WV: lambda: wkv.at[j, :, :, pl.ds(HEAD, HEAD)],
            WQ: lambda: wq.at[j],
            GAIN: lambda: gains.at[j],
            WO: lambda: wo.at[j],
            DOWN: lambda: down.at[j],
            UP: lambda: up.at[j],
        }[item]()

    sources = {WK: wk_hbm, WV: wv_hbm, WQ: wq_hbm, GAIN: gain_hbm, WO: wo_hbm}
    spare = {DOWN: down.at[2], UP: up.at[2]}

    def weight_copy(item):
        return remote({**sources, **spare}[item], weight(item, e), w_send.at[item], w_sem.at[e, item],
                      section=partner)

    small_copies = [
        pltpu.make_async_copy(qd_hbm, qd, small_sem.at[0]),
        pltpu.make_async_copy(vd_hbm, vd, small_sem.at[1]),
        pltpu.make_async_copy(tables.at[place(c)], trig, small_sem.at[2]),
    ]

    @pl.when(first_pair)
    def _():
        token_copy().start()

    for copy in small_copies:
        copy.start()
    for item, source in sources.items():
        pltpu.make_async_copy(source, weight(item, e), w_sem.at[e, item]).start()

    barrier = pltpu.get_barrier_semaphore()
    neighbour = (around(z, 1, n_tp), around(z, -1, n_tp))
    peers = [(s, c, around(z, i, n_tp)) for i in range(1, n_tp)]
    peers += [(s, around(c, i, n_ctx), z) for i in range(1, n_ctx)]
    peers += [(around(s, i, sections), c, z) for i in range(1, sections)]
    peers += [(around(s, 2, sections), across, to) for to in (z,) + neighbour]
    for peer in peers:
        pl.semaphore_signal(barrier, 1, device_id=peer, device_id_type=MESH)

    def pick_adapters():
        for copy in small_copies:
            copy.wait()
        for slot, document in ((e, e), (2, 1 - e)):
            t = tenants[document]
            up[slot] = jnp.zeros(up.shape[1:], BF16)
            down[slot, :rank] = qd[t]
            down[slot, rank:] = vd[t]
            up[slot, :rank, :heads * HEAD] = q_up[t]
            up[slot, rank:, heads * HEAD:] = v_up[t]

    pl.semaphore_wait(barrier, len(peers))

    two_on = (around(z, 2, n_tp), around(z, -2, n_tp))

    def ag_copy(j, d, r, q, src):
        return remote(src.at[span(q)], agb.at[j, d, r, span(q)], ag_send.at[j, 0],
                      ag_recv.at[j, d, r, q if r < 2 else 0], tp=neighbour[d])

    def ag_far(j, q):
        d = side(q)
        return remote(agb.at[j, d, 1, span(q)], agf.at[j, span(q)], ag_send.at[j, 1],
                      ag_recv.at[j, 0, FAR, 0], tp=two_on[d])

    def rs_copy(j, d, r, q):
        return remote(rso.at[j, d, r, span(q)], rsb.at[j, d, r, span(q)], rs_send.at[j, 0],
                      rs_recv.at[j, d, r, q], tp=neighbour[d])

    def rs_far(j, q):
        d = side(q)
        return remote(rsfo.at[j, span(q)], rsf.at[j, span(q)], rs_send.at[j, 1],
                      rs_recv.at[j, d, FAR, q], tp=two_on[d])

    def prt_copy(j, d, q):
        slot = jnp.where(j == 0, 1, jnp.where(last_pair, 2, 0))
        moves = (j == 1) & jnp.logical_not(last_pair)
        return remote(rso.at[j, d, 2, span(q)], prt.at[slot, d, span(q)], rs_send.at[j, 0],
                      prt_recv.at[slot, d, q], tp=neighbour[d], ctx=jnp.where(moves, across, c),
                      section=jnp.where(moves, around(s, 2, sections), s))

    def pass_copy(buf, i):
        return remote(buf.at[2], buf.at[0], pass_send.at[i], pass_recv.at[i], ctx=across,
                      section=around(s, 2, sections))

    def ctx_peer(dy, dx):
        return around(c // swap, dy, 2) * swap + around(lax.rem(c, swap), dx, swap)

    ctx_ids = {offset: ctx_peer(*offset) for offset in NEAR + REST}

    def kv_copy(j, offset):
        return remote(kvbuf.at[j, c], kvbuf.at[j, c], kv_send.at[j],
                      kv_recv.at[j, 0 if offset in NEAR else 1], ctx=ctx_ids[offset])

    def ss_copy(i):
        return remote(ssb.at[0], ssb.at[i], few_send.at[0], few_recv.at[0], tp=around(z, i, n_tp))

    def pp_copy(i):
        return remote(ppb.at[0], ppb.at[i], few_send.at[1], few_recv.at[1], ctx=around(c, i, n_ctx))

    def sq_copy(i):
        return remote(sqb.at[0], sqb.at[i], few_send.at[2], few_recv.at[2], tp=around(z, i, n_tp))

    def fin_copy(i):
        return remote(res.at[e], res.at[e], fin_send.at[i], fin_recv.at[e], section=around(s, i, sections))

    def rotate(x):
        return x * trig[0] + pltpu.roll(x, HEAD // 2, axis=1) * trig[1]

    def take(j, blocks, first=False, queries=True, others=True):
        values = None
        for block, g in blocks:
            h = block.astype(F32)
            columns = pl.ds(pl.multiple_of(g * width, width), width)
            x = (h * gains[j, :, columns]).astype(BF16)
            new = []
            if others:
                new += [
                    fold(h * h),
                    jnp.dot(x, wkv[j, g], preferred_element_type=F32),
                    lax.dot_general(
                        x, down[j, :, columns], (((1,), (1,)), ((), ())), preferred_element_type=F32),
                ]
            if queries:
                new.append(jnp.dot(x, wq[j, g], preferred_element_type=F32))
            values = new if values is None else [a + b for a, b in zip(values, new)]
        refs = ((squares, acc_kv, acc_l) if others else ()) + ((acc_q,) if queries else ())
        for ref, value in zip(refs, values):
            ref[...] = value if first else ref[...] + value

    def join(i, q):
        for d in range(2):
            arrive(prt.at[i, d, span(q)], prt_recv.at[i, d, q])
        at = slice(q * part, (q + 1) * part)
        sums = prt[i, 0, at].astype(F32) + prt[i, 1, at].astype(F32)
        hidden[i + 1, at] = (hidden[i, at].astype(F32) + own[i, at].astype(F32) + sums).astype(BF16)

    def layer(j, carry):
        @pl.when(first_pair & (j == 0))
        def _():
            token_copy().wait()

        @pl.when(jnp.logical_not(first_pair) & (j == 0))
        def _():
            arrive(hidden.at[0], pass_recv.at[0])
            arrive(own.at[0], pass_recv.at[1])

        for q in range(PIECES):
            @pl.when(jnp.logical_not(first_pair) | (j == 1))
            def _():
                join(j, q)

            for d in range(2):
                ag_copy(j, d, 0, q, hidden.at[j + 1]).start()

        @pl.when(first_pair & (j == 0))
        def _():
            for item in (WK, WV, WQ, GAIN):
                weight_copy(item).start()
            pick_adapters()
            for item in (DOWN, UP):
                weight_copy(item).start()

        @pl.when((j == 1) & jnp.logical_not(last_pair))
        def _():
            pass_copy(hidden, 0).start()

        def own_take():
            for item in (GAIN, WK, WV, WQ):
                arrive(weight(item, j), w_sem.at[j, item])

            @pl.when(j != e)
            def _():
                for item in (DOWN, UP):
                    arrive(weight(item, j), w_sem.at[j, item])

            take(j, [(hidden[j + 1], z)], first=True)

        def pair(r):
            return [(agb[j, d, r], around(z, -1 - r if d == 0 else 1 + r, n_tp)) for d in range(2)]

        late = first_pair & (e == 1) & (j == 0)
        prompt = jnp.logical_not(late)

        @pl.when(prompt)
        def _():
            own_take()

        for r in range(2):
            for q in range(PIECES):
                for d in range(2):
                    arrive(agb.at[j, d, r, span(q)], ag_recv.at[j, d, r, q])
                    ag_copy(j, d, r + 1, q, agb.at[j, d, r]).start()
                    if r == 1 and d == side(q):
                        ag_far(j, q).start()

            @pl.when(prompt)
            def _():
                take(j, pair(r))

        @pl.when(first_pair & (j == 0))
        def _():
            weight_copy(WO).start()

        @pl.when(late)
        def _():
            own_take()
            for r in range(2):
                take(j, pair(r))

        for d in range(2):
            arrive(agb.at[j, d, 2], ag_recv.at[j, d, 2, 0])
        take(j, pair(2), queries=False)
        arrive(agf.at[j], ag_recv.at[j, 0, FAR, 0])
        far = [(agf[j], around(z, 4, n_tp))]
        take(j, far, queries=False)

        mean = jnp.sum(squares[...], axis=1, keepdims=True) * (1.0 / full_width)
        scale = lax.rsqrt(mean + 1e-5)
        low = (acc_l[...] * scale).astype(BF16)
        kv = acc_kv[...] * scale
        kvbuf[j, c, :, :HEAD] = rotate(kv[:, :HEAD]).astype(BF16)
        added = jnp.dot(low, up[j, :, heads * HEAD:], preferred_element_type=F32)
        kvbuf[j, c, :, HEAD:] = (kv[:, HEAD:] + added).astype(BF16)
        for offset in NEAR + REST:
            kv_copy(j, offset).start()
        take(j, pair(2) + far, others=False)
        factor = HEAD ** -0.5 * math.log2(math.e)
        for g in range(heads):
            cols = slice(g * HEAD, (g + 1) * HEAD)
            q = acc_q[:, cols] * scale + jnp.dot(low, up[j, :, cols], preferred_element_type=F32)
            qbuf[g] = (rotate(q) * factor).astype(BF16)

        n = lengths[e]
        lane = lax.broadcasted_iota(jnp.int32, (1, rows), 1)

        def keys_of(offsets):
            sources = [ctx_peer(-dy, -dx) for dy, dx in offsets]
            blocks = [kvbuf[j, source] for source in sources]
            valid = jnp.concatenate([lane + place(source) * rows < n for source in sources], axis=1)
            return (jnp.concatenate([block[:, :HEAD] for block in blocks], axis=0),
                    jnp.concatenate([block[:, HEAD:] for block in blocks], axis=0), valid)

        def scored(g, keys, valid):
            scores = lax.dot_general(
                qbuf[g], keys, (((1,), (1,)), ((), ())), preferred_element_type=F32)
            return jnp.where(valid, scores, -1e30)

        arrive(kvbuf.at[j, pl.ds(0, len(NEAR))], kv_recv.at[j, 0])
        keys, values, valid = keys_of(((0, 0),) + NEAR)
        near = []
        for g in range(heads):
            scores = scored(g, keys, valid)
            top = jnp.max(scores, axis=1, keepdims=True)
            weights = jnp.exp2(scores - top)
            total = jnp.sum(weights, axis=1, keepdims=True)
            near.append((top, total, jnp.dot(weights.astype(BF16), values, preferred_element_type=F32)))
        arrive(kvbuf.at[j, pl.ds(0, len(REST))], kv_recv.at[j, 1])
        keys, values, valid = keys_of(REST)
        for g in range(heads):
            top_near, total_near, mixed_near = near[g]
            scores = scored(g, keys, valid)
            top = jnp.maximum(jnp.max(scores, axis=1, keepdims=True), top_near)
            weights = jnp.exp2(scores - top)
            fade = jnp.exp2(top_near - top)
            total = jnp.sum(weights, axis=1, keepdims=True) + total_near * fade
            mixed = jnp.dot(weights.astype(BF16), values, preferred_element_type=F32) + mixed_near * fade
            att[:, g * HEAD:(g + 1) * HEAD] = (mixed * (1.0 / total)).astype(BF16)

        arrive(weight(WO, j), w_sem.at[j, WO])

        def term(index):
            columns = pl.ds(pl.multiple_of(index * width, width), width)
            return jnp.dot(att[...], wo[j, :, columns], preferred_element_type=F32)

        def term_at(d, distance):
            return term(around(z, distance if d == 0 else -distance, n_tp))

        rsfo[j] = term_at(0, 4).astype(BF16)
        for q in range(PIECES):
            rs_far(j, q).start()
        for d in range(2):
            rso[j, d, 0] = term_at(d, 3).astype(BF16)
            for q in range(PIECES):
                rs_copy(j, d, 0, q).start()
        for d in range(2):
            terms[d] = term_at(d, 2)
        own[j + 1] = term(z).astype(BF16)

        @pl.when((j == 1) & jnp.logical_not(last_pair))
        def _():
            pass_copy(own, 1).start()

        for q in range(PIECES):
            at = slice(q * part, (q + 1) * part)
            for d in (side(q), 1 - side(q)):
                arrive(rsb.at[j, d, 0, span(q)], rs_recv.at[j, d, 0, q])
                value = terms[d, at] + rsb[j, d, 0, at].astype(F32)
                if d == side(q):
                    arrive(rsf.at[j, span(q)], rs_recv.at[j, d, FAR, q])
                    value = value + rsf[j, at].astype(F32)
                rso[j, d, 1, at] = value.astype(BF16)
                rs_copy(j, d, 1, q).start()
        for d in range(2):
            terms[d] = term_at(d, 1)
        for q in range(PIECES):
            at = slice(q * part, (q + 1) * part)
            for d in range(2):
                arrive(rsb.at[j, d, 1, span(q)], rs_recv.at[j, d, 1, q])
                rso[j, d, 2, at] = (terms[d, at] + rsb[j, d, 1, at].astype(F32)).astype(BF16)
                prt_copy(j, d, q).start()
        return carry

    @pl.when(jnp.logical_not(first_pair))
    def _():
        for item in (WK, WV, WQ, WO, GAIN):
            weight_copy(item).start()
        pick_adapters()
        for item in (DOWN, UP):
            weight_copy(item).start()

    lax.fori_loop(0, 2, layer, 0)

    @pl.when(last_pair)
    def _():
        for q in range(PIECES):
            join(2, q)
        wide = hidden[3].astype(F32)
        folded = fold(wide * wide)
        row = jnp.sum(jnp.transpose(folded), axis=0, keepdims=True)
        ssb[0] = jnp.broadcast_to(row, (8, rows))
        for i in range(1, n_tp):
            ss_copy(i).start()
        arrive(ssb.at[pl.ds(1, n_tp - 1)], few_recv.at[0])
        row = jnp.sum(ssb[...], axis=0)[:1]
        column = jnp.transpose(jnp.broadcast_to(row, (rows, rows)))[:, :1]
        scale = lax.rsqrt(column * (1.0 / full_width) + 1e-5)
        n = lengths[e]
        position = place(c) * rows + lax.broadcasted_iota(jnp.int32, (rows, 1), 0)
        scale = jnp.where(position < n, scale, 0.0)
        pooled = jnp.sum(hidden[3].astype(F32) * scale, axis=0, keepdims=True)
        ppb[0] = jnp.broadcast_to(pooled * closing[...] / n.astype(F32), (8, width))
        for i in range(1, n_ctx):
            pp_copy(i).start()
        arrive(ppb.at[pl.ds(1, n_ctx - 1)], few_recv.at[1])
        pooled = jnp.sum(ppb[...], axis=0)
        sqb[0] = jnp.broadcast_to(jnp.sum(pooled * pooled, axis=1, keepdims=True), (8, HEAD))
        for i in range(1, n_tp):
            sq_copy(i).start()
        arrive(sqb.at[pl.ds(1, n_tp - 1)], few_recv.at[2])
        norms = jnp.sum(sqb[...], axis=0)[:, :1]
        res[e] = pooled * lax.rsqrt(norms * (1.0 / full_width) + 1e-6)
        for i in range(1, sections):
            fin_copy(i).start()
        arrive(res.at[1 - e], fin_recv.at[1 - e])
        for i, buf in enumerate((ssb, ppb, sqb)):
            arrive(buf.at[pl.ds(1, buf.shape[0] - 1)], few_send.at[i])
        for i in range(1, sections):
            fin_copy(i).wait_send()

    @pl.when(jnp.logical_not(last_pair))
    def _():
        pass_copy(hidden, 0).wait_send()
        pass_copy(own, 1).wait_send()
        for i in range(micro):
            arrive(res.at[i], fin_recv.at[i])

    for i in range(micro):
        out[i:i + 1] = res[i, :1]

    for item in range(7):
        weight_copy(item).wait_send()
    for j in range(2):
        arrive(agb.at[j], ag_send.at[j, 0])
        arrive(agf.at[j], ag_send.at[j, 1])
        arrive(rso.at[j], rs_send.at[j, 0])
        arrive(rsfo.at[j], rs_send.at[j, 1])
        arrive(kvbuf.at[j, pl.ds(1, n_ctx - 1)], kv_send.at[j])


def build(mesh):
    sections, n_ctx, n_tp = (mesh.shape[a] for a in ("section", "ctx", "tp"))

    def shards(
        tokens, document_lengths, tenant_indices, attention_norm_gain, query_weight, key_weight,
        value_weight, output_weight, query_adapter_down, query_adapter_up, value_adapter_down,
        value_adapter_up, closing_norm_gain,
    ):
        micro, rows, width = tokens.shape
        query_width = query_weight.shape[2]
        tenant_count, rank = query_adapter_down.shape[1], query_adapter_down.shape[3]
        heads = query_width // HEAD

        freq = (500000.0 ** (-np.arange(HEAD // 2) / (HEAD // 2))).astype(np.float32)
        angle = np.arange(rows * n_ctx, dtype=np.float32)[:, None] * freq[None, :]
        cosine, sine = np.cos(angle.astype(np.float64)), np.sin(angle.astype(np.float64))
        tables = np.stack([np.concatenate([cosine, cosine], 1), np.concatenate([-sine, sine], 1)])
        tables = tables.reshape(2, n_ctx, rows, HEAD).transpose(1, 0, 2, 3).astype(np.float32)

        vmem = pl.BlockSpec(memory_space=pltpu.VMEM)
        hbm = pl.BlockSpec(memory_space=pl.ANY)
        smem = pl.BlockSpec(memory_space=pltpu.SMEM)
        dma = pltpu.SemaphoreType.DMA
        block = (rows, width)

        def body(*refs):
            kernel((sections, n_ctx, n_tp, micro, rows, width), *refs)

        return pl.pallas_call(
            body,
            out_shape=jax.ShapeDtypeStruct((micro, width), F32),
            in_specs=[smem, smem, hbm, hbm, vmem, hbm, hbm, hbm, hbm, hbm, hbm, hbm, vmem, vmem],
            out_specs=vmem,
            scratch_shapes=[
                pltpu.VMEM((2, n_tp, width, query_width), BF16),
                pltpu.VMEM((2, n_tp, width, 2 * HEAD), BF16),
                pltpu.VMEM((2, query_width, width * n_tp), BF16),
                pltpu.VMEM((2, 1, width * n_tp), F32),
                pltpu.VMEM((tenant_count, rank, width * n_tp), BF16),
                pltpu.VMEM((tenant_count, rank, width * n_tp), BF16),
                pltpu.VMEM((3, 2 * rank, width * n_tp), BF16),
                pltpu.VMEM((3, 2 * rank, query_width + HEAD), BF16),
                pltpu.VMEM((2, rows, HEAD), F32),
                pltpu.VMEM((4,) + block, BF16),
                pltpu.VMEM((3,) + block, BF16),
                pltpu.VMEM((2, 2, 3) + block, BF16),
                pltpu.VMEM((2,) + block, BF16),
                pltpu.VMEM((2, 2, 2) + block, BF16),
                pltpu.VMEM((2,) + block, BF16),
                pltpu.VMEM((2, 2, 3) + block, BF16),
                pltpu.VMEM((2,) + block, BF16),
                pltpu.VMEM((3, 2) + block, BF16),
                pltpu.VMEM((2, n_ctx, rows, 2 * HEAD), BF16),
                pltpu.VMEM((rows, query_width), F32),
                pltpu.VMEM((rows, 2 * HEAD), F32),
                pltpu.VMEM((rows, 2 * rank), F32),
                pltpu.VMEM((rows, HEAD), F32),
                pltpu.VMEM((heads, rows, HEAD), BF16),
                pltpu.VMEM((rows, query_width), BF16),
                pltpu.VMEM((2,) + block, F32),
                pltpu.VMEM((n_tp, 8, rows), F32),
                pltpu.VMEM((n_ctx, 8, width), F32),
                pltpu.VMEM((n_tp, 8, HEAD), F32),
                pltpu.VMEM((micro, 8, width), F32),
                dma((2, 7)),
                dma((7,)),
                dma((3,)),
                dma((1,)),
                dma((2, 2)),
                dma((2, 2, 4, PIECES)),
                dma((2, 2)),
                dma((2, 2, 4, PIECES)),
                dma((3, 2, PIECES)),
                dma((2,)),
                dma((2, 2)),
                dma((2,)),
                dma((2,)),
                dma((3,)),
                dma((3,)),
                dma((sections,)),
                dma((micro,)),
            ],
            compiler_params=pltpu.CompilerParams(
                collective_id=0, has_side_effects=True, vmem_limit_bytes=60 << 20),
            cost_estimate=pl.CostEstimate(
                flops=micro * 2 * rows * (n_tp * width * (query_width + 3 * HEAD) * 2),
                bytes_accessed=16 << 20, transcendentals=micro * heads * rows * rows * n_ctx),
        )(
            document_lengths, tenant_indices, tokens, attention_norm_gain,
            closing_norm_gain.reshape(1, width), jnp.asarray(tables),
            query_weight.reshape(n_tp, width, query_width),
            key_weight.reshape(n_tp, width, HEAD), value_weight.reshape(n_tp, width, HEAD),
            output_weight[0],
            jnp.swapaxes(query_adapter_down[0], 1, 2), jnp.swapaxes(value_adapter_down[0], 1, 2),
            query_adapter_up[0], value_adapter_up[0],
        )

    return shards


def solution(mesh):
    placed = (
        P(None, "ctx", "tp"),
        P(),
        P(),
        P("section", None),
        P("section", None, "tp"),
        P("section", None, "tp"),
        P("section", None, "tp"),
        P("section", "tp", None),
        P("section", None, None, None),
        P("section", None, None, "tp"),
        P("section", None, None, None),
        P("section", None, None, "tp"),
        P("tp"),
    )
    return jax.shard_map(
        build(mesh), mesh=mesh, in_specs=placed, out_specs=P(None, "tp"), check_vma=False
    )
```

```python
import math

import jax
import jax.numpy as jnp
import numpy as np
from jax import lax
from jax.experimental import pallas as pl
from jax.experimental.pallas import tpu as pltpu
from jax.sharding import PartitionSpec as P

HEAD = 128
F32 = jnp.float32
BF16 = jnp.bfloat16
MESH = pl.DeviceIdType.MESH

PIECES = 8
FAR = 3
WK, WV, WQ, GAIN, WO, DOWN, UP = range(7)
NEAR = ((1, 0), (0, 1), (0, 3))
REST = ((1, 1), (1, 3), (0, 2), (1, 2))


def fold(x):
    total = x[:, :HEAD]
    for i in range(1, x.shape[1] // HEAD):
        total = total + x[:, i * HEAD:(i + 1) * HEAD]
    return total


def kernel(
    sizes,
    lengths, tenants, tokens, gain_hbm, closing, tables, wq_hbm, wk_hbm, wv_hbm, wo_hbm,
    qd_hbm, vd_hbm, q_up, v_up,
    out,
    wq, wkv, wo, gains, qd, vd, down, up, trig,
    hidden, own, agb, agf, rsb, rsf, rso, rsfo, prt, kvbuf,
    acc_q, acc_kv, acc_l, squares, qbuf, att, terms,
    ssb, ppb, sqb, res,
    w_sem, w_send, small_sem, in_sem, ag_send, ag_recv, rs_send, rs_recv, prt_recv,
    kv_send, kv_recv, pass_send, pass_recv, few_send, few_recv,
    fin_send, fin_recv,
):
    sections, n_ctx, n_tp, micro, rows, width = sizes
    full_width = width * n_tp
    part = rows // PIECES
    heads = wq.shape[3] // HEAD
    rank = q_up.shape[1]
    s = lax.axis_index("section")
    c = lax.axis_index("ctx")
    z = lax.axis_index("tp")
    e = lax.rem(s, 2)
    first_pair = s < 2
    last_pair = s >= sections - 2
    partner = s + 1 - 2 * e

    def around(at, by, n):
        return lax.rem(at + (by + n), n)

    swap = n_ctx // 2
    across = around(c, swap, n_ctx)

    def place(at):
        return jnp.where(first_pair, at, around(at, swap, n_ctx))

    def remote(src, dst, send, recv, section=s, ctx=c, tp=z):
        return pltpu.make_async_remote_copy(
            src_ref=src, dst_ref=dst, send_sem=send, recv_sem=recv, device_id=(section, ctx, tp),
            device_id_type=MESH)

    def arrive(ref, sem):
        pltpu.make_async_copy(ref, ref, sem).wait()

    def span(q):
        return pl.ds(q * part, part)

    def side(q):
        return q * 2 // PIECES

    def token_copy():
        return pltpu.make_async_copy(tokens.at[e], hidden.at[1], in_sem.at[0])

    def weight(item, j):
        return {
            WK: lambda: wkv.at[j, :, :, pl.ds(0, HEAD)],
            WV: lambda: wkv.at[j, :, :, pl.ds(HEAD, HEAD)],
            WQ: lambda: wq.at[j],
            GAIN: lambda: gains.at[j],
            WO: lambda: wo.at[j],
            DOWN: lambda: down.at[j],
            UP: lambda: up.at[j],
        }[item]()

    sources = {WK: wk_hbm, WV: wv_hbm, WQ: wq_hbm, GAIN: gain_hbm, WO: wo_hbm}
    spare = {DOWN: down.at[2], UP: up.at[2]}

    def weight_copy(item):
        return remote({**sources, **spare}[item], weight(item, e), w_send.at[item], w_sem.at[e, item],
                      section=partner)

    small_copies = [
        pltpu.make_async_copy(qd_hbm, qd, small_sem.at[0]),
        pltpu.make_async_copy(vd_hbm, vd, small_sem.at[1]),
        pltpu.make_async_copy(tables.at[place(c)], trig, small_sem.at[2]),
    ]

    @pl.when(first_pair)
    def _():
        token_copy().start()

    for copy in small_copies:
        copy.start()
    for item, source in sources.items():
        pltpu.make_async_copy(source, weight(item, e), w_sem.at[e, item]).start()

    barrier = pltpu.get_barrier_semaphore()
    neighbour = (around(z, 1, n_tp), around(z, -1, n_tp))
    peers = [(s, c, around(z, i, n_tp)) for i in range(1, n_tp)]
    peers += [(s, around(c, i, n_ctx), z) for i in range(1, n_ctx)]
    peers += [(around(s, i, sections), c, z) for i in range(1, sections)]
    peers += [(around(s, 2, sections), across, to) for to in (z,) + neighbour]
    for peer in peers:
        pl.semaphore_signal(barrier, 1, device_id=peer, device_id_type=MESH)

    def pick_adapters():
        for copy in small_copies:
            copy.wait()
        for slot, document in ((e, e), (2, 1 - e)):
            t = tenants[document]
            up[slot] = jnp.zeros(up.shape[1:], BF16)
            down[slot, :rank] = qd[t]
            down[slot, rank:] = vd[t]
            up[slot, :rank, :heads * HEAD] = q_up[t]
            up[slot, rank:, heads * HEAD:] = v_up[t]

    pl.semaphore_wait(barrier, len(peers))

    two_on = (around(z, 2, n_tp), around(z, -2, n_tp))

    def ag_copy(j, d, r, q, src):
        return remote(src.at[span(q)], agb.at[j, d, r, span(q)], ag_send.at[j, 0],
                      ag_recv.at[j, d, r, q if r < 2 else 0], tp=neighbour[d])

    def ag_far(j, q):
        d = side(q)
        return remote(agb.at[j, d, 1, span(q)], agf.at[j, span(q)], ag_send.at[j, 1],
                      ag_recv.at[j, 0, FAR, 0], tp=two_on[d])

    def rs_copy(j, d, r, q):
        return remote(rso.at[j, d, r, span(q)], rsb.at[j, d, r, span(q)], rs_send.at[j, 0],
                      rs_recv.at[j, d, r, q], tp=neighbour[d])

    def rs_far(j, q):
        d = side(q)
        return remote(rsfo.at[j, span(q)], rsf.at[j, span(q)], rs_send.at[j, 1],
                      rs_recv.at[j, d, FAR, q], tp=two_on[d])

    def prt_copy(j, d, q):
        slot = jnp.where(j == 0, 1, jnp.where(last_pair, 2, 0))
        moves = (j == 1) & jnp.logical_not(last_pair)
        return remote(rso.at[j, d, 2, span(q)], prt.at[slot, d, span(q)], rs_send.at[j, 0],
                      prt_recv.at[slot, d, q], tp=neighbour[d], ctx=jnp.where(moves, across, c),
                      section=jnp.where(moves, around(s, 2, sections), s))

    def pass_copy(buf, i):
        return remote(buf.at[2], buf.at[0], pass_send.at[i], pass_recv.at[i], ctx=across,
                      section=around(s, 2, sections))

    def ctx_peer(dy, dx):
        return around(c // swap, dy, 2) * swap + around(lax.rem(c, swap), dx, swap)

    ctx_ids = {offset: ctx_peer(*offset) for offset in NEAR + REST}

    def kv_copy(j, offset):
        return remote(kvbuf.at[j, c], kvbuf.at[j, c], kv_send.at[j],
                      kv_recv.at[j, 0 if offset in NEAR else 1], ctx=ctx_ids[offset])

    def ss_copy(i):
        return remote(ssb.at[0], ssb.at[i], few_send.at[0], few_recv.at[0], tp=around(z, i, n_tp))

    def pp_copy(i):
        return remote(ppb.at[0], ppb.at[i], few_send.at[1], few_recv.at[1], ctx=around(c, i, n_ctx))

    def sq_copy(i):
        return remote(sqb.at[0], sqb.at[i], few_send.at[2], few_recv.at[2], tp=around(z, i, n_tp))

    def fin_copy(i):
        return remote(res.at[e], res.at[e], fin_send.at[i], fin_recv.at[e], section=around(s, i, sections))

    def rotate(x):
        return x * trig[0] + pltpu.roll(x, HEAD // 2, axis=1) * trig[1]

    def take(j, blocks, first=False, queries=True, others=True):
        values = None
        for block, g in blocks:
            h = block.astype(F32)
            columns = pl.ds(pl.multiple_of(g * width, width), width)
            x = (h * gains[j, :, columns]).astype(BF16)
            new = []
            if others:
                new += [
                    fold(h * h),
                    jnp.dot(x, wkv[j, g], preferred_element_type=F32),
                    lax.dot_general(
                        x, down[j, :, columns], (((1,), (1,)), ((), ())), preferred_element_type=F32),
                ]
            if queries:
                new.append(jnp.dot(x, wq[j, g], preferred_element_type=F32))
            values = new if values is None else [a + b for a, b in zip(values, new)]
        refs = ((squares, acc_kv, acc_l) if others else ()) + ((acc_q,) if queries else ())
        for ref, value in zip(refs, values):
            ref[...] = value if first else ref[...] + value

    def join(i, q):
        for d in range(2):
            arrive(prt.at[i, d, span(q)], prt_recv.at[i, d, q])
        at = slice(q * part, (q + 1) * part)
        sums = prt[i, 0, at].astype(F32) + prt[i, 1, at].astype(F32)
        hidden[i + 1, at] = (hidden[i, at].astype(F32) + own[i, at].astype(F32) + sums).astype(BF16)

    def layer(j, carry):
        @pl.when(first_pair & (j == 0))
        def _():
            token_copy().wait()

        @pl.when(jnp.logical_not(first_pair) & (j == 0))
        def _():
            arrive(hidden.at[0], pass_recv.at[0])
            arrive(own.at[0], pass_recv.at[1])

        for q in range(PIECES):
            @pl.when(jnp.logical_not(first_pair) | (j == 1))
            def _():
                join(j, q)

            for d in range(2):
                ag_copy(j, d, 0, q, hidden.at[j + 1]).start()

        @pl.when(first_pair & (j == 0))
        def _():
            for item in (WK, WV, WQ, GAIN):
                weight_copy(item).start()
            pick_adapters()
            for item in (DOWN, UP):
                weight_copy(item).start()

        @pl.when((j == 1) & jnp.logical_not(last_pair))
        def _():
            pass_copy(hidden, 0).start()

        def own_take():
            for item in (GAIN, WK, WV, WQ):
                arrive(weight(item, j), w_sem.at[j, item])

            @pl.when(j != e)
            def _():
                for item in (DOWN, UP):
                    arrive(weight(item, j), w_sem.at[j, item])

            take(j, [(hidden[j + 1], z)], first=True)

        def pair(r):
            return [(agb[j, d, r], around(z, -1 - r if d == 0 else 1 + r, n_tp)) for d in range(2)]

        late = first_pair & (e == 1) & (j == 0)
        prompt = jnp.logical_not(late)

        @pl.when(prompt)
        def _():
            own_take()

        for r in range(2):
            for q in range(PIECES):
                for d in range(2):
                    arrive(agb.at[j, d, r, span(q)], ag_recv.at[j, d, r, q])
                    ag_copy(j, d, r + 1, q, agb.at[j, d, r]).start()
                    if r == 1 and d == side(q):
                        ag_far(j, q).start()

            @pl.when(prompt)
            def _():
                take(j, pair(r))

        @pl.when(first_pair & (j == 0))
        def _():
            weight_copy(WO).start()

        @pl.when(late)
        def _():
            own_take()
            for r in range(2):
                take(j, pair(r))

        for d in range(2):
            arrive(agb.at[j, d, 2], ag_recv.at[j, d, 2, 0])
        take(j, pair(2), queries=False)
        arrive(agf.at[j], ag_recv.at[j, 0, FAR, 0])
        far = [(agf[j], around(z, 4, n_tp))]
        take(j, far, queries=False)

        mean = jnp.sum(squares[...], axis=1, keepdims=True) * (1.0 / full_width)
        scale = lax.rsqrt(mean + 1e-5)
        low = (acc_l[...] * scale).astype(BF16)
        kv = acc_kv[...] * scale
        kvbuf[j, c, :, :HEAD] = rotate(kv[:, :HEAD]).astype(BF16)
        added = jnp.dot(low, up[j, :, heads * HEAD:], preferred_element_type=F32)
        kvbuf[j, c, :, HEAD:] = (kv[:, HEAD:] + added).astype(BF16)
        for offset in NEAR + REST:
            kv_copy(j, offset).start()
        take(j, pair(2) + far, others=False)
        factor = HEAD ** -0.5 * math.log2(math.e)
        for g in range(heads):
            cols = slice(g * HEAD, (g + 1) * HEAD)
            q = acc_q[:, cols] * scale + jnp.dot(low, up[j, :, cols], preferred_element_type=F32)
            qbuf[g] = (rotate(q) * factor).astype(BF16)

        n = lengths[e]
        lane = lax.broadcasted_iota(jnp.int32, (1, rows), 1)

        def keys_of(offsets):
            sources = [ctx_peer(-dy, -dx) for dy, dx in offsets]
            blocks = [kvbuf[j, source] for source in sources]
            valid = jnp.concatenate([lane + place(source) * rows < n for source in sources], axis=1)
            return (jnp.concatenate([block[:, :HEAD] for block in blocks], axis=0),
                    jnp.concatenate([block[:, HEAD:] for block in blocks], axis=0), valid)

        def scored(g, keys, valid):
            scores = lax.dot_general(
                qbuf[g], keys, (((1,), (1,)), ((), ())), preferred_element_type=F32)
            return jnp.where(valid, scores, -1e30)

        arrive(kvbuf.at[j, pl.ds(0, len(NEAR))], kv_recv.at[j, 0])
        keys, values, valid = keys_of(((0, 0),) + NEAR)
        near = []
        for g in range(heads):
            scores = scored(g, keys, valid)
            top = jnp.max(scores, axis=1, keepdims=True)
            weights = jnp.exp2(scores - top)
            total = jnp.sum(weights, axis=1, keepdims=True)
            near.append((top, total, jnp.dot(weights.astype(BF16), values, preferred_element_type=F32)))
        arrive(kvbuf.at[j, pl.ds(0, len(REST))], kv_recv.at[j, 1])
        keys, values, valid = keys_of(REST)
        for g in range(heads):
            top_near, total_near, mixed_near = near[g]
            scores = scored(g, keys, valid)
            top = jnp.maximum(jnp.max(scores, axis=1, keepdims=True), top_near)
            weights = jnp.exp2(scores - top)
            fade = jnp.exp2(top_near - top)
            total = jnp.sum(weights, axis=1, keepdims=True) + total_near * fade
            mixed = jnp.dot(weights.astype(BF16), values, preferred_element_type=F32) + mixed_near * fade
            att[:, g * HEAD:(g + 1) * HEAD] = (mixed * (1.0 / total)).astype(BF16)

        arrive(weight(WO, j), w_sem.at[j, WO])

        def term(index):
            columns = pl.ds(pl.multiple_of(index * width, width), width)
            return jnp.dot(att[...], wo[j, :, columns], preferred_element_type=F32)

        def term_at(d, distance):
            return term(around(z, distance if d == 0 else -distance, n_tp))

        rsfo[j] = term_at(0, 4).astype(BF16)
        for q in range(PIECES):
            rs_far(j, q).start()
        for d in range(2):
            rso[j, d, 0] = term_at(d, 3).astype(BF16)
            for q in range(PIECES):
                rs_copy(j, d, 0, q).start()
        for d in range(2):
            terms[d] = term_at(d, 2)
        own[j + 1] = term(z).astype(BF16)

        @pl.when((j == 1) & jnp.logical_not(last_pair))
        def _():
            pass_copy(own, 1).start()

        for q in range(PIECES):
            at = slice(q * part, (q + 1) * part)
            for d in (side(q), 1 - side(q)):
                arrive(rsb.at[j, d, 0, span(q)], rs_recv.at[j, d, 0, q])
                value = terms[d, at] + rsb[j, d, 0, at].astype(F32)
                if d == side(q):
                    arrive(rsf.at[j, span(q)], rs_recv.at[j, d, FAR, q])
                    value = value + rsf[j, at].astype(F32)
                rso[j, d, 1, at] = value.astype(BF16)
                rs_copy(j, d, 1, q).start()
        for d in range(2):
            terms[d] = term_at(d, 1)
        for q in range(PIECES):
            at = slice(q * part, (q + 1) * part)
            for d in range(2):
                arrive(rsb.at[j, d, 1, span(q)], rs_recv.at[j, d, 1, q])
                rso[j, d, 2, at] = (terms[d, at] + rsb[j, d, 1, at].astype(F32)).astype(BF16)
                prt_copy(j, d, q).start()
        return carry

    @pl.when(jnp.logical_not(first_pair))
    def _():
        for item in (WK, WV, WQ, WO, GAIN):
            weight_copy(item).start()
        pick_adapters()
        for item in (DOWN, UP):
            weight_copy(item).start()

    lax.fori_loop(0, 2, layer, 0)

    @pl.when(last_pair)
    def _():
        for q in range(PIECES):
            join(2, q)
        wide = hidden[3].astype(F32)
        folded = fold(wide * wide)
        row = jnp.sum(jnp.transpose(folded), axis=0, keepdims=True)
        ssb[0] = jnp.broadcast_to(row, (8, rows))
        for i in range(1, n_tp):
            ss_copy(i).start()
        arrive(ssb.at[pl.ds(1, n_tp - 1)], few_recv.at[0])
        row = jnp.sum(ssb[...], axis=0)[:1]
        column = jnp.transpose(jnp.broadcast_to(row, (rows, rows)))[:, :1]
        scale = lax.rsqrt(column * (1.0 / full_width) + 1e-5)
        n = lengths[e]
        position = place(c) * rows + lax.broadcasted_iota(jnp.int32, (rows, 1), 0)
        scale = jnp.where(position < n, scale, 0.0)
        pooled = jnp.sum(hidden[3].astype(F32) * scale, axis=0, keepdims=True)
        ppb[0] = jnp.broadcast_to(pooled * closing[...] / n.astype(F32), (8, width))
        for i in range(1, n_ctx):
            pp_copy(i).start()
        arrive(ppb.at[pl.ds(1, n_ctx - 1)], few_recv.at[1])
        pooled = jnp.sum(ppb[...], axis=0)
        sqb[0] = jnp.broadcast_to(jnp.sum(pooled * pooled, axis=1, keepdims=True), (8, HEAD))
        for i in range(1, n_tp):
            sq_copy(i).start()
        arrive(sqb.at[pl.ds(1, n_tp - 1)], few_recv.at[2])
        norms = jnp.sum(sqb[...], axis=0)[:, :1]
        res[e] = pooled * lax.rsqrt(norms * (1.0 / full_width) + 1e-6)
        for i in range(1, sections):
            fin_copy(i).start()
        arrive(res.at[1 - e], fin_recv.at[1 - e])
        for i, buf in enumerate((ssb, ppb, sqb)):
            arrive(buf.at[pl.ds(1, buf.shape[0] - 1)], few_send.at[i])
        for i in range(1, sections):
            fin_copy(i).wait_send()

    @pl.when(jnp.logical_not(last_pair))
    def _():
        pass_copy(hidden, 0).wait_send()
        pass_copy(own, 1).wait_send()
        for i in range(micro):
            arrive(res.at[i], fin_recv.at[i])

    for i in range(micro):
        out[i:i + 1] = res[i, :1]

    for item in range(7):
        weight_copy(item).wait_send()
    for j in range(2):
        arrive(agb.at[j], ag_send.at[j, 0])
        arrive(agf.at[j], ag_send.at[j, 1])
        arrive(rso.at[j], rs_send.at[j, 0])
        arrive(rsfo.at[j], rs_send.at[j, 1])
        arrive(kvbuf.at[j, pl.ds(1, n_ctx - 1)], kv_send.at[j])


def build(mesh):
    sections, n_ctx, n_tp = (mesh.shape[a] for a in ("section", "ctx", "tp"))

    def shards(
        tokens, document_lengths, tenant_indices, attention_norm_gain, query_weight, key_weight,
        value_weight, output_weight, query_adapter_down, query_adapter_up, value_adapter_down,
        value_adapter_up, closing_norm_gain,
    ):
        micro, rows, width = tokens.shape
        query_width = query_weight.shape[2]
        tenant_count, rank = query_adapter_down.shape[1], query_adapter_down.shape[3]
        heads = query_width // HEAD

        freq = (500000.0 ** (-np.arange(HEAD // 2) / (HEAD // 2))).astype(np.float32)
        angle = np.arange(rows * n_ctx, dtype=np.float32)[:, None] * freq[None, :]
        cosine, sine = np.cos(angle.astype(np.float64)), np.sin(angle.astype(np.float64))
        tables = np.stack([np.concatenate([cosine, cosine], 1), np.concatenate([-sine, sine], 1)])
        tables = tables.reshape(2, n_ctx, rows, HEAD).transpose(1, 0, 2, 3).astype(np.float32)

        vmem = pl.BlockSpec(memory_space=pltpu.VMEM)
        hbm = pl.BlockSpec(memory_space=pl.ANY)
        smem = pl.BlockSpec(memory_space=pltpu.SMEM)
        dma = pltpu.SemaphoreType.DMA
        block = (rows, width)

        def body(*refs):
            kernel((sections, n_ctx, n_tp, micro, rows, width), *refs)

        return pl.pallas_call(
            body,
            out_shape=jax.ShapeDtypeStruct((micro, width), F32),
            in_specs=[smem, smem, hbm, hbm, vmem, hbm, hbm, hbm, hbm, hbm, hbm, hbm, vmem, vmem],
            out_specs=vmem,
            scratch_shapes=[
                pltpu.VMEM((2, n_tp, width, query_width), BF16),
                pltpu.VMEM((2, n_tp, width, 2 * HEAD), BF16),
                pltpu.VMEM((2, query_width, width * n_tp), BF16),
                pltpu.VMEM((2, 1, width * n_tp), F32),
                pltpu.VMEM((tenant_count, rank, width * n_tp), BF16),
                pltpu.VMEM((tenant_count, rank, width * n_tp), BF16),
                pltpu.VMEM((3, 2 * rank, width * n_tp), BF16),
                pltpu.VMEM((3, 2 * rank, query_width + HEAD), BF16),
                pltpu.VMEM((2, rows, HEAD), F32),
                pltpu.VMEM((4,) + block, BF16),
                pltpu.VMEM((3,) + block, BF16),
                pltpu.VMEM((2, 2, 3) + block, BF16),
                pltpu.VMEM((2,) + block, BF16),
                pltpu.VMEM((2, 2, 2) + block, BF16),
                pltpu.VMEM((2,) + block, BF16),
                pltpu.VMEM((2, 2, 3) + block, BF16),
                pltpu.VMEM((2,) + block, BF16),
                pltpu.VMEM((3, 2) + block, BF16),
                pltpu.VMEM((2, n_ctx, rows, 2 * HEAD), BF16),
                pltpu.VMEM((rows, query_width), F32),
                pltpu.VMEM((rows, 2 * HEAD), F32),
                pltpu.VMEM((rows, 2 * rank), F32),
                pltpu.VMEM((rows, HEAD), F32),
                pltpu.VMEM((heads, rows, HEAD), BF16),
                pltpu.VMEM((rows, query_width), BF16),
                pltpu.VMEM((2,) + block, F32),
                pltpu.VMEM((n_tp, 8, rows), F32),
                pltpu.VMEM((n_ctx, 8, width), F32),
                pltpu.VMEM((n_tp, 8, HEAD), F32),
                pltpu.VMEM((micro, 8, width), F32),
                dma((2, 7)),
                dma((7,)),
                dma((3,)),
                dma((1,)),
                dma((2, 2)),
                dma((2, 2, 4, PIECES)),
                dma((2, 2)),
                dma((2, 2, 4, PIECES)),
                dma((3, 2, PIECES)),
                dma((2,)),
                dma((2, 2)),
                dma((2,)),
                dma((2,)),
                dma((3,)),
                dma((3,)),
                dma((sections,)),
                dma((micro,)),
            ],
            compiler_params=pltpu.CompilerParams(
                collective_id=0, has_side_effects=True, vmem_limit_bytes=60 << 20),
            cost_estimate=pl.CostEstimate(
                flops=micro * 2 * rows * (n_tp * width * (query_width + 3 * HEAD) * 2),
                bytes_accessed=16 << 20, transcendentals=micro * heads * rows * rows * n_ctx),
        )(
            document_lengths, tenant_indices, tokens, attention_norm_gain,
            closing_norm_gain.reshape(1, width), jnp.asarray(tables),
            query_weight.reshape(n_tp, width, query_width),
            key_weight.reshape(n_tp, width, HEAD), value_weight.reshape(n_tp, width, HEAD),
            output_weight[0],
            jnp.swapaxes(query_adapter_down[0], 1, 2), jnp.swapaxes(value_adapter_down[0], 1, 2),
            query_adapter_up[0], value_adapter_up[0],
        )

    return shards


def solution(mesh):
    placed = (
        P(None, "ctx", "tp"),
        P(),
        P(),
        P("section", None),
        P("section", None, "tp"),
        P("section", None, "tp"),
        P("section", None, "tp"),
        P("section", "tp", None),
        P("section", None, None, None),
        P("section", None, None, "tp"),
        P("section", None, None, None),
        P("section", None, None, "tp"),
        P("tp"),
    )
    return jax.shard_map(
        build(mesh), mesh=mesh, in_specs=placed, out_specs=P(None, "tp"), check_vma=False
    )
```

```python
import math

import jax
import jax.numpy as jnp
import numpy as np
from jax import lax
from jax.experimental import pallas as pl
from jax.experimental.pallas import tpu as pltpu
from jax.sharding import PartitionSpec as P

HEAD = 128
F32 = jnp.float32
BF16 = jnp.bfloat16
MESH = pl.DeviceIdType.MESH

PIECES = 8
FAR = 3
WK, WV, WQ, GAIN, WO, DOWN, UP = range(7)
NEAR = ((1, 0), (0, 1), (0, 3))
REST = ((1, 1), (1, 3), (0, 2), (1, 2))
FIRST = REST[2:]


def fold(x):
    total = x[:, :HEAD]
    for i in range(1, x.shape[1] // HEAD):
        total = total + x[:, i * HEAD:(i + 1) * HEAD]
    return total


def kernel(
    sizes,
    lengths, tenants, tokens, gain_hbm, closing, tables, wq_hbm, wk_hbm, wv_hbm, wo_hbm,
    qd_hbm, vd_hbm, q_up, v_up,
    out,
    wq, wkv, wo, gains, qd, vd, down, up, trig,
    hidden, own, agb, agf, rsb, rsf, rso, rsfo, prt, kvbuf,
    acc_q, acc_kv, acc_l, squares, qbuf, att, terms,
    ssb, ppb, sqb, res,
    w_sem, w_send, small_sem, in_sem, ag_send, ag_recv, rs_send, rs_recv, prt_recv,
    kv_send, kv_recv, pass_send, pass_recv, few_send, few_recv,
    fin_send, fin_recv,
):
    sections, n_ctx, n_tp, micro, rows, width = sizes
    full_width = width * n_tp
    part = rows // PIECES
    heads = wq.shape[3] // HEAD
    rank = q_up.shape[1]
    s = lax.axis_index("section")
    c = lax.axis_index("ctx")
    z = lax.axis_index("tp")
    e = lax.rem(s, 2)
    first_pair = s < 2
    last_pair = s >= sections - 2
    partner = s + 1 - 2 * e

    def around(at, by, n):
        return lax.rem(at + (by + n), n)

    swap = n_ctx // 2
    across = around(c, swap, n_ctx)

    def place(at):
        return jnp.where(first_pair, at, around(at, swap, n_ctx))

    def remote(src, dst, send, recv, section=s, ctx=c, tp=z):
        return pltpu.make_async_remote_copy(
            src_ref=src, dst_ref=dst, send_sem=send, recv_sem=recv, device_id=(section, ctx, tp),
            device_id_type=MESH)

    def arrive(ref, sem):
        pltpu.make_async_copy(ref, ref, sem).wait()

    def span(q):
        return pl.ds(q * part, part)

    def side(q):
        return q * 2 // PIECES

    def token_copy():
        return pltpu.make_async_copy(tokens.at[e], hidden.at[1], in_sem.at[0])

    def weight(item, j):
        return {
            WK: lambda: wkv.at[j, :, :, pl.ds(0, HEAD)],
            WV: lambda: wkv.at[j, :, :, pl.ds(HEAD, HEAD)],
            WQ: lambda: wq.at[j],
            GAIN: lambda: gains.at[j],
            WO: lambda: wo.at[j],
            DOWN: lambda: down.at[j],
            UP: lambda: up.at[j],
        }[item]()

    sources = {WK: wk_hbm, WV: wv_hbm, WQ: wq_hbm, GAIN: gain_hbm, WO: wo_hbm}
    spare = {DOWN: down.at[2], UP: up.at[2]}

    def weight_copy(item):
        return remote({**sources, **spare}[item], weight(item, e), w_send.at[item], w_sem.at[e, item],
                      section=partner)

    small_copies = [
        pltpu.make_async_copy(qd_hbm, qd, small_sem.at[0]),
        pltpu.make_async_copy(vd_hbm, vd, small_sem.at[1]),
        pltpu.make_async_copy(tables.at[place(c)], trig, small_sem.at[2]),
    ]

    @pl.when(first_pair)
    def _():
        token_copy().start()

    for copy in small_copies:
        copy.start()
    for item, source in sources.items():
        pltpu.make_async_copy(source, weight(item, e), w_sem.at[e, item]).start()

    barrier = pltpu.get_barrier_semaphore()
    neighbour = (around(z, 1, n_tp), around(z, -1, n_tp))
    peers = [(s, c, around(z, i, n_tp)) for i in range(1, n_tp)]
    peers += [(s, around(c, i, n_ctx), z) for i in range(1, n_ctx)]
    peers += [(around(s, i, sections), c, z) for i in range(1, sections)]
    peers += [(around(s, 2, sections), across, to) for to in (z,) + neighbour]
    for peer in peers:
        pl.semaphore_signal(barrier, 1, device_id=peer, device_id_type=MESH)

    def pick_adapters():
        for copy in small_copies:
            copy.wait()
        for slot, document in ((e, e), (2, 1 - e)):
            t = tenants[document]
            up[slot] = jnp.zeros(up.shape[1:], BF16)
            down[slot, :rank] = qd[t]
            down[slot, rank:] = vd[t]
            up[slot, :rank, :heads * HEAD] = q_up[t]
            up[slot, rank:, heads * HEAD:] = v_up[t]

    pl.semaphore_wait(barrier, len(peers))

    two_on = (around(z, 2, n_tp), around(z, -2, n_tp))

    def ag_copy(j, d, r, q, src):
        return remote(src.at[span(q)], agb.at[j, d, r, span(q)], ag_send.at[j, 0],
                      ag_recv.at[j, d, r, q if r < 2 else 0], tp=neighbour[d])

    def ag_far(j, q):
        d = side(q)
        return remote(agb.at[j, d, 1, span(q)], agf.at[j, span(q)], ag_send.at[j, 1],
                      ag_recv.at[j, 0, FAR, 0], tp=two_on[d])

    def rs_copy(j, d, r, q):
        return remote(rso.at[j, d, r, span(q)], rsb.at[j, d, r, span(q)], rs_send.at[j, 0],
                      rs_recv.at[j, d, r, q], tp=neighbour[d])

    def rs_far(j, q):
        d = side(q)
        return remote(rsfo.at[j, span(q)], rsf.at[j, span(q)], rs_send.at[j, 1],
                      rs_recv.at[j, d, FAR, q], tp=two_on[d])

    def prt_copy(j, d, q):
        slot = jnp.where(j == 0, 1, jnp.where(last_pair, 2, 0))
        moves = (j == 1) & jnp.logical_not(last_pair)
        return remote(rso.at[j, d, 2, span(q)], prt.at[slot, d, span(q)], rs_send.at[j, 0],
                      prt_recv.at[slot, d, q], tp=neighbour[d], ctx=jnp.where(moves, across, c),
                      section=jnp.where(moves, around(s, 2, sections), s))

    def pass_copy(buf, i):
        return remote(buf.at[2], buf.at[0], pass_send.at[i], pass_recv.at[i], ctx=across,
                      section=around(s, 2, sections))

    def ctx_peer(dy, dx):
        return around(c // swap, dy, 2) * swap + around(lax.rem(c, swap), dx, swap)

    ctx_ids = {offset: ctx_peer(*offset) for offset in NEAR + REST}

    def kv_copy(j, offset):
        return remote(kvbuf.at[j, c], kvbuf.at[j, c], kv_send.at[j],
                      kv_recv.at[j, 0 if offset in NEAR else 1], ctx=ctx_ids[offset])

    def ss_copy(i):
        return remote(ssb.at[0], ssb.at[i], few_send.at[0], few_recv.at[0], tp=around(z, i, n_tp))

    def pp_copy(i):
        return remote(ppb.at[0], ppb.at[i], few_send.at[1], few_recv.at[1], ctx=around(c, i, n_ctx))

    def sq_copy(i):
        return remote(sqb.at[0], sqb.at[i], few_send.at[2], few_recv.at[2], tp=around(z, i, n_tp))

    def fin_copy(i):
        return remote(res.at[e], res.at[e], fin_send.at[i], fin_recv.at[e], section=around(s, i, sections))

    def rotate(x):
        return x * trig[0] + pltpu.roll(x, HEAD // 2, axis=1) * trig[1]

    def take(j, blocks, first=False, queries=True, others=True):
        values = None
        for block, g in blocks:
            h = block.astype(F32)
            columns = pl.ds(pl.multiple_of(g * width, width), width)
            x = (h * gains[j, :, columns]).astype(BF16)
            new = []
            if others:
                new += [
                    fold(h * h),
                    jnp.dot(x, wkv[j, g], preferred_element_type=F32),
                    lax.dot_general(
                        x, down[j, :, columns], (((1,), (1,)), ((), ())), preferred_element_type=F32),
                ]
            if queries:
                new.append(jnp.dot(x, wq[j, g], preferred_element_type=F32))
            values = new if values is None else [a + b for a, b in zip(values, new)]
        refs = ((squares, acc_kv, acc_l) if others else ()) + ((acc_q,) if queries else ())
        for ref, value in zip(refs, values):
            ref[...] = value if first else ref[...] + value

    def join(i, q):
        for d in range(2):
            arrive(prt.at[i, d, span(q)], prt_recv.at[i, d, q])
        at = slice(q * part, (q + 1) * part)
        sums = prt[i, 0, at].astype(F32) + prt[i, 1, at].astype(F32)
        hidden[i + 1, at] = (hidden[i, at].astype(F32) + own[i, at].astype(F32) + sums).astype(BF16)

    def layer(j, carry):
        @pl.when(first_pair & (j == 0))
        def _():
            token_copy().wait()

        @pl.when(jnp.logical_not(first_pair) & (j == 0))
        def _():
            arrive(hidden.at[0], pass_recv.at[0])
            arrive(own.at[0], pass_recv.at[1])

        for q in range(PIECES):
            @pl.when(jnp.logical_not(first_pair) | (j == 1))
            def _():
                join(j, q)

            for d in range(2):
                ag_copy(j, d, 0, q, hidden.at[j + 1]).start()

        @pl.when(first_pair & (j == 0))
        def _():
            for item in (WK, WV, WQ, GAIN):
                weight_copy(item).start()
            pick_adapters()
            for item in (DOWN, UP):
                weight_copy(item).start()

        @pl.when((j == 1) & jnp.logical_not(last_pair))
        def _():
            pass_copy(hidden, 0).start()

        def own_take():
            for item in (GAIN, WK, WV, WQ):
                arrive(weight(item, j), w_sem.at[j, item])

            @pl.when(j != e)
            def _():
                for item in (DOWN, UP):
                    arrive(weight(item, j), w_sem.at[j, item])

            take(j, [(hidden[j + 1], z)], first=True)

        def pair(r):
            return [(agb[j, d, r], around(z, -1 - r if d == 0 else 1 + r, n_tp)) for d in range(2)]

        late = first_pair & (e == 1) & (j == 0)
        prompt = jnp.logical_not(late)

        @pl.when(prompt)
        def _():
            own_take()

        for r in range(2):
            for q in range(PIECES):
                for d in range(2):
                    arrive(agb.at[j, d, r, span(q)], ag_recv.at[j, d, r, q])
                    ag_copy(j, d, r + 1, q, agb.at[j, d, r]).start()
                    if r == 1 and d == side(q):
                        ag_far(j, q).start()

            @pl.when(prompt)
            def _():
                take(j, pair(r))

        @pl.when(first_pair & (j == 0))
        def _():
            weight_copy(WO).start()

        @pl.when(late)
        def _():
            own_take()
            for r in range(2):
                take(j, pair(r))

        for d in range(2):
            arrive(agb.at[j, d, 2], ag_recv.at[j, d, 2, 0])
        take(j, pair(2), queries=False)
        arrive(agf.at[j], ag_recv.at[j, 0, FAR, 0])
        far = [(agf[j], around(z, 4, n_tp))]
        take(j, far, queries=False)

        mean = jnp.sum(squares[...], axis=1, keepdims=True) * (1.0 / full_width)
        scale = lax.rsqrt(mean + 1e-5)
        low = (acc_l[...] * scale).astype(BF16)
        kv = acc_kv[...] * scale
        kvbuf[j, c, :, :HEAD] = rotate(kv[:, :HEAD]).astype(BF16)
        added = jnp.dot(low, up[j, :, heads * HEAD:], preferred_element_type=F32)
        kvbuf[j, c, :, HEAD:] = (kv[:, HEAD:] + added).astype(BF16)
        for offset in FIRST + NEAR + REST[:2]:
            kv_copy(j, offset).start()
        take(j, pair(2) + far, others=False)
        factor = HEAD ** -0.5 * math.log2(math.e)
        for g in range(heads):
            cols = slice(g * HEAD, (g + 1) * HEAD)
            q = acc_q[:, cols] * scale + jnp.dot(low, up[j, :, cols], preferred_element_type=F32)
            qbuf[g] = (rotate(q) * factor).astype(BF16)

        n = lengths[e]
        lane = lax.broadcasted_iota(jnp.int32, (1, rows), 1)

        def keys_of(offsets):
            sources = [ctx_peer(-dy, -dx) for dy, dx in offsets]
            blocks = [kvbuf[j, source] for source in sources]
            valid = jnp.concatenate([lane + place(source) * rows < n for source in sources], axis=1)
            return (jnp.concatenate([block[:, :HEAD] for block in blocks], axis=0),
                    jnp.concatenate([block[:, HEAD:] for block in blocks], axis=0), valid)

        def scored(g, keys, valid):
            scores = lax.dot_general(
                qbuf[g], keys, (((1,), (1,)), ((), ())), preferred_element_type=F32)
            return jnp.where(valid, scores, -1e30)

        arrive(kvbuf.at[j, pl.ds(0, len(NEAR))], kv_recv.at[j, 0])
        keys, values, valid = keys_of(((0, 0),) + NEAR)
        near = []
        for g in range(heads):
            scores = scored(g, keys, valid)
            top = jnp.max(scores, axis=1, keepdims=True)
            weights = jnp.exp2(scores - top)
            total = jnp.sum(weights, axis=1, keepdims=True)
            near.append((top, total, jnp.dot(weights.astype(BF16), values, preferred_element_type=F32)))
        arrive(kvbuf.at[j, pl.ds(0, len(REST))], kv_recv.at[j, 1])
        keys, values, valid = keys_of(REST)
        for g in range(heads):
            top_near, total_near, mixed_near = near[g]
            scores = scored(g, keys, valid)
            top = jnp.maximum(jnp.max(scores, axis=1, keepdims=True), top_near)
            weights = jnp.exp2(scores - top)
            fade = jnp.exp2(top_near - top)
            total = jnp.sum(weights, axis=1, keepdims=True) + total_near * fade
            mixed = jnp.dot(weights.astype(BF16), values, preferred_element_type=F32) + mixed_near * fade
            att[:, g * HEAD:(g + 1) * HEAD] = (mixed * (1.0 / total)).astype(BF16)

        arrive(weight(WO, j), w_sem.at[j, WO])

        def term(index):
            columns = pl.ds(pl.multiple_of(index * width, width), width)
            return jnp.dot(att[...], wo[j, :, columns], preferred_element_type=F32)

        def term_at(d, distance):
            return term(around(z, distance if d == 0 else -distance, n_tp))

        rsfo[j] = term_at(0, 4).astype(BF16)
        for q in range(PIECES):
            rs_far(j, q).start()
        for d in range(2):
            rso[j, d, 0] = term_at(d, 3).astype(BF16)
            for q in range(PIECES):
                rs_copy(j, d, 0, q).start()
        for d in range(2):
            terms[d] = term_at(d, 2)
        own[j + 1] = term(z).astype(BF16)

        @pl.when((j == 1) & jnp.logical_not(last_pair))
        def _():
            pass_copy(own, 1).start()

        for q in range(PIECES):
            at = slice(q * part, (q + 1) * part)
            for d in (side(q), 1 - side(q)):
                arrive(rsb.at[j, d, 0, span(q)], rs_recv.at[j, d, 0, q])
                value = terms[d, at] + rsb[j, d, 0, at].astype(F32)
                if d == side(q):
                    arrive(rsf.at[j, span(q)], rs_recv.at[j, d, FAR, q])
                    value = value + rsf[j, at].astype(F32)
                rso[j, d, 1, at] = value.astype(BF16)
                rs_copy(j, d, 1, q).start()
        for d in range(2):
            terms[d] = term_at(d, 1)
        for q in range(PIECES):
            at = slice(q * part, (q + 1) * part)
            for d in range(2):
                arrive(rsb.at[j, d, 1, span(q)], rs_recv.at[j, d, 1, q])
                rso[j, d, 2, at] = (terms[d, at] + rsb[j, d, 1, at].astype(F32)).astype(BF16)
                prt_copy(j, d, q).start()
        return carry

    @pl.when(jnp.logical_not(first_pair))
    def _():
        for item in (WK, WV, WQ, WO, GAIN):
            weight_copy(item).start()
        pick_adapters()
        for item in (DOWN, UP):
            weight_copy(item).start()

    lax.fori_loop(0, 2, layer, 0)

    @pl.when(last_pair)
    def _():
        for q in range(PIECES):
            join(2, q)
        wide = hidden[3].astype(F32)
        folded = fold(wide * wide)
        row = jnp.sum(jnp.transpose(folded), axis=0, keepdims=True)
        ssb[0] = jnp.broadcast_to(row, (8, rows))
        for i in range(1, n_tp):
            ss_copy(i).start()
        arrive(ssb.at[pl.ds(1, n_tp - 1)], few_recv.at[0])
        row = jnp.sum(ssb[...], axis=0)[:1]
        column = jnp.transpose(jnp.broadcast_to(row, (rows, rows)))[:, :1]
        scale = lax.rsqrt(column * (1.0 / full_width) + 1e-5)
        n = lengths[e]
        position = place(c) * rows + lax.broadcasted_iota(jnp.int32, (rows, 1), 0)
        scale = jnp.where(position < n, scale, 0.0)
        pooled = jnp.sum(hidden[3].astype(F32) * scale, axis=0, keepdims=True)
        ppb[0] = jnp.broadcast_to(pooled * closing[...] / n.astype(F32), (8, width))
        for i in range(1, n_ctx):
            pp_copy(i).start()
        arrive(ppb.at[pl.ds(1, n_ctx - 1)], few_recv.at[1])
        pooled = jnp.sum(ppb[...], axis=0)
        sqb[0] = jnp.broadcast_to(jnp.sum(pooled * pooled, axis=1, keepdims=True), (8, HEAD))
        for i in range(1, n_tp):
            sq_copy(i).start()
        arrive(sqb.at[pl.ds(1, n_tp - 1)], few_recv.at[2])
        norms = jnp.sum(sqb[...], axis=0)[:, :1]
        res[e] = pooled * lax.rsqrt(norms * (1.0 / full_width) + 1e-6)
        for i in range(1, sections):
            fin_copy(i).start()
        arrive(res.at[1 - e], fin_recv.at[1 - e])
        for i, buf in enumerate((ssb, ppb, sqb)):
            arrive(buf.at[pl.ds(1, buf.shape[0] - 1)], few_send.at[i])
        for i in range(1, sections):
            fin_copy(i).wait_send()

    @pl.when(jnp.logical_not(last_pair))
    def _():
        pass_copy(hidden, 0).wait_send()
        pass_copy(own, 1).wait_send()
        for i in range(micro):
            arrive(res.at[i], fin_recv.at[i])

    for i in range(micro):
        out[i:i + 1] = res[i, :1]

    for item in range(7):
        weight_copy(item).wait_send()
    for j in range(2):
        arrive(agb.at[j], ag_send.at[j, 0])
        arrive(agf.at[j], ag_send.at[j, 1])
        arrive(rso.at[j], rs_send.at[j, 0])
        arrive(rsfo.at[j], rs_send.at[j, 1])
        arrive(kvbuf.at[j, pl.ds(1, n_ctx - 1)], kv_send.at[j])


def build(mesh):
    sections, n_ctx, n_tp = (mesh.shape[a] for a in ("section", "ctx", "tp"))

    def shards(
        tokens, document_lengths, tenant_indices, attention_norm_gain, query_weight, key_weight,
        value_weight, output_weight, query_adapter_down, query_adapter_up, value_adapter_down,
        value_adapter_up, closing_norm_gain,
    ):
        micro, rows, width = tokens.shape
        query_width = query_weight.shape[2]
        tenant_count, rank = query_adapter_down.shape[1], query_adapter_down.shape[3]
        heads = query_width // HEAD

        freq = (500000.0 ** (-np.arange(HEAD // 2) / (HEAD // 2))).astype(np.float32)
        angle = np.arange(rows * n_ctx, dtype=np.float32)[:, None] * freq[None, :]
        cosine, sine = np.cos(angle.astype(np.float64)), np.sin(angle.astype(np.float64))
        tables = np.stack([np.concatenate([cosine, cosine], 1), np.concatenate([-sine, sine], 1)])
        tables = tables.reshape(2, n_ctx, rows, HEAD).transpose(1, 0, 2, 3).astype(np.float32)

        vmem = pl.BlockSpec(memory_space=pltpu.VMEM)
        hbm = pl.BlockSpec(memory_space=pl.ANY)
        smem = pl.BlockSpec(memory_space=pltpu.SMEM)
        dma = pltpu.SemaphoreType.DMA
        block = (rows, width)

        def body(*refs):
            kernel((sections, n_ctx, n_tp, micro, rows, width), *refs)

        return pl.pallas_call(
            body,
            out_shape=jax.ShapeDtypeStruct((micro, width), F32),
            in_specs=[smem, smem, hbm, hbm, vmem, hbm, hbm, hbm, hbm, hbm, hbm, hbm, vmem, vmem],
            out_specs=vmem,
            scratch_shapes=[
                pltpu.VMEM((2, n_tp, width, query_width), BF16),
                pltpu.VMEM((2, n_tp, width, 2 * HEAD), BF16),
                pltpu.VMEM((2, query_width, width * n_tp), BF16),
                pltpu.VMEM((2, 1, width * n_tp), F32),
                pltpu.VMEM((tenant_count, rank, width * n_tp), BF16),
                pltpu.VMEM((tenant_count, rank, width * n_tp), BF16),
                pltpu.VMEM((3, 2 * rank, width * n_tp), BF16),
                pltpu.VMEM((3, 2 * rank, query_width + HEAD), BF16),
                pltpu.VMEM((2, rows, HEAD), F32),
                pltpu.VMEM((4,) + block, BF16),
                pltpu.VMEM((3,) + block, BF16),
                pltpu.VMEM((2, 2, 3) + block, BF16),
                pltpu.VMEM((2,) + block, BF16),
                pltpu.VMEM((2, 2, 2) + block, BF16),
                pltpu.VMEM((2,) + block, BF16),
                pltpu.VMEM((2, 2, 3) + block, BF16),
                pltpu.VMEM((2,) + block, BF16),
                pltpu.VMEM((3, 2) + block, BF16),
                pltpu.VMEM((2, n_ctx, rows, 2 * HEAD), BF16),
                pltpu.VMEM((rows, query_width), F32),
                pltpu.VMEM((rows, 2 * HEAD), F32),
                pltpu.VMEM((rows, 2 * rank), F32),
                pltpu.VMEM((rows, HEAD), F32),
                pltpu.VMEM((heads, rows, HEAD), BF16),
                pltpu.VMEM((rows, query_width), BF16),
                pltpu.VMEM((2,) + block, F32),
                pltpu.VMEM((n_tp, 8, rows), F32),
                pltpu.VMEM((n_ctx, 8, width), F32),
                pltpu.VMEM((n_tp, 8, HEAD), F32),
                pltpu.VMEM((micro, 8, width), F32),
                dma((2, 7)),
                dma((7,)),
                dma((3,)),
                dma((1,)),
                dma((2, 2)),
                dma((2, 2, 4, PIECES)),
                dma((2, 2)),
                dma((2, 2, 4, PIECES)),
                dma((3, 2, PIECES)),
                dma((2,)),
                dma((2, 2)),
                dma((2,)),
                dma((2,)),
                dma((3,)),
                dma((3,)),
                dma((sections,)),
                dma((micro,)),
            ],
            compiler_params=pltpu.CompilerParams(
                collective_id=0, has_side_effects=True, vmem_limit_bytes=60 << 20),
            cost_estimate=pl.CostEstimate(
                flops=micro * 2 * rows * (n_tp * width * (query_width + 3 * HEAD) * 2),
                bytes_accessed=16 << 20, transcendentals=micro * heads * rows * rows * n_ctx),
        )(
            document_lengths, tenant_indices, tokens, attention_norm_gain,
            closing_norm_gain.reshape(1, width), jnp.asarray(tables),
            query_weight.reshape(n_tp, width, query_width),
            key_weight.reshape(n_tp, width, HEAD), value_weight.reshape(n_tp, width, HEAD),
            output_weight[0],
            jnp.swapaxes(query_adapter_down[0], 1, 2), jnp.swapaxes(value_adapter_down[0], 1, 2),
            query_adapter_up[0], value_adapter_up[0],
        )

    return shards


def solution(mesh):
    placed = (
        P(None, "ctx", "tp"),
        P(),
        P(),
        P("section", None),
        P("section", None, "tp"),
        P("section", None, "tp"),
        P("section", None, "tp"),
        P("section", "tp", None),
        P("section", None, None, None),
        P("section", None, None, "tp"),
        P("section", None, None, None),
        P("section", None, None, "tp"),
        P("tp"),
    )
    return jax.shard_map(
        build(mesh), mesh=mesh, in_specs=placed, out_specs=P(None, "tp"), check_vma=False
    )
```
